32 devices in a mesh: dp: 16 (over z, x, core), fsdp: 2 (over y).
Axes of the slice: x: 2, y: 2, z: 4, core: 2. Of those that a mesh axis runs over, the one named last changes fastest.
Arguments:
- tokens: bfloat16 [78848, 288], P(('dp', 'fsdp')), may hold values from -6 to 6
- cotangent: bfloat16 [78848, 288], P(('dp', 'fsdp')), may hold values from -6 to 6
- crop_order: int32 [32, 32], P(('dp', 'fsdp')), may hold values from 0 to 31, each once within a row
- ln1_gain: bfloat16 [288], P('dp'), may hold values from 0.099609375 to 1.8984375
- ln1_bias: bfloat16 [288], P('dp'), may hold values from -3 to 3
- w_qkv: bfloat16 [288, 864], P('fsdp', 'dp'), may hold values from -0.375 to 0.375
- b_query: bfloat16 [288], P('dp'), may hold values from -3 to 3
- b_value: bfloat16 [288], P('dp'), may hold values from -3 to 3
- w_proj: bfloat16 [288, 288], P('fsdp', 'dp'), may hold values from -1.5 to 1.5
- b_proj: bfloat16 [288], P('dp'), may hold values from -3 to 3
- ln2_gain: bfloat16 [288], P('dp'), may hold values from 0.099609375 to 1.8984375
- ln2_bias: bfloat16 [288], P('dp'), may hold values from -3 to 3
- w_up: bfloat16 [288, 1152], P('fsdp', 'dp'), may hold values from -0.375 to 0.375
- b_up: bfloat16 [1152], P('dp'), may hold values from -3 to 3
- w_down: bfloat16 [1152, 288], P('fsdp', 'dp'), may hold values from -0.1875 to 0.1875
- b_down: bfloat16 [288], P('dp'), may hold values from -3 to 3
Outputs:
- block_out: bfloat16 [78848, 288], P(('dp', 'fsdp'))
- grad_tokens: float32 [78848, 288], P(('dp', 'fsdp'))
- grad_ln1_gain: float32 [288], P('dp')
- grad_ln1_bias: float32 [288], P('dp')
- grad_w_qkv: float32 [288, 864], P('fsdp', 'dp')
- grad_b_query: float32 [288], P('dp')
- grad_b_value: float32 [288], P('dp')
- grad_w_proj: float32 [288, 288], P('fsdp', 'dp')
- grad_b_proj: float32 [288], P('dp')
- grad_ln2_gain: float32 [288], P('dp')
- grad_ln2_bias: float32 [288], P('dp')
- grad_w_up: float32 [288, 1152], P('fsdp', 'dp')
- grad_b_up: float32 [1152], P('dp')
- grad_w_down: float32 [1152, 288], P('fsdp', 'dp')
- grad_b_down: float32 [288], P('dp')
The draws below stay inside these ranges and needn't reach their ends.
Inputs may be any that keep to these rules, and one draw needn't show every extreme that they name: Each row of crop_order lists every number 0 to 31 once; entries below 8 mark a 224-pixel crop of 197 rows, the others a 96-pixel crop of 37 rows, so each group of 2464 rows holds 8 large and 24 small crops in the order of its slots.
All inputs are finite; a program needn't handle non-finite values.
Results may differ from the reference program's by a relative error of at most 0.011.
Values may be sent and summed in bfloat16 or wider, within the bound.
A program may use at most 128 MiB of HBM per device.

```python
import jax
import jax.numpy as jnp
from jax import lax

D = 288
HEADS = 6
FF = 1152
HEAD_DIM = 48
BIG_LEN = 197
SMALL_LEN = 37
IMG_DEV = 4
IMG_ROWS = 616
ROWS_DEV = 2464
CROPS_DEV = 32
MARGIN = 200
KEY_WINDOW = 1024
ROWS = 78848
N_DP = 16
N_FSDP = 2


def levels(rng, dims, pieces, least, top_value):
    loudness = 1.0
    for axis_at, parts in pieces:
        steps = jax.random.uniform(jax.random.fold_in(jax.random.fold_in(rng, 6), axis_at), (parts,), jnp.float32, least / len(pieces), top_value / len(pieces))
        loudness = loudness * jnp.repeat(jnp.exp(steps), dims[axis_at] // parts).reshape((-1,) + (1,) * (len(dims) - 1 - axis_at))
    return loudness


def gaussian(rng, dims, scale, limit, pieces=(), kind=jnp.bfloat16):
    values = scale * jax.random.normal(rng, dims, jnp.float32)
    if pieces:
        values = values * levels(rng, dims, pieces, -0.22, 0.18)
    return jnp.clip(values, -limit, limit).astype(kind)


def setup_inputs(seed: int = 0) -> dict:
    splits = jax.random.split(jax.random.key(seed), 17)
    return {
        "tokens": gaussian(splits[0], (ROWS, D), 1.0, 6.0, ((0, 32),)),
        "cotangent": gaussian(splits[1], (ROWS, D), 1.0, 6.0, ((0, 32),)),
        "crop_order": jax.vmap(lambda own: jax.random.permutation(own, CROPS_DEV))(jax.random.split(splits[2], (N_DP * N_FSDP))).reshape((N_DP * N_FSDP, CROPS_DEV)).astype(jnp.int32),
        "ln1_gain": jnp.clip(1.0 + 0.18 * jax.random.normal(splits[3], (D,), jnp.float32), 0.099609375, 1.8984375).astype(jnp.bfloat16),
        "ln1_bias": gaussian(splits[4], (D,), 0.5, 3.0, ((0, 16),)),
        "w_qkv": gaussian(splits[5], (D, 3 * D), D ** -0.5, 0.375, ((0, 2), (1, 16))),
        "b_query": gaussian(splits[6], (D,), 0.5, 3.0, ((0, 16),)),
        "b_value": gaussian(splits[7], (D,), 0.5, 3.0, ((0, 16),)),
        "w_proj": gaussian(splits[8], (D, D), (D // 16) ** -0.5, 1.5, ((0, 2), (1, 16))),
        "b_proj": gaussian(splits[9], (D,), 0.5, 3.0, ((0, 16),)),
        "ln2_gain": jnp.clip(1.0 + 0.18 * jax.random.normal(splits[10], (D,), jnp.float32), 0.099609375, 1.8984375).astype(jnp.bfloat16),
        "ln2_bias": gaussian(splits[11], (D,), 0.5, 3.0, ((0, 16),)),
        "w_up": gaussian(splits[12], (D, FF), D ** -0.5, 0.375, ((0, 2), (1, 16))),
        "b_up": gaussian(splits[13], (FF,), 0.5, 3.0, ((0, 16),)),
        "w_down": gaussian(splits[14], (FF, D), FF ** -0.5, 0.1875, ((0, 2), (1, 16))),
        "b_down": gaussian(splits[15], (D,), 0.5, 3.0, ((0, 16),)),
    }


@jax.custom_vjp
def low(v):
    return lax.optimization_barrier(v.astype(jnp.bfloat16)).astype(jnp.float32)

@jax.custom_vjp
def low_back(v):
    return v

def low_keep(v):
    return (low(v), None)

def low_pass(kept, grad):
    return (grad,)

def back_keep(v):
    return (v, None)

def back_low(kept, grad):
    return (low(grad),)
low.defvjp(low_keep, low_pass)
low_back.defvjp(back_keep, back_low)
epsilon = 1e-06
masked_score = -1e+30

def matmul(left, right):
    return jnp.dot(left, right, precision=lax.Precision.HIGHEST, preferred_element_type=jnp.float32)

def layer_norm(inputs, norm_gain, norm_shift):
    row_mean = lax.optimization_barrier(jnp.mean(inputs, axis=-1, keepdims=True))
    centered = inputs - row_mean
    variance = lax.optimization_barrier(jnp.mean(centered * centered, axis=-1, keepdims=True))
    return centered * lax.rsqrt(variance + epsilon) * norm_gain + norm_shift

def crop_labels(crop_row):
    crop_sizes = jnp.where(crop_row < 2 * IMG_DEV, BIG_LEN, SMALL_LEN).astype(jnp.int32)
    crop_ends = jnp.cumsum(crop_sizes).astype(jnp.int32)
    row_ids = jnp.arange(ROWS_DEV, dtype=jnp.int32)
    return lax.optimization_barrier(jnp.sum((row_ids[:, None] >= crop_ends[None, :]).astype(jnp.int32), axis=1)).astype(jnp.int32)

def attend(queries, keys_all, values_all, labels):

    def one_block(block_index):
        begin_row = (block_index * IMG_ROWS).astype(jnp.int32)
        window_first = jnp.clip(begin_row - MARGIN, 0, ROWS_DEV - KEY_WINDOW).astype(jnp.int32)
        query_block = lax.dynamic_slice_in_dim(queries, begin_row, IMG_ROWS, 0)
        key_block = lax.dynamic_slice_in_dim(keys_all, window_first, KEY_WINDOW, 0)
        value_block = lax.dynamic_slice_in_dim(values_all, window_first, KEY_WINDOW, 0)
        label_query = lax.dynamic_slice_in_dim(labels, begin_row, IMG_ROWS, 0)
        label_key = lax.dynamic_slice_in_dim(labels, window_first, KEY_WINDOW, 0)
        same_crop = label_query[:, None] == label_key[None, :]
        scores = jnp.einsum('qhd,khd->hqk', query_block, key_block, precision=lax.Precision.HIGHEST)
        scores = low_back(scores)
        scores = jnp.where(same_crop[None], scores, masked_score)
        probs = low(jax.nn.softmax(scores, axis=-1))
        return jnp.einsum('hqk,khd->qhd', probs, value_block, precision=lax.Precision.HIGHEST)
    contexts = lax.map(jax.checkpoint(one_block), jnp.arange(IMG_DEV, dtype=jnp.int32))
    return contexts.reshape(ROWS_DEV, D)

def forward(inputs, params, labels):
    ln1_gain, ln1_bias, w_qkv, b_query, b_value, w_proj, b_proj, ln2_gain, ln2_bias, w_up, b_up, w_down, b_down = params
    normed = low(layer_norm(inputs, ln1_gain, ln1_bias))
    bias_all = jnp.concatenate([b_query, jnp.zeros_like(b_query), b_value])
    mixed_qkv = low_back(matmul(normed, w_qkv) + bias_all)
    queries = low(mixed_qkv[:, :D] * HEAD_DIM ** (-0.5)).reshape(ROWS_DEV, HEADS, HEAD_DIM)
    keys_all = low(mixed_qkv[:, D:2 * D]).reshape(ROWS_DEV, HEADS, HEAD_DIM)
    values_all = low(mixed_qkv[:, 2 * D:]).reshape(ROWS_DEV, HEADS, HEAD_DIM)
    context = low(low_back(attend(queries, keys_all, values_all, labels)))
    branch = low_back(matmul(context, w_proj) + b_proj)
    middle = inputs + branch
    normed_two = low(layer_norm(middle, ln2_gain, ln2_bias))
    hidden_pre = low_back(matmul(normed_two, w_up) + b_up)
    activated = low(jax.nn.gelu(hidden_pre, approximate=False))
    branch_two = low_back(matmul(activated, w_down) + b_down)
    return middle + branch_two

def add_pair(left, right):
    return left + right

def reference(tokens, cotangent, crop_order, ln1_gain, ln1_bias, w_qkv, b_query, b_value, w_proj, b_proj, ln2_gain, ln2_bias, w_up, b_up, w_down, b_down):
    params = tuple((piece.astype(jnp.float32) for piece in (ln1_gain, ln1_bias, w_qkv, b_query, b_value, w_proj, b_proj, ln2_gain, ln2_bias, w_up, b_up, w_down, b_down)))
    groups = N_DP * N_FSDP
    token_rows = tokens.astype(jnp.float32).reshape(groups, ROWS_DEV, D)
    cotan_rows = cotangent.astype(jnp.float32).reshape(groups, ROWS_DEV, D)

    def one_group(totals, group_item):
        group_tokens, group_cotan, crop_row = group_item
        labels = crop_labels(crop_row)

        def forward_rows(inputs, weights):
            return forward(inputs, weights, labels)
        result, pullback = jax.vjp(forward_rows, group_tokens, params)
        grad_input, grad_params = pullback(group_cotan)
        totals = jax.tree.map(add_pair, totals, grad_params)
        return (totals, (result.astype(jnp.bfloat16), grad_input))
    zero_grads = jax.tree.map(jnp.zeros_like, params)
    totals, (outputs, input_grads) = lax.scan(one_group, zero_grads, (token_rows, cotan_rows, crop_order))
    block_out = outputs.reshape(groups * ROWS_DEV, D)
    grad_tokens = input_grads.reshape(groups * ROWS_DEV, D)
    return (block_out, grad_tokens, totals[0], totals[1], totals[2], totals[3], totals[4], totals[5], totals[6], totals[7], totals[8], totals[9], totals[10], totals[11], totals[12])
```

```python
from functools import partial

import jax
import jax.numpy as jnp
from jax import lax
from jax.experimental import pallas as pl
from jax.experimental.pallas import tpu as pltpu
from jax.sharding import PartitionSpec as P

HEADS = 6
HEAD_DIM = 48
BIG_LEN = 197
SMALL_LEN = 37
BIGS = 8
SMALLS = 24
WIDTH = 288
EXT = 304
FF = 1152
FF_EXT = 1168
ROWS = 2464
ROWS_PAD = 2560
LANES = 256
BLOCKS = 11
COLS = BLOCKS * LANES
BIG_WIN = 384
SMALL_WIN = 256
FF_STEP = 128
EPS = 1e-06
BF = jnp.bfloat16
F32 = jnp.float32
MESH = pl.DeviceIdType.MESH


def nn(a, b):
    return jnp.dot(a, b, preferred_element_type=F32)


def nt(a, b):
    return lax.dot_general(a, b, (((1,), (1,)), ((), ())), preferred_element_type=F32)


def tn(a, b):
    return lax.dot_general(a, b, (((0,), (0,)), ((), ())), preferred_element_type=F32)


def iota(shape, dim):
    return lax.broadcasted_iota(jnp.int32, shape, dim)


def wide(col):
    return jnp.concatenate([col, col], axis=1)


def block_cols(b):
    return pl.ds(pl.multiple_of(b * LANES, LANES), LANES)


class Plan:
    def __init__(self, n_dp, n_fs):
        self.n_dp, self.n_fs = n_dp, n_fs
        self.n_core = 2
        self.n_z = 4
        self.n_x = n_dp // (self.n_core * self.n_z)
        self.slots = n_dp * n_fs
        self.rows = WIDTH // n_fs
        self.qkv, self.vec, self.up = 3 * WIDTH // n_dp, WIDTH // n_dp, FF // n_dp
        self.pack_rows = -(-(self.rows + 1) // 16) * 16
        self.at_proj = self.qkv
        self.at_up = self.at_proj + self.vec
        self.at_down = self.at_up + self.up
        self.pack_cols = -(-(self.at_down + 4 * self.vec) // 128) * 128
        self.vec_cols = 8 * self.vec + self.up

    def dp(self, z, x, core):
        return (z * self.n_x + x) * self.n_core + core

    def slot(self, z, x, core, fs):
        return self.dp(z, x, core) * self.n_fs + fs

    def here(self):
        dp, fs = lax.axis_index("dp"), lax.axis_index("fsdp")
        core = lax.rem(dp, self.n_core)
        rest = lax.div(dp, self.n_core)
        return lax.div(rest, self.n_x), lax.rem(rest, self.n_x), core, fs


def other(me, step, size):
    return lax.rem(me + step, size)


def peers(plan, z, x, core, fs):
    found = [(plan.dp(z, x, other(core, 1, 2)), fs)]
    found += [(plan.dp(z, x, core), other(fs, d, plan.n_fs)) for d in range(1, plan.n_fs)]
    found += [(plan.dp(z, other(x, d, plan.n_x), core), fs) for d in range(1, plan.n_x)]
    found += [(plan.dp(other(z, d, plan.n_z), x, core), fs) for d in range(1, plan.n_z)]
    return found


def meet(places):
    barrier = pltpu.get_barrier_semaphore()
    for place in places:
        pl.semaphore_signal(barrier, inc=1, device_id=place, device_id_type=MESH)
    pl.semaphore_wait(barrier, len(places))


def gather_kernel(plan, qkv_ref, proj_ref, up_ref, down_ref, vec_ref, all_ref, pack, send_sem, recv_sem, own_sem):
    z, x, core, fs = plan.here()
    r, v = plan.rows, plan.vec
    pack[...] = jnp.zeros_like(pack)
    pack[:r, : plan.qkv] = qkv_ref[...].T
    pack[:r, plan.at_proj : plan.at_proj + v] = proj_ref[...].T
    pack[:r, plan.at_up : plan.at_up + plan.up] = up_ref[...]
    for c in range(4):
        pack[:r, plan.at_down + c * v : plan.at_down + (c + 1) * v] = down_ref[:, c * r : (c + 1) * r].T
    pack[r : r + 1, : plan.vec_cols] = vec_ref[...]
    mine = plan.slot(z, x, core, fs)
    keep = pltpu.make_async_copy(pack, all_ref.at[mine], own_sem)
    keep.start()
    meet(peers(plan, z, x, core, fs))
    sent = []

    def send(slot, place):
        src = pack if slot is mine else all_ref.at[slot]
        copy = pltpu.make_async_remote_copy(
            src_ref=src,
            dst_ref=all_ref.at[slot],
            send_sem=send_sem.at[len(sent)],
            recv_sem=recv_sem.at[slot],
            device_id=place,
            device_id_type=MESH,
        )
        copy.start()
        sent.append(copy)

    def arrived(slot):
        pltpu.make_async_remote_copy(
            src_ref=all_ref.at[slot],
            dst_ref=all_ref.at[slot],
            send_sem=send_sem.at[0],
            recv_sem=recv_sem.at[slot],
            device_id=(plan.dp(z, x, other(core, 1, 2)), fs),
            device_id_type=MESH,
        ).wait_recv()

    for d in range(1, plan.n_z):
        send(mine, (plan.dp(other(z, d, plan.n_z), x, core), fs))
    for d in range(1, plan.n_x):
        send(mine, (plan.dp(z, other(x, d, plan.n_x), core), fs))
    for d in range(1, plan.n_fs):
        send(mine, (plan.dp(z, x, core), other(fs, d, plan.n_fs)))
    send(mine, (plan.dp(z, x, other(core, 1, 2)), fs))
    for dz in range(1, plan.n_z):
        slot = plan.slot(other(z, dz, plan.n_z), x, core, fs)
        arrived(slot)
        for d in range(1, plan.n_x):
            send(slot, (plan.dp(z, other(x, d, plan.n_x), core), fs))
        for d in range(1, plan.n_fs):
            send(slot, (plan.dp(z, x, core), other(fs, d, plan.n_fs)))
        send(slot, (plan.dp(z, x, other(core, 1, 2)), fs))
    for dx in range(1, plan.n_x):
        for dz in range(plan.n_z):
            slot = plan.slot(other(z, dz, plan.n_z), other(x, dx, plan.n_x), core, fs)
            arrived(slot)
            for d in range(1, plan.n_fs):
                send(slot, (plan.dp(z, x, core), other(fs, d, plan.n_fs)))
            send(slot, (plan.dp(z, x, other(core, 1, 2)), fs))
    for df in range(1, plan.n_fs):
        for dx in range(plan.n_x):
            for dz in range(plan.n_z):
                slot = plan.slot(
                    other(z, dz, plan.n_z), other(x, dx, plan.n_x), core, other(fs, df, plan.n_fs)
                )
                arrived(slot)
                send(slot, (plan.dp(z, x, other(core, 1, 2)), fs))
    for df in range(plan.n_fs):
        for dx in range(plan.n_x):
            for dz in range(plan.n_z):
                arrived(
                    plan.slot(
                        other(z, dz, plan.n_z),
                        other(x, dx, plan.n_x),
                        other(core, 1, 2),
                        other(fs, df, plan.n_fs),
                    )
                )
    for copy in sent:
        copy.wait_send()
    keep.wait()


def gather_call(plan, qkv, proj, up, down, vec):
    vmem = pl.BlockSpec(memory_space=pltpu.VMEM)
    shape = (plan.slots, plan.pack_rows, plan.pack_cols)
    return pl.pallas_call(
        partial(gather_kernel, plan),
        out_shape=jax.ShapeDtypeStruct(shape, BF),
        in_specs=[vmem] * 5,
        out_specs=vmem,
        scratch_shapes=[
            pltpu.VMEM(shape[1:], BF),
            pltpu.SemaphoreType.DMA((plan.slots - 1,)),
            pltpu.SemaphoreType.DMA((plan.slots,)),
            pltpu.SemaphoreType.DMA,
        ],
        compiler_params=pltpu.CompilerParams(
            collective_id=0, has_side_effects=True, vmem_limit_bytes=32 * 1024 * 1024
        ),
        name="gather_weights",
    )(qkv, proj, up, down, vec)


def reduce_kernel(plan, part_ref, sum_ref, acc, got_c, got_f, got_x, got_z, send_sem, sem_c, sem_f, sem_x, sem_z):
    z, x, core, fs = plan.here()
    nz, nx, nf = plan.n_z, plan.n_x, plan.n_fs
    peer = other(core, 1, 2)
    meet(peers(plan, z, x, core, fs))
    sent = []

    def send(src, dst, sem, place):
        copy = pltpu.make_async_remote_copy(
            src_ref=src,
            dst_ref=dst,
            send_sem=send_sem.at[len(sent)],
            recv_sem=sem,
            device_id=place,
            device_id_type=MESH,
        )
        copy.start()
        sent.append(copy)

    def take(buffer, sem, index):
        pltpu.make_async_remote_copy(
            src_ref=buffer.at[index],
            dst_ref=buffer.at[index],
            send_sem=send_sem.at[0],
            recv_sem=sem.at[index],
            device_id=(plan.dp(z, x, peer), fs),
            device_id_type=MESH,
        ).wait_recv()
        return buffer[index].astype(F32)

    def order():
        for df in list(range(1, nf)) + [0]:
            for dx in list(range(1, nx)) + [0]:
                for dz in list(range(1, nz)) + [0]:
                    yield df, dx, dz

    def at(df, dx, dz):
        return other(z, dz, nz), other(x, dx, nx), other(fs, df, nf)

    for df, dx, dz in order():
        tz, tx, tf = at(df, dx, dz)
        index = (df * nx + dx) * nz + dz
        send(part_ref.at[plan.slot(tz, tx, peer, tf)], got_c.at[index], sem_c.at[index], (plan.dp(z, x, peer), fs))
    for df, dx, dz in order():
        tz, tx, tf = at(df, dx, dz)
        index = (df * nx + dx) * nz + dz
        total = part_ref[plan.slot(tz, tx, core, tf)].astype(F32) + take(got_c, sem_c, index)
        if df:
            acc[index] = total.astype(BF)
            back = (nf - df) - 1
            spot = (back * nx + dx) * nz + dz
            send(acc.at[index], got_f.at[spot], sem_f.at[spot], (plan.dp(z, x, core), tf))
            continue
        for step in range(1, nf):
            total = total + take(got_f, sem_f, ((step - 1) * nx + dx) * nz + dz)
        if dx:
            acc[index] = total.astype(BF)
            spot = (nx - dx - 1) * nz + dz
            send(acc.at[index], got_x.at[spot], sem_x.at[spot], (plan.dp(z, tx, core), fs))
            continue
        for step in range(1, nx):
            total = total + take(got_x, sem_x, (step - 1) * nz + dz)
        if dz:
            acc[index] = total.astype(BF)
            spot = nz - dz - 1
            send(acc.at[index], got_z.at[spot], sem_z.at[spot], (plan.dp(tz, x, core), fs))
            continue
        for step in range(1, nz):
            total = total + take(got_z, sem_z, step - 1)
        sum_ref[...] = total
    for copy in sent:
        copy.wait_send()


def reduce_call(plan, part):
    vmem = pl.BlockSpec(memory_space=pltpu.VMEM)
    one = (plan.pack_rows, plan.pack_cols)
    n_c = plan.n_z * plan.n_x * plan.n_fs
    n_f = plan.n_z * plan.n_x * (plan.n_fs - 1)
    n_x = plan.n_z * (plan.n_x - 1)
    n_z = plan.n_z - 1
    return pl.pallas_call(
        partial(reduce_kernel, plan),
        out_shape=jax.ShapeDtypeStruct(one, F32),
        in_specs=[vmem],
        out_specs=vmem,
        scratch_shapes=[
            pltpu.VMEM((n_c,) + one, BF),
            pltpu.VMEM((n_c,) + one, BF),
            pltpu.VMEM((n_f,) + one, BF),
            pltpu.VMEM((n_x,) + one, BF),
            pltpu.VMEM((n_z,) + one, BF),
            pltpu.SemaphoreType.DMA((n_c + n_f + n_x + n_z,)),
            pltpu.SemaphoreType.DMA((n_c,)),
            pltpu.SemaphoreType.DMA((n_f,)),
            pltpu.SemaphoreType.DMA((n_x,)),
            pltpu.SemaphoreType.DMA((n_z,)),
        ],
        compiler_params=pltpu.CompilerParams(
            collective_id=1, has_side_effects=True, vmem_limit_bytes=48 * 1024 * 1024
        ),
        name="reduce_grads",
    )(part)


def normal_parts(rows):
    mean = jnp.sum(rows, axis=0, keepdims=True) * (1.0 / WIDTH)
    centered = rows - mean
    variance = jnp.sum(centered * centered, axis=0, keepdims=True) * (1.0 / WIDTH)
    inverse = lax.rsqrt(variance + EPS)
    return centered * inverse, inverse


def norm_back(grad, normal, inverse, gain):
    scaled = grad * gain
    first = jnp.sum(scaled, axis=0, keepdims=True) * (1.0 / WIDTH)
    second = jnp.sum(scaled * normal, axis=0, keepdims=True) * (1.0 / WIDTH)
    return inverse * (scaled - first - normal * second)


def gelu_both(u):
    z = jnp.abs(u)
    d = 1.0 + z * (0.3275911 * 0.7071067811865476)
    t = pl.reciprocal(d, approx=True)
    t = t * (2.0 - d * t)
    e = jnp.exp(u * u * -0.5)
    poly = 0.5 * 1.061405429
    poly = poly * t + 0.5 * -1.453152027
    poly = poly * t + 0.5 * 1.421413741
    poly = poly * t + 0.5 * -0.284496736
    poly = poly * t + 0.5 * 0.254829592
    tail = poly * t * e
    phi = jnp.where(u >= 0.0, 1.0 - tail, tail)
    return u * phi, phi + u * e * 0.3989422804014327


def slot_starts(order_ref, big_start, small_start):
    row = jnp.int32(0)
    big_count = jnp.int32(0)
    small_count = jnp.int32(0)
    for k in range(SMALLS, 26):
        small_start[k] = jnp.int32(1 << 20)

    def one(j, carry):
        row, big_count, small_count = carry
        big = order_ref[0, j] < BIGS

        @pl.when(big)
        def _():
            big_start[big_count] = row

        @pl.when(jnp.logical_not(big))
        def _():
            small_start[small_count] = row

        step = jnp.where(big, 1, 0)
        return (row + SMALL_LEN + (BIG_LEN - SMALL_LEN) * step, big_count + step, small_count + 1 - step)

    lax.fori_loop(0, BIGS + SMALLS, one, (row, big_count, small_count))


def window(start, size):
    first = jnp.minimum(start - lax.rem(start, jnp.int32(128)), ROWS_PAD - size)
    return pl.ds(pl.multiple_of(first, 128), size), start - first


def pieces_of(block, big_start, small_start, paired):
    if paired:
        return [
            (big_start[block], BIG_LEN, 0, BIG_WIN),
            (small_start[block], SMALL_LEN, BIG_LEN, SMALL_WIN),
        ]
    base = BIGS + 6 * (block - BIGS)
    return [(small_start[base + k], SMALL_LEN, SMALL_LEN * k, SMALL_WIN) for k in range(6)]


def chooser(offset, length, lane0, size, inward):
    shape = (size, LANES) if inward else (LANES, size)
    lane = iota(shape, 1 if inward else 0)
    column = iota(shape, 0 if inward else 1)
    hit = (column - lane == offset - lane0) & (lane >= lane0) & (lane < lane0 + length)
    return jnp.where(hit, 1.0, 0.0).astype(BF)


def crop_mask(paired):
    key = iota((LANES, LANES), 0)
    query = iota((LANES, LANES), 1)
    if paired:
        label_key = jnp.where(key < BIG_LEN, 0, jnp.where(key < BIG_LEN + SMALL_LEN, 1, 2))
        label_query = jnp.where(query < BIG_LEN, 0, jnp.where(query < BIG_LEN + SMALL_LEN, 1, 2))
    else:
        label_key = jnp.zeros_like(key)
        label_query = jnp.zeros_like(key)
        for k in range(1, 7):
            label_key = label_key + jnp.where(key >= SMALL_LEN * k, 1, 0)
            label_query = label_query + jnp.where(query >= SMALL_LEN * k, 1, 0)
    return jnp.where(label_key == label_query, 0.0, -1e30)


def unpack_weights(plan, all_ref, wqkv, wproj, wup, wdown, norms):
    r, v = plan.rows, plan.vec
    wqkv[WIDTH:, :] = jnp.zeros((EXT - WIDTH, 3 * WIDTH), BF)
    wproj[WIDTH:, :] = jnp.zeros((EXT - WIDTH, WIDTH), BF)
    wup[WIDTH:, :] = jnp.zeros((EXT - WIDTH, FF), BF)
    wdown[FF:, :] = jnp.zeros((FF_EXT - FF, WIDTH), BF)
    norms[...] = jnp.zeros_like(norms)
    for i in range(plan.n_dp):
        for j in range(plan.n_fs):
            slot = i * plan.n_fs + j
            rows = slice(j * r, (j + 1) * r)
            wqkv[rows, i * plan.qkv : (i + 1) * plan.qkv] = all_ref[slot, :r, : plan.qkv]
            wproj[rows, i * v : (i + 1) * v] = all_ref[slot, :r, plan.at_proj : plan.at_proj + v]
            wup[rows, i * plan.up : (i + 1) * plan.up] = all_ref[slot, :r, plan.at_up : plan.at_up + plan.up]
            for c in range(4):
                wdown[(4 * j + c) * r : (4 * j + c + 1) * r, i * v : (i + 1) * v] = all_ref[
                    slot, :r, plan.at_down + c * v : plan.at_down + (c + 1) * v
                ]
        slot = i * plan.n_fs
        here = slice(i * v, (i + 1) * v)

        def vector(k, width):
            return all_ref[slot, r : r + 1, k * v : k * v + width]

        norms[0:1, here] = vector(0, v)
        norms[1:2, here] = vector(1, v)
        norms[2:3, here] = vector(5, v)
        norms[3:4, here] = vector(6, v)
        wqkv[WIDTH : WIDTH + 1, i * v : (i + 1) * v] = vector(2, v)
        wqkv[WIDTH : WIDTH + 1, 2 * WIDTH + i * v : 2 * WIDTH + (i + 1) * v] = vector(3, v)
        wproj[WIDTH : WIDTH + 1, here] = vector(4, v)
        wdown[FF : FF + 1, here] = vector(7, v)
        wup[WIDTH : WIDTH + 1, i * plan.up : (i + 1) * plan.up] = vector(8, plan.up)


def pack_grads(plan, part_ref, dqkv, dproj, dup, ddown, dnorm):
    r, v = plan.rows, plan.vec
    part_ref[...] = jnp.zeros_like(part_ref)
    for i in range(plan.n_dp):
        here = slice(i * v, (i + 1) * v)
        for j in range(plan.n_fs):
            slot = i * plan.n_fs + j
            rows = slice(j * r, (j + 1) * r)
            part_ref[slot, :r, : plan.qkv] = dqkv[rows, i * plan.qkv : (i + 1) * plan.qkv].astype(BF)
            part_ref[slot, :r, plan.at_proj : plan.at_proj + v] = dproj[rows, here].astype(BF)
            part_ref[slot, :r, plan.at_up : plan.at_up + plan.up] = dup[
                rows, i * plan.up : (i + 1) * plan.up
            ].astype(BF)
            for c in range(4):
                part_ref[slot, :r, plan.at_down + c * v : plan.at_down + (c + 1) * v] = ddown[
                    (4 * j + c) * r : (4 * j + c + 1) * r, here
                ].astype(BF)
            vectors = [
                dnorm[0:1, here],
                dnorm[1:2, here],
                dqkv[WIDTH : WIDTH + 1, i * v : (i + 1) * v],
                dqkv[WIDTH : WIDTH + 1, 2 * WIDTH + i * v : 2 * WIDTH + (i + 1) * v],
                dproj[WIDTH : WIDTH + 1, here],
                dnorm[2:3, here],
                dnorm[3:4, here],
                ddown[FF : FF + 1, here],
            ]
            for k, row in enumerate(vectors):
                part_ref[slot, r : r + 1, k * v : (k + 1) * v] = row.astype(BF)
            part_ref[slot, r : r + 1, 8 * v : 8 * v + plan.up] = dup[
                WIDTH : WIDTH + 1, i * plan.up : (i + 1) * plan.up
            ].astype(BF)


def main_kernel(
    plan,
    order_ref,
    tokens_ref,
    cotan_ref,
    all_ref,
    out_ref,
    gtok_ref,
    part_ref,
    big_start,
    small_start,
    tokens_s,
    cotan_s,
    wqkv_s,
    wproj_s,
    wup_s,
    wdown_s,
    norms_s,
    wqkv_t,
    wproj_t,
    wup_t,
    wdown_t,
    gains,
    mask_s,
    x_s,
    c_s,
    h1_s,
    qkv_s,
    prob_s,
    ctx_s,
    h2_s,
    act_s,
    du_s,
    da_s,
    dy1_s,
    do_s,
    da3_s,
    dqkv_s,
    dproj_s,
    dup_s,
    ddown_s,
    ddown_n,
    dnorm_s,
    acc_s,
):
    slot_starts(order_ref, big_start, small_start)
    unpack_weights(plan, all_ref, wqkv_s, wproj_s, wup_s, wdown_s, norms_s)
    wqkv_t[...] = wqkv_s[...].T
    wproj_t[...] = wproj_s[...].T
    wup_t[...] = wup_s[...].T
    wdown_t[...] = wdown_s[...].T
    for k in range(4):
        pick = jnp.where(iota((16, 128), 0) == k, 1.0, 0.0).astype(BF)
        gains[k] = tn(norms_s[...], pick)
    mask_s[0] = crop_mask(True)
    mask_s[1] = crop_mask(False)
    ones = jnp.where(iota((16, COLS), 0) == 0, 1.0, 0.0).astype(BF)
    h1_s[WIDTH:, :] = ones
    ctx_s[WIDTH:, :] = ones
    h2_s[WIDTH:, :] = ones[:, :LANES]
    act_s[FF:, :] = ones[:, :LANES]
    acc_s[...] = jnp.zeros_like(acc_s)
    dproj_s[...] = jnp.zeros_like(dproj_s)
    dup_s[...] = jnp.zeros_like(dup_s)
    ddown_s[...] = jnp.zeros_like(ddown_s)
    for rows, ref in ((tokens_s, tokens_ref), (cotan_s, cotan_ref)):
        rows[:, ROWS_PAD - 128 :] = jnp.zeros((WIDTH, 128), BF)
        rows[:, :ROWS] = ref[...]
    scale = HEAD_DIM ** (-0.5)

    def load_block(block, paired):
        cols = block_cols(block)
        x = None
        c = None
        for start, length, lane0, size in pieces_of(block, big_start, small_start, paired):
            columns, offset = window(start, size)
            sel = chooser(offset, length, lane0, size, True)
            xp = nn(tokens_s[:, columns], sel)
            cp = nn(cotan_s[:, columns], sel)
            x = xp if x is None else x + xp
            c = cp if c is None else c + cp
        x_s[:, cols] = x.astype(BF)
        c_s[:, cols] = c.astype(BF)

    def load_paired(b, _):
        load_block(b, True)
        return 0

    def load_small(b, _):
        load_block(b, False)
        return 0

    lax.fori_loop(0, BIGS, load_paired, 0)
    lax.fori_loop(BIGS, BLOCKS, load_small, 0)

    def forward(b, _):
        cols = block_cols(b)
        normal, _ = normal_parts(x_s[:, cols].astype(F32))
        h1_s[:WIDTH, cols] = (normal * wide(gains[0]) + wide(gains[1])).astype(BF)
        mixed = nn(wqkv_t[...], h1_s[:, cols])
        queries = (mixed[:WIDTH] * scale).astype(BF)
        keys = mixed[WIDTH : 2 * WIDTH].astype(BF)
        values = mixed[2 * WIDTH :].astype(BF)
        qkv_s[:WIDTH, cols] = queries
        qkv_s[WIDTH : 2 * WIDTH, cols] = keys
        qkv_s[2 * WIDTH :, cols] = values
        mask = mask_s[jnp.where(b < BIGS, 0, 1)]
        blank = jnp.zeros((HEAD_DIM, LANES), BF)
        for pair in range(HEADS // 2):
            two = slice(2 * HEAD_DIM * pair, 2 * HEAD_DIM * (pair + 1))
            key_rows = keys[two].T
            for half in range(2):
                h = 2 * pair + half
                one = slice(HEAD_DIM * h, HEAD_DIM * (h + 1))
                query = queries[one]
                query = jnp.concatenate([query, blank] if half == 0 else [blank, query], axis=0)
                scores = nn(key_rows, query) + mask
                top = jnp.max(scores, axis=0, keepdims=True)
                expo = jnp.exp(scores - top)
                total = jnp.sum(expo, axis=0, keepdims=True)
                prob = (expo * (1.0 / total)).astype(BF)
                prob_s[b, h] = prob
                ctx_s[one, cols] = nn(values[one], prob).astype(BF)
        return 0

    lax.fori_loop(0, BLOCKS, forward, 0)

    def middle(b, _):
        cols = block_cols(b)
        mid = x_s[:, cols].astype(F32) + nn(wproj_t[...], ctx_s[:, cols])
        normal, inverse = normal_parts(mid)
        h2_s[:WIDTH, :] = (normal * wide(gains[2]) + wide(gains[3])).astype(BF)
        h2 = h2_s[...]
        cotan = c_s[:, cols]
        for f in range(0, FF, FF_STEP):
            part = slice(f, f + FF_STEP)
            act, slope = gelu_both(nn(wup_t[part, :], h2))
            act_s[part, :] = act.astype(BF)
            du_s[part, :] = (nn(wdown_s[part, :], cotan) * slope).astype(BF)
        out = mid + nn(wdown_t[...], act_s[...])
        out_ref[:, cols] = out.astype(BF)
        grad = nn(wup_s[:WIDTH, :], du_s[...])
        dup_s[...] += nt(h2, du_s[...])
        ddown_s[...] += nt(cotan, act_s[...])
        acc_s[2] += grad * normal
        acc_s[3] += grad
        dy1 = cotan.astype(F32) + norm_back(grad, normal, inverse, wide(gains[2]))
        dy1_s[:, cols] = dy1
        da = dy1.astype(BF)
        da_s[:, cols] = da
        do_s[:, cols] = nn(wproj_s[:WIDTH, :], da).astype(BF)
        return 0

    lax.fori_loop(0, BLOCKS, middle, 0)
    dproj_s[...] = nt(ctx_s[...], da_s[...])

    def backward(b, _):
        cols = block_cols(b)
        blank = jnp.zeros((HEAD_DIM, LANES), BF)
        for pair in range(HEADS // 2):
            low = 2 * HEAD_DIM * pair
            value_rows = qkv_s[2 * WIDTH + low : 2 * WIDTH + low + 2 * HEAD_DIM, cols].T
            for half in range(2):
                h = 2 * pair + half
                first = HEAD_DIM * h
                one = slice(first, first + HEAD_DIM)
                grad = do_s[one, cols]
                both = jnp.concatenate([grad, blank] if half == 0 else [blank, grad], axis=0)
                grad_prob = nn(value_rows, both)
                low_prob = prob_s[b, h]
                prob = low_prob.astype(F32)
                term = prob * grad_prob
                weighted = jnp.sum(term, axis=0, keepdims=True)
                ds = (term - prob * weighted).astype(BF)
                dq = nn(qkv_s[WIDTH + first : WIDTH + first + HEAD_DIM, cols], ds) * scale
                dk = nt(qkv_s[one, cols], ds)
                dv = nt(grad, low_prob)
                da3_s[one, cols] = dq.astype(BF)
                da3_s[WIDTH + first : WIDTH + first + HEAD_DIM, cols] = dk.astype(BF)
                da3_s[2 * WIDTH + first : 2 * WIDTH + first + HEAD_DIM, cols] = dv.astype(BF)
        return 0

    lax.fori_loop(0, BLOCKS, backward, 0)
    dqkv_s[...] = nt(h1_s[...], da3_s[...])

    def last(b, _):
        cols = block_cols(b)
        grad = nn(wqkv_s[:WIDTH, :], da3_s[:, cols])
        normal, inverse = normal_parts(x_s[:, cols].astype(F32))
        acc_s[0] += grad * normal
        acc_s[1] += grad
        gtok = dy1_s[:, cols] + norm_back(grad, normal, inverse, wide(gains[0]))
        gtok_ref[:, cols] = gtok.astype(BF)
        return 0

    lax.fori_loop(0, BLOCKS, last, 0)
    for k in range(4):
        both = acc_s[k]
        column = both[:, :128] + both[:, 128:]
        dnorm_s[k : k + 1, :] = jnp.sum(column.T, axis=0, keepdims=True)
    ddown_n[...] = ddown_s[...].T
    pack_grads(plan, part_ref, dqkv_s, dproj_s, dup_s, ddown_n, dnorm_s)


def main_call(plan, order, tokens, cotan, packs):
    vmem = pl.BlockSpec(memory_space=pltpu.VMEM)
    return pl.pallas_call(
        partial(main_kernel, plan),
        out_shape=(
            jax.ShapeDtypeStruct((WIDTH, COLS), BF),
            jax.ShapeDtypeStruct((WIDTH, COLS), BF),
            jax.ShapeDtypeStruct(packs.shape, BF),
        ),
        in_specs=[pl.BlockSpec(memory_space=pltpu.SMEM)] + [vmem] * 3,
        out_specs=(vmem,) * 3,
        scratch_shapes=[
            pltpu.SMEM((BIGS,), jnp.int32),
            pltpu.SMEM((26,), jnp.int32),
            pltpu.VMEM((WIDTH, ROWS_PAD), BF),
            pltpu.VMEM((WIDTH, ROWS_PAD), BF),
            pltpu.VMEM((EXT, 3 * WIDTH), BF),
            pltpu.VMEM((EXT, WIDTH), BF),
            pltpu.VMEM((EXT, FF), BF),
            pltpu.VMEM((FF_EXT, WIDTH), BF),
            pltpu.VMEM((16, WIDTH), BF),
            pltpu.VMEM((3 * WIDTH, EXT), BF),
            pltpu.VMEM((WIDTH, EXT), BF),
            pltpu.VMEM((FF, EXT), BF),
            pltpu.VMEM((WIDTH, FF_EXT), BF),
            pltpu.VMEM((4, WIDTH, 128), F32),
            pltpu.VMEM((2, LANES, LANES), F32),
            pltpu.VMEM((WIDTH, COLS), BF),
            pltpu.VMEM((WIDTH, COLS), BF),
            pltpu.VMEM((EXT, COLS), BF),
            pltpu.VMEM((3 * WIDTH, COLS), BF),
            pltpu.VMEM((BLOCKS, HEADS, LANES, LANES), BF),
            pltpu.VMEM((EXT, COLS), BF),
            pltpu.VMEM((EXT, LANES), BF),
            pltpu.VMEM((FF_EXT, LANES), BF),
            pltpu.VMEM((FF, LANES), BF),
            pltpu.VMEM((WIDTH, COLS), BF),
            pltpu.VMEM((WIDTH, COLS), F32),
            pltpu.VMEM((WIDTH, COLS), BF),
            pltpu.VMEM((3 * WIDTH, COLS), BF),
            pltpu.VMEM((EXT, 3 * WIDTH), F32),
            pltpu.VMEM((EXT, WIDTH), F32),
            pltpu.VMEM((EXT, FF), F32),
            pltpu.VMEM((WIDTH, FF_EXT), F32),
            pltpu.VMEM((FF_EXT, WIDTH), F32),
            pltpu.VMEM((4, WIDTH), F32),
            pltpu.VMEM((4, WIDTH, LANES), F32),
        ],
        compiler_params=pltpu.CompilerParams(vmem_limit_bytes=64 * 1024 * 1024 - 65536),
        name="block_main",
    )(order, tokens, cotan, packs)


def place_kernel(plan, order_ref, out_c_ref, gtok_c_ref, sum_ref, *refs):
    out_ref, gtok_ref, dqkv_ref, dproj_ref, dup_ref, ddown_ref = refs[:6]
    vectors = refs[6:15]
    big_start, small_start, out_s, gtok_s = refs[15:]
    slot_starts(order_ref, big_start, small_start)
    out_s[...] = jnp.zeros_like(out_s)
    gtok_s[...] = jnp.zeros_like(gtok_s)

    def place(block, paired):
        cols = block_cols(block)
        rows = jnp.concatenate([out_c_ref[:, cols], gtok_c_ref[:, cols]], axis=0)
        for start, length, lane0, size in pieces_of(block, big_start, small_start, paired):
            columns, offset = window(start, size)
            moved = nn(rows, chooser(offset, length, lane0, size, False))
            out_s[:, columns] += moved[:WIDTH].astype(BF)
            gtok_s[:, columns] += moved[WIDTH:]

    def place_paired(b, _):
        place(b, True)
        return 0

    def place_small(b, _):
        place(b, False)
        return 0

    lax.fori_loop(0, BIGS, place_paired, 0)
    lax.fori_loop(BIGS, BLOCKS, place_small, 0)
    out_ref[...] = out_s[:, :ROWS]
    gtok_ref[...] = gtok_s[:, :ROWS]
    r, v = plan.rows, plan.vec
    dqkv_ref[...] = sum_ref[:r, : plan.qkv].T
    dproj_ref[...] = sum_ref[:r, plan.at_proj : plan.at_proj + v].T
    dup_ref[...] = sum_ref[:r, plan.at_up : plan.at_up + plan.up]
    for c in range(4):
        ddown_ref[:, c * r : (c + 1) * r] = sum_ref[:r, plan.at_down + c * v : plan.at_down + (c + 1) * v].T
    for k in range(9):
        width = v if k < 8 else plan.up
        vectors[k][...] = sum_ref[r : r + 1, k * v : k * v + width]


def place_call(plan, order, out_c, gtok_c, total):
    vmem = pl.BlockSpec(memory_space=pltpu.VMEM)
    f32 = lambda *shape: jax.ShapeDtypeStruct(shape, F32)
    r, v = plan.rows, plan.vec
    return pl.pallas_call(
        partial(place_kernel, plan),
        out_shape=(
            jax.ShapeDtypeStruct((WIDTH, ROWS), BF),
            f32(WIDTH, ROWS),
            f32(plan.qkv, r),
            f32(v, r),
            f32(r, plan.up),
            f32(v, 4 * r),
        )
        + (f32(1, v),) * 8
        + (f32(1, plan.up),),
        in_specs=[pl.BlockSpec(memory_space=pltpu.SMEM)] + [vmem] * 3,
        out_specs=(vmem,) * 15,
        scratch_shapes=[
            pltpu.SMEM((BIGS,), jnp.int32),
            pltpu.SMEM((26,), jnp.int32),
            pltpu.VMEM((WIDTH, ROWS_PAD), BF),
            pltpu.VMEM((WIDTH, ROWS_PAD), F32),
        ],
        compiler_params=pltpu.CompilerParams(vmem_limit_bytes=48 * 1024 * 1024),
        name="block_place",
    )(order, out_c, gtok_c, total)


def local(plan, *args):
    (
        tokens,
        cotangent,
        crop_order,
        ln1_gain,
        ln1_bias,
        w_qkv,
        b_query,
        b_value,
        w_proj,
        b_proj,
        ln2_gain,
        ln2_bias,
        w_up,
        b_up,
        w_down,
        b_down,
    ) = args
    vec = jnp.concatenate([ln1_gain, ln1_bias, b_query, b_value, b_proj, ln2_gain, ln2_bias, b_down, b_up])
    packs = gather_call(plan, w_qkv.T, w_proj.T, w_up, w_down.T, vec[None])
    out_c, gtok_c, part = main_call(plan, crop_order, tokens.T, cotangent.T, packs)
    total = reduce_call(plan, part)
    out, gtok, dqkv, dproj, dup, ddown, *vectors = place_call(plan, crop_order, out_c, gtok_c, total)
    g1, s1, bq, bv, bp, g2, s2, bd, bu = [one[0] for one in vectors]
    return (out.T, gtok.T, g1, s1, dqkv.T, bq, bv, dproj.T, bp, g2, s2, dup, bu, ddown.T, bd)


def solution(mesh):
    plan = Plan(mesh.shape["dp"], mesh.shape["fsdp"])
    rows = P(("dp", "fsdp"), None)
    vec = P("dp")
    mat = P("fsdp", "dp")
    return jax.shard_map(
        partial(local, plan),
        mesh=mesh,
        in_specs=(rows, rows, rows, vec, vec, mat, vec, vec, mat, vec, vec, vec, mat, vec, mat, vec),
        out_specs=(rows, rows, vec, vec, mat, vec, vec, mat, vec, vec, vec, mat, vec, mat, vec),
        check_vma=False,
    )
```

```python
from functools import partial

import jax
import jax.numpy as jnp
from jax import lax
from jax.experimental import pallas as pl
from jax.experimental.pallas import tpu as pltpu
from jax.sharding import PartitionSpec as P

HEADS = 6
HEAD_DIM = 48
BIG_LEN = 197
SMALL_LEN = 37
BIGS = 8
SMALLS = 24
WIDTH = 288
EXT = 304
FF = 1152
FF_EXT = 1168
ROWS = 2464
ROWS_PAD = 2560
LANES = 256
BLOCKS = 11
COLS = BLOCKS * LANES
BIG_WIN = 384
SMALL_WIN = 256
FF_STEP = 288
EPS = 1e-06
BF = jnp.bfloat16
F32 = jnp.float32
MESH = pl.DeviceIdType.MESH


def nn(a, b):
    return jnp.dot(a, b, preferred_element_type=F32)


def nt(a, b):
    return lax.dot_general(a, b, (((1,), (1,)), ((), ())), preferred_element_type=F32)


def tn(a, b):
    return lax.dot_general(a, b, (((0,), (0,)), ((), ())), preferred_element_type=F32)


def iota(shape, dim):
    return lax.broadcasted_iota(jnp.int32, shape, dim)


def wide(col):
    return jnp.concatenate([col, col], axis=1)


def block_cols(b):
    return pl.ds(pl.multiple_of(b * LANES, LANES), LANES)


class Plan:
    def __init__(self, n_dp, n_fs):
        self.n_dp, self.n_fs = n_dp, n_fs
        self.n_core = 2
        self.n_z = 4
        self.n_x = n_dp // (self.n_core * self.n_z)
        self.slots = n_dp * n_fs
        self.rows = WIDTH // n_fs
        self.qkv, self.vec, self.up = 3 * WIDTH // n_dp, WIDTH // n_dp, FF // n_dp
        self.pack_rows = -(-(self.rows + 1) // 16) * 16
        self.at_proj = self.qkv
        self.at_up = self.at_proj + self.vec
        self.at_down = self.at_up + self.up
        self.pack_cols = -(-(self.at_down + 4 * self.vec) // 128) * 128
        self.vec_cols = 8 * self.vec + self.up

    def dp(self, z, x, core):
        return (z * self.n_x + x) * self.n_core + core

    def slot(self, z, x, core, fs):
        return self.dp(z, x, core) * self.n_fs + fs

    def here(self):
        dp, fs = lax.axis_index("dp"), lax.axis_index("fsdp")
        core = lax.rem(dp, self.n_core)
        rest = lax.div(dp, self.n_core)
        return lax.div(rest, self.n_x), lax.rem(rest, self.n_x), core, fs


def other(me, step, size):
    return lax.rem(me + step, size)


def peers(plan, z, x, core, fs):
    found = [(plan.dp(z, x, other(core, 1, 2)), fs)]
    found += [(plan.dp(z, x, core), other(fs, d, plan.n_fs)) for d in range(1, plan.n_fs)]
    found += [(plan.dp(z, other(x, d, plan.n_x), core), fs) for d in range(1, plan.n_x)]
    found += [(plan.dp(other(z, d, plan.n_z), x, core), fs) for d in range(1, plan.n_z)]
    return found


def meet(places):
    barrier = pltpu.get_barrier_semaphore()
    for place in places:
        pl.semaphore_signal(barrier, inc=1, device_id=place, device_id_type=MESH)
    pl.semaphore_wait(barrier, len(places))


def gather(plan, qkv_ref, proj_ref, up_ref, down_ref, vec_ref, all_ref, pack, send_sem, recv_sem, own_sem):
    z, x, core, fs = plan.here()
    r, v = plan.rows, plan.vec
    pack[...] = jnp.zeros_like(pack)
    pack[:r, : plan.qkv] = qkv_ref[...].T
    pack[:r, plan.at_proj : plan.at_proj + v] = proj_ref[...].T
    pack[:r, plan.at_up : plan.at_up + plan.up] = up_ref[...]
    for c in range(4):
        pack[:r, plan.at_down + c * v : plan.at_down + (c + 1) * v] = down_ref[:, c * r : (c + 1) * r].T
    pack[r : r + 1, : plan.vec_cols] = vec_ref[...]
    mine = plan.slot(z, x, core, fs)
    keep = pltpu.make_async_copy(pack, all_ref.at[mine], own_sem)
    keep.start()
    meet(peers(plan, z, x, core, fs))
    sent = []

    def send(slot, place):
        src = pack if slot is mine else all_ref.at[slot]
        copy = pltpu.make_async_remote_copy(
            src_ref=src,
            dst_ref=all_ref.at[slot],
            send_sem=send_sem.at[len(sent)],
            recv_sem=recv_sem.at[slot],
            device_id=place,
            device_id_type=MESH,
        )
        copy.start()
        sent.append(copy)

    def arrived(slot):
        pltpu.make_async_remote_copy(
            src_ref=all_ref.at[slot],
            dst_ref=all_ref.at[slot],
            send_sem=send_sem.at[0],
            recv_sem=recv_sem.at[slot],
            device_id=(plan.dp(z, x, other(core, 1, 2)), fs),
            device_id_type=MESH,
        ).wait_recv()

    for d in range(1, plan.n_z):
        send(mine, (plan.dp(other(z, d, plan.n_z), x, core), fs))
    for d in range(1, plan.n_x):
        send(mine, (plan.dp(z, other(x, d, plan.n_x), core), fs))
    for d in range(1, plan.n_fs):
        send(mine, (plan.dp(z, x, core), other(fs, d, plan.n_fs)))
    send(mine, (plan.dp(z, x, other(core, 1, 2)), fs))
    for dz in range(1, plan.n_z):
        slot = plan.slot(other(z, dz, plan.n_z), x, core, fs)
        arrived(slot)
        for d in range(1, plan.n_x):
            send(slot, (plan.dp(z, other(x, d, plan.n_x), core), fs))
        for d in range(1, plan.n_fs):
            send(slot, (plan.dp(z, x, core), other(fs, d, plan.n_fs)))
        send(slot, (plan.dp(z, x, other(core, 1, 2)), fs))
    for dx in range(1, plan.n_x):
        for dz in range(plan.n_z):
            slot = plan.slot(other(z, dz, plan.n_z), other(x, dx, plan.n_x), core, fs)
            arrived(slot)
            for d in range(1, plan.n_fs):
                send(slot, (plan.dp(z, x, core), other(fs, d, plan.n_fs)))
            send(slot, (plan.dp(z, x, other(core, 1, 2)), fs))
    for df in range(1, plan.n_fs):
        for dx in range(plan.n_x):
            for dz in range(plan.n_z):
                slot = plan.slot(
                    other(z, dz, plan.n_z), other(x, dx, plan.n_x), core, other(fs, df, plan.n_fs)
                )
                arrived(slot)
                send(slot, (plan.dp(z, x, other(core, 1, 2)), fs))
    for df in range(plan.n_fs):
        for dx in range(plan.n_x):
            for dz in range(plan.n_z):
                arrived(
                    plan.slot(
                        other(z, dz, plan.n_z),
                        other(x, dx, plan.n_x),
                        other(core, 1, 2),
                        other(fs, df, plan.n_fs),
                    )
                )
    for copy in sent:
        copy.wait_send()
    keep.wait()


def reduce(plan, part_ref, sum_ref, acc, got_c, got_f, got_x, got_z, send_sem, sem_c, sem_f, sem_x, sem_z):
    z, x, core, fs = plan.here()
    nz, nx, nf = plan.n_z, plan.n_x, plan.n_fs
    peer = other(core, 1, 2)
    sent = []

    def send(src, dst, sem, place):
        copy = pltpu.make_async_remote_copy(
            src_ref=src,
            dst_ref=dst,
            send_sem=send_sem.at[len(sent)],
            recv_sem=sem,
            device_id=place,
            device_id_type=MESH,
        )
        copy.start()
        sent.append(copy)

    def take(buffer, sem, index):
        pltpu.make_async_remote_copy(
            src_ref=buffer.at[index],
            dst_ref=buffer.at[index],
            send_sem=send_sem.at[0],
            recv_sem=sem.at[index],
            device_id=(plan.dp(z, x, peer), fs),
            device_id_type=MESH,
        ).wait_recv()
        return buffer[index].astype(F32)

    def order():
        for df in list(range(1, nf)) + [0]:
            for dx in list(range(1, nx)) + [0]:
                for dz in list(range(1, nz)) + [0]:
                    yield df, dx, dz

    def at(df, dx, dz):
        return other(z, dz, nz), other(x, dx, nx), other(fs, df, nf)

    for df, dx, dz in order():
        tz, tx, tf = at(df, dx, dz)
        index = (df * nx + dx) * nz + dz
        send(part_ref.at[plan.slot(tz, tx, peer, tf)], got_c.at[index], sem_c.at[index], (plan.dp(z, x, peer), fs))
    for df, dx, dz in order():
        tz, tx, tf = at(df, dx, dz)
        index = (df * nx + dx) * nz + dz
        total = part_ref[plan.slot(tz, tx, core, tf)].astype(F32) + take(got_c, sem_c, index)
        if df:
            acc[index] = total.astype(BF)
            back = (nf - df) - 1
            spot = (back * nx + dx) * nz + dz
            send(acc.at[index], got_f.at[spot], sem_f.at[spot], (plan.dp(z, x, core), tf))
            continue
        for step in range(1, nf):
            total = total + take(got_f, sem_f, ((step - 1) * nx + dx) * nz + dz)
        if dx:
            acc[index] = total.astype(BF)
            spot = (nx - dx - 1) * nz + dz
            send(acc.at[index], got_x.at[spot], sem_x.at[spot], (plan.dp(z, tx, core), fs))
            continue
        for step in range(1, nx):
            total = total + take(got_x, sem_x, (step - 1) * nz + dz)
        if dz:
            acc[index] = total.astype(BF)
            spot = nz - dz - 1
            send(acc.at[index], got_z.at[spot], sem_z.at[spot], (plan.dp(tz, x, core), fs))
            continue
        for step in range(1, nz):
            total = total + take(got_z, sem_z, step - 1)
        sum_ref[...] = total
    for copy in sent:
        copy.wait_send()


def normal_parts(rows):
    mean = jnp.sum(rows, axis=0, keepdims=True) * (1.0 / WIDTH)
    centered = rows - mean
    variance = jnp.sum(centered * centered, axis=0, keepdims=True) * (1.0 / WIDTH)
    inverse = lax.rsqrt(variance + EPS)
    return centered * inverse, inverse


def norm_back(grad, normal, inverse, gain):
    scaled = grad * gain
    first = jnp.sum(scaled, axis=0, keepdims=True) * (1.0 / WIDTH)
    second = jnp.sum(scaled * normal, axis=0, keepdims=True) * (1.0 / WIDTH)
    return inverse * (scaled - first - normal * second)


def gelu_both(u):
    z = jnp.abs(u)
    d = 1.0 + z * (0.3275911 * 0.7071067811865476)
    t = pl.reciprocal(d, approx=True)
    t = t * (2.0 - d * t)
    e = jnp.exp(u * u * -0.5)
    poly = 0.5 * 1.061405429
    poly = poly * t + 0.5 * -1.453152027
    poly = poly * t + 0.5 * 1.421413741
    poly = poly * t + 0.5 * -0.284496736
    poly = poly * t + 0.5 * 0.254829592
    tail = poly * t * e
    phi = jnp.where(u >= 0.0, 1.0 - tail, tail)
    return u * phi, phi + u * e * 0.3989422804014327


def slot_starts(order_ref, big_start, small_start):
    far = jnp.int32(1 << 20)

    def one(j, carry):
        row, big_count, starts = carry
        big = jnp.where(order_ref[0, j] < BIGS, 1, 0)
        rank = jnp.where(big == 1, big_count, BIGS + j - big_count)
        starts = tuple(jnp.where(rank == k, row, start) for k, start in enumerate(starts))
        return row + SMALL_LEN + (BIG_LEN - SMALL_LEN) * big, big_count + big, starts

    _, _, starts = lax.fori_loop(
        0, BIGS + SMALLS, one, (jnp.int32(0), jnp.int32(0), (far,) * (BIGS + SMALLS + 2))
    )
    for k in range(BIGS):
        big_start[k] = starts[k]
    for k in range(SMALLS + 2):
        small_start[k] = starts[BIGS + k]


def window(start, size):
    first = jnp.minimum(start - lax.rem(start, jnp.int32(128)), ROWS_PAD - size)
    return pl.ds(pl.multiple_of(first, 128), size), start - first


def pieces_of(block, big_start, small_start, paired):
    if paired:
        return [
            (big_start[block], BIG_LEN, 0, BIG_WIN),
            (small_start[block], SMALL_LEN, BIG_LEN, SMALL_WIN),
        ]
    base = BIGS + 6 * (block - BIGS)
    return [(small_start[base + k], SMALL_LEN, SMALL_LEN * k, SMALL_WIN) for k in range(6)]


def chooser(offset, length, lane0, size, inward):
    shape = (size, LANES) if inward else (LANES, size)
    lane = iota(shape, 1 if inward else 0)
    column = iota(shape, 0 if inward else 1)
    hit = (column - lane == offset - lane0) & (lane >= lane0) & (lane < lane0 + length)
    return jnp.where(hit, 1.0, 0.0).astype(BF)


def crop_mask(paired):
    key = iota((LANES, LANES), 0)
    query = iota((LANES, LANES), 1)
    if paired:
        label_key = jnp.where(key < BIG_LEN, 0, jnp.where(key < BIG_LEN + SMALL_LEN, 1, 2))
        label_query = jnp.where(query < BIG_LEN, 0, jnp.where(query < BIG_LEN + SMALL_LEN, 1, 2))
    else:
        label_key = jnp.zeros_like(key)
        label_query = jnp.zeros_like(key)
        for k in range(1, 7):
            label_key = label_key + jnp.where(key >= SMALL_LEN * k, 1, 0)
            label_query = label_query + jnp.where(query >= SMALL_LEN * k, 1, 0)
    return jnp.where(label_key == label_query, 0.0, -1e30)


def unpack_weights(plan, all_ref, wqkv, wproj, wup, wdown, norms):
    r, v = plan.rows, plan.vec
    wqkv[WIDTH:, :] = jnp.zeros((EXT - WIDTH, 3 * WIDTH), BF)
    wproj[WIDTH:, :] = jnp.zeros((EXT - WIDTH, WIDTH), BF)
    wup[WIDTH:, :] = jnp.zeros((EXT - WIDTH, FF), BF)
    wdown[FF:, :] = jnp.zeros((FF_EXT - FF, WIDTH), BF)
    norms[...] = jnp.zeros_like(norms)
    for i in range(plan.n_dp):
        for j in range(plan.n_fs):
            slot = i * plan.n_fs + j
            rows = slice(j * r, (j + 1) * r)
            wqkv[rows, i * plan.qkv : (i + 1) * plan.qkv] = all_ref[slot, :r, : plan.qkv]
            wproj[rows, i * v : (i + 1) * v] = all_ref[slot, :r, plan.at_proj : plan.at_proj + v]
            wup[rows, i * plan.up : (i + 1) * plan.up] = all_ref[slot, :r, plan.at_up : plan.at_up + plan.up]
            for c in range(4):
                wdown[(4 * j + c) * r : (4 * j + c + 1) * r, i * v : (i + 1) * v] = all_ref[
                    slot, :r, plan.at_down + c * v : plan.at_down + (c + 1) * v
                ]
        slot = i * plan.n_fs
        here = slice(i * v, (i + 1) * v)

        def vector(k, width):
            return all_ref[slot, r : r + 1, k * v : k * v + width]

        norms[0:1, here] = vector(0, v)
        norms[1:2, here] = vector(1, v)
        norms[2:3, here] = vector(5, v)
        norms[3:4, here] = vector(6, v)
        wqkv[WIDTH : WIDTH + 1, i * v : (i + 1) * v] = vector(2, v)
        wqkv[WIDTH : WIDTH + 1, 2 * WIDTH + i * v : 2 * WIDTH + (i + 1) * v] = vector(3, v)
        wproj[WIDTH : WIDTH + 1, here] = vector(4, v)
        wdown[FF : FF + 1, here] = vector(7, v)
        wup[WIDTH : WIDTH + 1, i * plan.up : (i + 1) * plan.up] = vector(8, plan.up)


def pack_grads(plan, part_ref, dqkv, dproj, dup, ddown, dnorm):
    r, v = plan.rows, plan.vec
    part_ref[...] = jnp.zeros_like(part_ref)
    for i in range(plan.n_dp):
        here = slice(i * v, (i + 1) * v)
        for j in range(plan.n_fs):
            slot = i * plan.n_fs + j
            rows = slice(j * r, (j + 1) * r)
            part_ref[slot, :r, : plan.qkv] = dqkv[rows, i * plan.qkv : (i + 1) * plan.qkv].astype(BF)
            part_ref[slot, :r, plan.at_proj : plan.at_proj + v] = dproj[rows, here].astype(BF)
            part_ref[slot, :r, plan.at_up : plan.at_up + plan.up] = dup[
                rows, i * plan.up : (i + 1) * plan.up
            ].astype(BF)
            for c in range(4):
                part_ref[slot, :r, plan.at_down + c * v : plan.at_down + (c + 1) * v] = ddown[
                    (4 * j + c) * r : (4 * j + c + 1) * r, here
                ].astype(BF)
            vectors = [
                dnorm[0:1, here],
                dnorm[1:2, here],
                dqkv[WIDTH : WIDTH + 1, i * v : (i + 1) * v],
                dqkv[WIDTH : WIDTH + 1, 2 * WIDTH + i * v : 2 * WIDTH + (i + 1) * v],
                dproj[WIDTH : WIDTH + 1, here],
                dnorm[2:3, here],
                dnorm[3:4, here],
                ddown[FF : FF + 1, here],
            ]
            for k, row in enumerate(vectors):
                part_ref[slot, r : r + 1, k * v : (k + 1) * v] = row.astype(BF)
            part_ref[slot, r : r + 1, 8 * v : 8 * v + plan.up] = dup[
                WIDTH : WIDTH + 1, i * plan.up : (i + 1) * plan.up
            ].astype(BF)


def main_kernel(
    plan,
    order_ref,
    tokens_ref,
    cotan_ref,
    qkv_ref,
    proj_ref,
    up_ref,
    down_ref,
    vec_ref,
    out_ref,
    gtok_ref,
    sum_ref,
    all_ref,
    part_ref,
    pack,
    acc,
    got_c,
    got_f,
    got_x,
    got_z,
    g_send,
    g_recv,
    g_own,
    r_send,
    r_c,
    r_f,
    r_x,
    r_z,
    big_start,
    small_start,
    wqkv_s,
    wproj_s,
    wup_s,
    wdown_s,
    norms_s,
    wqkv_t,
    wproj_t,
    wup_t,
    wdown_t,
    gains,
    mask_s,
    x_s,
    c_s,
    h1_s,
    qkv_s,
    prob_s,
    ctx_s,
    h2_s,
    act_s,
    du_s,
    da_s,
    dy1_s,
    do_s,
    da3_s,
    dqkv_s,
    dproj_s,
    dup_s,
    ddown_s,
    ddown_n,
    dnorm_s,
    acc_s,
    work_s,
    ds_s,
    target_s,
):
    slot_starts(order_ref, big_start, small_start)
    gather(plan, qkv_ref, proj_ref, up_ref, down_ref, vec_ref, all_ref, pack, g_send, g_recv, g_own)
    unpack_weights(plan, all_ref, wqkv_s, wproj_s, wup_s, wdown_s, norms_s)
    wqkv_t[...] = wqkv_s[...].T
    wproj_t[...] = wproj_s[...].T
    wup_t[...] = wup_s[...].T
    wdown_t[...] = wdown_s[...].T
    for k in range(4):
        pick = jnp.where(iota((16, 128), 0) == k, 1.0, 0.0).astype(BF)
        gains[k] = tn(norms_s[...], pick)
    mask_s[0] = crop_mask(True)
    mask_s[1] = crop_mask(False)
    ones = jnp.where(iota((16, COLS), 0) == 0, 1.0, 0.0).astype(BF)
    h1_s[WIDTH:, :] = ones
    ctx_s[WIDTH:, :] = ones
    h2_s[WIDTH:, :] = ones[:, :LANES]
    act_s[FF:, :] = ones[:, :LANES]
    acc_s[...] = jnp.zeros_like(acc_s)
    dproj_s[...] = jnp.zeros_like(dproj_s)
    dup_s[...] = jnp.zeros_like(dup_s)
    ddown_s[...] = jnp.zeros_like(ddown_s)
    da3_s[: 2 * WIDTH, ROWS_PAD - 128 : ROWS_PAD] = jnp.zeros((2 * WIDTH, 128), BF)
    da3_s[:WIDTH, :ROWS] = tokens_ref[...]
    da3_s[WIDTH : 2 * WIDTH, :ROWS] = cotan_ref[...]
    scale = HEAD_DIM ** (-0.5)

    lane = iota((1, LANES), 1)
    targets = []
    for b in range(BIGS):
        small = jnp.where(lane < BIG_LEN + SMALL_LEN, small_start[b] - BIG_LEN + lane, -1)
        targets.append(jnp.where(lane < BIG_LEN, big_start[b] + lane, small))
    for b in range(BIGS, BLOCKS):
        target = jnp.full((1, LANES), -1, jnp.int32)
        for k in range(6):
            start = small_start[BIGS + 6 * (b - BIGS) + k] - SMALL_LEN * k
            target = jnp.where((lane >= SMALL_LEN * k) & (lane < SMALL_LEN * (k + 1)), start + lane, target)
        targets.append(target)
    for b in range(BLOCKS):
        target_s[b] = targets[b]

    def load_block(b, _):
        cols = block_cols(b)
        sel = jnp.where(iota((ROWS_PAD, LANES), 0) == target_s[b], 1.0, 0.0).astype(BF)
        both = nn(da3_s[: 2 * WIDTH, :ROWS_PAD], sel)
        x_s[:, cols] = both[:WIDTH].astype(BF)
        c_s[:, cols] = both[WIDTH:].astype(BF)
        return 0

    lax.fori_loop(0, BLOCKS, load_block, 0)

    def forward(b, _):
        cols = block_cols(b)
        normal, _ = normal_parts(x_s[:, cols].astype(F32))
        h1_s[:WIDTH, cols] = (normal * wide(gains[0]) + wide(gains[1])).astype(BF)
        mixed = nn(wqkv_t[...], h1_s[:, cols])
        qkv_s[:WIDTH, cols] = (mixed[:WIDTH] * scale).astype(BF)
        qkv_s[WIDTH:, cols] = mixed[WIDTH:].astype(BF)
        kind = jnp.where(b < BIGS, 0, 1)
        blank = jnp.zeros((HEAD_DIM, LANES), BF)

        def score(h):
            pair, half = divmod(h, 2)
            low = WIDTH + 2 * HEAD_DIM * pair
            keys = qkv_s[low : low + 2 * HEAD_DIM, cols].T
            query = qkv_s[HEAD_DIM * h : HEAD_DIM * (h + 1), cols]
            query = jnp.concatenate([query, blank] if half == 0 else [blank, query], axis=0)
            work_s[h % 2] = nn(keys, query)

        def spread(h):
            for tile in (slice(0, 128), slice(128, 256)):
                scores = work_s[h % 2, :, tile] + mask_s[kind, :, tile]
                top = jnp.max(scores, axis=0, keepdims=True)
                expo = jnp.exp(scores - top)
                total = jnp.sum(expo, axis=0, keepdims=True)
                prob_s[b, h, :, tile] = (expo * (1.0 / total)).astype(BF)

        def mix(h):
            one = slice(HEAD_DIM * h, HEAD_DIM * (h + 1))
            values = qkv_s[2 * WIDTH + HEAD_DIM * h : 2 * WIDTH + HEAD_DIM * (h + 1), cols]
            ctx_s[one, cols] = nn(values, prob_s[b, h]).astype(BF)

        score(0)
        for h in range(HEADS):
            if h + 1 < HEADS:
                score(h + 1)
            spread(h)
            if h > 0:
                mix(h - 1)
        mix(HEADS - 1)
        return 0

    lax.fori_loop(0, BLOCKS, forward, 0)

    def middle(b, _):
        cols = block_cols(b)
        mid = x_s[:, cols].astype(F32) + nn(wproj_t[...], ctx_s[:, cols])
        normal, inverse = normal_parts(mid)
        h2_s[:WIDTH, :] = (normal * wide(gains[2]) + wide(gains[3])).astype(BF)
        h2 = h2_s[...]
        cotan = c_s[:, cols]
        for f in range(0, FF, FF_STEP):
            part = slice(f, f + FF_STEP)
            act, slope = gelu_both(nn(wup_t[part, :], h2))
            act_s[part, :] = act.astype(BF)
            du_s[part, :] = (nn(wdown_s[part, :], cotan) * slope).astype(BF)
        out = mid + nn(wdown_t[...], act_s[...])
        out_ref[:, cols] = out.astype(BF)
        grad = nn(wup_s[:WIDTH, :], du_s[...])
        dup_s[...] += nt(h2, du_s[...])
        ddown_s[...] += nt(cotan, act_s[...])
        acc_s[2] += grad * normal
        acc_s[3] += grad
        dy1 = cotan.astype(F32) + norm_back(grad, normal, inverse, wide(gains[2]))
        dy1_s[:, cols] = dy1
        da = dy1.astype(BF)
        da_s[:, cols] = da
        do_s[:, cols] = nn(wproj_s[:WIDTH, :], da).astype(BF)
        return 0

    lax.fori_loop(0, BLOCKS, middle, 0)
    dproj_s[...] = nt(ctx_s[...], da_s[...])

    def backward(b, _):
        cols = block_cols(b)
        blank = jnp.zeros((HEAD_DIM, LANES), BF)

        def of(part, h):
            return slice(part * WIDTH + HEAD_DIM * h, part * WIDTH + HEAD_DIM * (h + 1))

        def slope(h):
            pair, half = divmod(h, 2)
            low = 2 * WIDTH + 2 * HEAD_DIM * pair
            values = qkv_s[low : low + 2 * HEAD_DIM, cols].T
            grad = do_s[of(0, h), cols]
            both = jnp.concatenate([grad, blank] if half == 0 else [blank, grad], axis=0)
            work_s[h % 2] = nn(values, both)

        def score_grad(h):
            for tile in (slice(0, 128), slice(128, 256)):
                prob = prob_s[b, h, :, tile].astype(F32)
                term = prob * work_s[h % 2, :, tile]
                weighted = jnp.sum(term, axis=0, keepdims=True)
                ds_s[h % 2, :, tile] = (term - prob * weighted).astype(BF)

        def back(h):
            ds = ds_s[h % 2]
            da3_s[of(0, h), cols] = (nn(qkv_s[of(1, h), cols], ds) * scale).astype(BF)
            da3_s[of(1, h), cols] = nt(qkv_s[of(0, h), cols], ds).astype(BF)
            da3_s[of(2, h), cols] = nt(do_s[of(0, h), cols], prob_s[b, h]).astype(BF)

        slope(0)
        for h in range(HEADS):
            if h + 1 < HEADS:
                slope(h + 1)
            score_grad(h)
            if h > 0:
                back(h - 1)
        back(HEADS - 1)
        return 0

    lax.fori_loop(0, BLOCKS, backward, 0)
    dqkv_s[...] = nt(h1_s[...], da3_s[...])

    def last(b, _):
        cols = block_cols(b)
        grad = nn(wqkv_s[:WIDTH, :], da3_s[:, cols])
        normal, inverse = normal_parts(x_s[:, cols].astype(F32))
        acc_s[0] += grad * normal
        acc_s[1] += grad
        gtok = dy1_s[:, cols] + norm_back(grad, normal, inverse, wide(gains[0]))
        gtok_ref[:, cols] = gtok.astype(BF)
        return 0

    lax.fori_loop(0, BLOCKS, last, 0)
    for k in range(4):
        both = acc_s[k]
        column = both[:, :128] + both[:, 128:]
        dnorm_s[k : k + 1, :] = jnp.sum(column.T, axis=0, keepdims=True)
    ddown_n[...] = ddown_s[...].T
    pack_grads(plan, part_ref, dqkv_s, dproj_s, dup_s, ddown_n, dnorm_s)
    reduce(plan, part_ref, sum_ref, acc, got_c, got_f, got_x, got_z, r_send, r_c, r_f, r_x, r_z)


def main_call(plan, order, tokens, cotan, qkv, proj, up, down, vec):
    vmem = pl.BlockSpec(memory_space=pltpu.VMEM)
    one = (plan.pack_rows, plan.pack_cols)
    n_c = plan.n_z * plan.n_x * plan.n_fs
    n_f = plan.n_z * plan.n_x * (plan.n_fs - 1)
    n_x = plan.n_z * (plan.n_x - 1)
    n_z = plan.n_z - 1
    return pl.pallas_call(
        partial(main_kernel, plan),
        out_shape=(
            jax.ShapeDtypeStruct((WIDTH, COLS), BF),
            jax.ShapeDtypeStruct((WIDTH, COLS), BF),
            jax.ShapeDtypeStruct(one, F32),
        ),
        in_specs=[pl.BlockSpec(memory_space=pltpu.SMEM)] + [vmem] * 7,
        out_specs=(vmem,) * 3,
        scratch_shapes=[
            pltpu.VMEM((plan.slots,) + one, BF),
            pltpu.VMEM((plan.slots,) + one, BF),
            pltpu.VMEM(one, BF),
            pltpu.VMEM((n_c,) + one, BF),
            pltpu.VMEM((n_c,) + one, BF),
            pltpu.VMEM((n_f,) + one, BF),
            pltpu.VMEM((n_x,) + one, BF),
            pltpu.VMEM((n_z,) + one, BF),
            pltpu.SemaphoreType.DMA((plan.slots - 1,)),
            pltpu.SemaphoreType.DMA((plan.slots,)),
            pltpu.SemaphoreType.DMA,
            pltpu.SemaphoreType.DMA((n_c + n_f + n_x + n_z,)),
            pltpu.SemaphoreType.DMA((n_c,)),
            pltpu.SemaphoreType.DMA((n_f,)),
            pltpu.SemaphoreType.DMA((n_x,)),
            pltpu.SemaphoreType.DMA((n_z,)),
            pltpu.SMEM((BIGS,), jnp.int32),
            pltpu.SMEM((26,), jnp.int32),
            pltpu.VMEM((EXT, 3 * WIDTH), BF),
            pltpu.VMEM((EXT, WIDTH), BF),
            pltpu.VMEM((EXT, FF), BF),
            pltpu.VMEM((FF_EXT, WIDTH), BF),
            pltpu.VMEM((16, WIDTH), BF),
            pltpu.VMEM((3 * WIDTH, EXT), BF),
            pltpu.VMEM((WIDTH, EXT), BF),
            pltpu.VMEM((FF, EXT), BF),
            pltpu.VMEM((WIDTH, FF_EXT), BF),
            pltpu.VMEM((4, WIDTH, 128), F32),
            pltpu.VMEM((2, LANES, LANES), F32),
            pltpu.VMEM((WIDTH, COLS), BF),
            pltpu.VMEM((WIDTH, COLS), BF),
            pltpu.VMEM((EXT, COLS), BF),
            pltpu.VMEM((3 * WIDTH, COLS), BF),
            pltpu.VMEM((BLOCKS, HEADS, LANES, LANES), BF),
            pltpu.VMEM((EXT, COLS), BF),
            pltpu.VMEM((EXT, LANES), BF),
            pltpu.VMEM((FF_EXT, LANES), BF),
            pltpu.VMEM((FF, LANES), BF),
            pltpu.VMEM((WIDTH, COLS), BF),
            pltpu.VMEM((WIDTH, COLS), F32),
            pltpu.VMEM((WIDTH, COLS), BF),
            pltpu.VMEM((3 * WIDTH, COLS), BF),
            pltpu.VMEM((EXT, 3 * WIDTH), F32),
            pltpu.VMEM((EXT, WIDTH), F32),
            pltpu.VMEM((EXT, FF), F32),
            pltpu.VMEM((WIDTH, FF_EXT), F32),
            pltpu.VMEM((FF_EXT, WIDTH), F32),
            pltpu.VMEM((4, WIDTH), F32),
            pltpu.VMEM((4, WIDTH, LANES), F32),
            pltpu.VMEM((2, LANES, LANES), F32),
            pltpu.VMEM((2, LANES, LANES), BF),
            pltpu.VMEM((BLOCKS, 1, LANES), jnp.int32),
        ],
        compiler_params=pltpu.CompilerParams(
            collective_id=0, has_side_effects=True, vmem_limit_bytes=64 * 1024 * 1024 - 65536
        ),
        name="block_main",
    )(order, tokens, cotan, qkv, proj, up, down, vec)


def place_kernel(plan, order_ref, out_c_ref, gtok_c_ref, sum_ref, *refs):
    out_ref, gtok_ref, dqkv_ref, dproj_ref, dup_ref, ddown_ref = refs[:6]
    vectors = refs[6:15]
    big_start, small_start, out_s, gtok_s = refs[15:]
    slot_starts(order_ref, big_start, small_start)
    out_s[...] = jnp.zeros_like(out_s)
    gtok_s[...] = jnp.zeros_like(gtok_s)

    def place(block, paired):
        cols = block_cols(block)
        rows = jnp.concatenate([out_c_ref[:, cols], gtok_c_ref[:, cols]], axis=0)
        for start, length, lane0, size in pieces_of(block, big_start, small_start, paired):
            columns, offset = window(start, size)
            moved = nn(rows, chooser(offset, length, lane0, size, False))
            out_s[:, columns] += moved[:WIDTH].astype(BF)
            gtok_s[:, columns] += moved[WIDTH:]

    def place_paired(b, _):
        place(b, True)
        return 0

    def place_small(b, _):
        place(b, False)
        return 0

    lax.fori_loop(0, BIGS, place_paired, 0)
    lax.fori_loop(BIGS, BLOCKS, place_small, 0)
    out_ref[...] = out_s[:, :ROWS]
    gtok_ref[...] = gtok_s[:, :ROWS]
    r, v = plan.rows, plan.vec
    dqkv_ref[...] = sum_ref[:r, : plan.qkv].T
    dproj_ref[...] = sum_ref[:r, plan.at_proj : plan.at_proj + v].T
    dup_ref[...] = sum_ref[:r, plan.at_up : plan.at_up + plan.up]
    for c in range(4):
        ddown_ref[:, c * r : (c + 1) * r] = sum_ref[:r, plan.at_down + c * v : plan.at_down + (c + 1) * v].T
    for k in range(9):
        width = v if k < 8 else plan.up
        vectors[k][...] = sum_ref[r : r + 1, k * v : k * v + width]


def place_call(plan, order, out_c, gtok_c, total):
    vmem = pl.BlockSpec(memory_space=pltpu.VMEM)
    f32 = lambda *shape: jax.ShapeDtypeStruct(shape, F32)
    r, v = plan.rows, plan.vec
    return pl.pallas_call(
        partial(place_kernel, plan),
        out_shape=(
            jax.ShapeDtypeStruct((WIDTH, ROWS), BF),
            f32(WIDTH, ROWS),
            f32(plan.qkv, r),
            f32(v, r),
            f32(r, plan.up),
            f32(v, 4 * r),
        )
        + (f32(1, v),) * 8
        + (f32(1, plan.up),),
        in_specs=[pl.BlockSpec(memory_space=pltpu.SMEM)] + [vmem] * 3,
        out_specs=(vmem,) * 15,
        scratch_shapes=[
            pltpu.SMEM((BIGS,), jnp.int32),
            pltpu.SMEM((26,), jnp.int32),
            pltpu.VMEM((WIDTH, ROWS_PAD), BF),
            pltpu.VMEM((WIDTH, ROWS_PAD), F32),
        ],
        compiler_params=pltpu.CompilerParams(vmem_limit_bytes=48 * 1024 * 1024),
        name="block_place",
    )(order, out_c, gtok_c, total)


def local(plan, *args):
    (
        tokens,
        cotangent,
        crop_order,
        ln1_gain,
        ln1_bias,
        w_qkv,
        b_query,
        b_value,
        w_proj,
        b_proj,
        ln2_gain,
        ln2_bias,
        w_up,
        b_up,
        w_down,
        b_down,
    ) = args
    vec = jnp.concatenate([ln1_gain, ln1_bias, b_query, b_value, b_proj, ln2_gain, ln2_bias, b_down, b_up])
    out_c, gtok_c, total = main_call(
        plan, crop_order, tokens.T, cotangent.T, w_qkv.T, w_proj.T, w_up, w_down.T, vec[None]
    )
    out, gtok, dqkv, dproj, dup, ddown, *vectors = place_call(plan, crop_order, out_c, gtok_c, total)
    g1, s1, bq, bv, bp, g2, s2, bd, bu = [one[0] for one in vectors]
    return (out.T, gtok.T, g1, s1, dqkv.T, bq, bv, dproj.T, bp, g2, s2, dup, bu, ddown.T, bd)


def solution(mesh):
    plan = Plan(mesh.shape["dp"], mesh.shape["fsdp"])
    rows = P(("dp", "fsdp"), None)
    vec = P("dp")
    mat = P("fsdp", "dp")
    return jax.shard_map(
        partial(local, plan),
        mesh=mesh,
        in_specs=(rows, rows, rows, vec, vec, mat, vec, vec, mat, vec, vec, vec, mat, vec, mat, vec),
        out_specs=(rows, rows, vec, vec, mat, vec, vec, mat, vec, vec, vec, mat, vec, mat, vec),
        check_vma=False,
    )
```

```python
from functools import partial

import jax
import jax.numpy as jnp
from jax import lax
from jax.experimental import pallas as pl
from jax.experimental.pallas import tpu as pltpu
from jax.sharding import PartitionSpec as P

HEADS = 6
HEAD_DIM = 48
BIG_LEN = 197
SMALL_LEN = 37
BIGS = 8
SMALLS = 24
WIDTH = 288
EXT = 304
FF = 1152
FF_EXT = 1168
ROWS = 2464
ROWS_PAD = 2560
LANES = 256
BLOCKS = 11
COLS = BLOCKS * LANES
KEYS = 240
BIG_WIN = 384
SMALL_WIN = 256
FF_STEP = 288
VECTORS = 9
EPS = 1e-06
BF = jnp.bfloat16
F32 = jnp.float32
MESH = pl.DeviceIdType.MESH
VMEM_LIMIT = 64 * 1024 * 1024 - 65536


def nn(a, b):
    return jnp.dot(a, b, preferred_element_type=F32)


def nt(a, b):
    return lax.dot_general(a, b, (((1,), (1,)), ((), ())), preferred_element_type=F32)


def tn(a, b):
    return lax.dot_general(a, b, (((0,), (0,)), ((), ())), preferred_element_type=F32)


def iota(shape, dim):
    return lax.broadcasted_iota(jnp.int32, shape, dim)


def wide(col):
    return jnp.concatenate([col, col], axis=1)


def block_cols(b):
    return pl.ds(pl.multiple_of(b * LANES, LANES), LANES)


def up_to(size, unit):
    return -(-size // unit) * unit


class Plan:
    def __init__(self, n_dp, n_fs):
        self.n_dp, self.n_fs = n_dp, n_fs
        self.n_core = 2
        self.n_z = 4
        self.n_x = n_dp // (self.n_core * self.n_z)
        self.slots = n_dp * n_fs
        self.rows = WIDTH // n_fs
        self.qkv, self.vec, self.up = 3 * WIDTH // n_dp, WIDTH // n_dp, FF // n_dp
        self.q_wide = up_to(self.rows, 128) // 128
        self.q_tiles = up_to(self.qkv + VECTORS, 16) // 16 * self.q_wide
        self.u_tiles = up_to(self.rows, 16) // 16
        self.d_wide = up_to(5 * self.rows, 128) // 128
        self.r_tiles = self.u_tiles + up_to(self.vec, 16) // 16 * self.d_wide

    def dp(self, z, x, core):
        return (z * self.n_x + x) * self.n_core + core

    def slot(self, z, x, core, fs):
        return self.dp(z, x, core) * self.n_fs + fs

    def here(self):
        dp, fs = lax.axis_index("dp"), lax.axis_index("fsdp")
        core = lax.rem(dp, self.n_core)
        rest = lax.div(dp, self.n_core)
        return lax.div(rest, self.n_x), lax.rem(rest, self.n_x), core, fs


def cuts(row, col, rows, cols):
    done = 0
    while done < rows:
        tile, first = divmod(row + done, 16)
        count = min(16 - first, rows - done)
        across = 0
        while across < cols:
            lane_tile, lane = divmod(col + across, 128)
            width = min(128 - lane, cols - across)
            yield tile, lane_tile, first, lane, count, width, done, across
            across += width
        done += count


def put(ref, base, wide_by, row, col, value):
    for tile, lane_tile, first, lane, count, width, i, j in cuts(row, col, *value.shape):
        ref[base + tile * wide_by + lane_tile, first : first + count, lane : lane + width] = value[
            i : i + count, j : j + width
        ]


def get(ref, base, wide_by, row, col, rows, cols, target, top, left):
    for tile, lane_tile, first, lane, count, width, i, j in cuts(row, col, rows, cols):
        target[top + i : top + i + count, left + j : left + j + width] = ref[
            base + tile * wide_by + lane_tile, first : first + count, lane : lane + width
        ]


class Links:
    def __init__(self, plan):
        self.plan = plan
        self.z, self.x, self.core, self.fs = plan.here()
        self.zs = [lax.rem(self.z + d, plan.n_z) for d in range(plan.n_z)]
        self.xs = [lax.rem(self.x + d, plan.n_x) for d in range(plan.n_x)]
        self.fss = [lax.rem(self.fs + d, plan.n_fs) for d in range(plan.n_fs)]
        self.peer = lax.rem(self.core + 1, 2)
        self.to_core = (plan.dp(self.z, self.x, self.peer), self.fs)
        self.to_fs = [(plan.dp(self.z, self.x, self.core), fs) for fs in self.fss]
        self.to_x = [(plan.dp(self.z, x, self.core), self.fs) for x in self.xs]
        self.to_z = [(plan.dp(z, self.x, self.core), self.fs) for z in self.zs]

    def slot(self, dz, dx, dc, df):
        return self.plan.slot(self.zs[dz], self.xs[dx], (self.core, self.peer)[dc], self.fss[df])

    def meet(self):
        barrier = pltpu.get_barrier_semaphore()
        places = [self.to_core] + self.to_fs[1:] + self.to_x[1:] + self.to_z[1:]
        for place in places:
            pl.semaphore_signal(barrier, inc=1, device_id=place, device_id_type=MESH)
        pl.semaphore_wait(barrier, len(places))


def remote(src, dst, send_sem, recv_sem, place):
    return pltpu.make_async_remote_copy(
        src_ref=src, dst_ref=dst, send_sem=send_sem, recv_sem=recv_sem, device_id=place, device_id_type=MESH
    )


class Gather:
    def __init__(self, links, whole, send_sem, recv_sem):
        self.links, self.whole, self.send_sem, self.recv_sem = links, whole, send_sem, recv_sem
        plan = links.plan
        z, x, f = range(1, plan.n_z), range(1, plan.n_x), range(1, plan.n_fs)
        to_f = [links.to_fs[d] for d in f]
        to_xf = [links.to_x[d] for d in x] + to_f
        self.stages = [
            [((0, 0, 0, 0), [links.to_z[d] for d in z] + to_xf + [links.to_core])],
            [((dz, 0, 0, 0), to_xf + [links.to_core]) for dz in z],
            [((dz, dx, 0, 0), to_f + [links.to_core]) for dx in x for dz in range(plan.n_z)],
            [((dz, dx, 0, df), [links.to_core]) for df in f for dx in range(plan.n_x) for dz in range(plan.n_z)],
            [
                ((dz, dx, 1, df), [])
                for df in range(plan.n_fs)
                for dx in range(plan.n_x)
                for dz in range(plan.n_z)
            ],
        ]
        count = 0
        self.work = []
        for stage in self.stages:
            steps = []
            for steps_to, places in stage:
                steps.append((links.slot(*steps_to), [(count + n, place) for n, place in enumerate(places)]))
                count += len(places)
            self.work.append(steps)

    def copy(self, slot, index, place):
        one = self.whole.at[slot]
        return remote(one, one, self.send_sem.at[index], self.recv_sem.at[slot], place)

    def stage(self, number):
        for slot, sends in self.work[number]:
            if number:
                self.copy(slot, 0, self.links.to_core).wait_recv()
            for index, place in sends:
                self.copy(slot, index, place).start()

    def close(self):
        for steps in self.work:
            for slot, sends in steps:
                for index, place in sends:
                    self.copy(slot, index, place).wait_send()


class Reduce:
    def __init__(self, links, part, got, send_sem, recv_sem):
        self.links, self.part, self.got, self.send_sem, self.recv_sem = links, part, got, send_sem, recv_sem
        plan = links.plan
        nz, nx, nf = plan.n_z, plan.n_x, plan.n_fs
        last = lambda n: list(range(1, n)) + [0]
        order = [(df, dx, dz) for df in last(nf) for dx in last(nx) for dz in last(nz)]
        at_f = nf * nx * nz
        at_x = at_f + (nf - 1) * nx * nz
        at_z = at_x + (nx - 1) * nz
        self.count = at_z + nz - 1
        spot_c = lambda df, dx, dz: (df * nx + dx) * nz + dz
        spot_f = lambda df, dx, dz: at_f + ((df - 1) * nx + dx) * nz + dz
        spot_x = lambda dx, dz: at_x + (dx - 1) * nz + dz
        spot_z = lambda dz: at_z + dz - 1
        self.first = [(links.slot(dz, dx, 1, df), spot_c(df, dx, dz), links.to_core) for df, dx, dz in order]
        self.stages = [[], [], [], []]
        for df, dx, dz in order:
            slot = links.slot(dz, dx, 0, df)
            takes = [spot_c(df, dx, dz)]
            if df:
                self.stages[0].append((slot, takes, spot_f(nf - df, dx, dz), links.to_fs[df]))
                continue
            takes += [spot_f(d, dx, dz) for d in range(1, nf)]
            if dx:
                self.stages[1].append((slot, takes, spot_x(nx - dx, dz), links.to_x[dx]))
                continue
            takes += [spot_x(d, dz) for d in range(1, nx)]
            if dz:
                self.stages[2].append((slot, takes, spot_z(nz - dz), links.to_z[dz]))
                continue
            takes += [spot_z(d) for d in range(1, nz)]
            self.stages[3].append((slot, takes, None, None))

    def copy(self, slot, spot, place):
        return remote(
            self.part.at[slot], self.got.at[spot], self.send_sem.at[spot], self.recv_sem.at[spot], place
        )

    def start(self):
        for slot, spot, place in self.first:
            self.copy(slot, spot, place).start()

    def stage(self, number):
        for slot, takes, spot, place in self.stages[number]:
            total = self.part[slot].astype(F32)
            for index in takes:
                self.copy(slot, index, self.links.to_core).wait_recv()
                total = total + self.got[index].astype(F32)
            if place is None:
                return total
            self.part[slot] = total.astype(BF)
            self.copy(slot, spot, place).start()

    def close(self):
        for slot, spot, place in self.first:
            self.copy(slot, spot, place).wait_send()
        for steps in self.stages[:3]:
            for slot, _, spot, place in steps:
                self.copy(slot, spot, place).wait_send()


def normal_parts(rows):
    mean = jnp.sum(rows, axis=0, keepdims=True) * (1.0 / WIDTH)
    centered = rows - mean
    variance = jnp.sum(centered * centered, axis=0, keepdims=True) * (1.0 / WIDTH)
    inverse = lax.rsqrt(variance + EPS)
    return centered * inverse, inverse


def norm_back(grad, normal, inverse, gain):
    scaled = grad * gain
    first = jnp.sum(scaled, axis=0, keepdims=True) * (1.0 / WIDTH)
    second = jnp.sum(scaled * normal, axis=0, keepdims=True) * (1.0 / WIDTH)
    return inverse * (scaled - first - normal * second)


def gelu_both(u):
    z = jnp.abs(u)
    d = 1.0 + z * (0.3275911 * 0.7071067811865476)
    t = pl.reciprocal(d, approx=True)
    t = t * (2.0 - d * t)
    e = jnp.exp(u * u * -0.5)
    poly = 0.5 * 1.061405429
    poly = poly * t + 0.5 * -1.453152027
    poly = poly * t + 0.5 * 1.421413741
    poly = poly * t + 0.5 * -0.284496736
    poly = poly * t + 0.5 * 0.254829592
    tail = poly * t * e
    phi = jnp.where(u >= 0.0, 1.0 - tail, tail)
    return u * phi, phi + u * e * 0.3989422804014327


def slot_starts(order_ref, big_start, small_start):
    far = jnp.int32(1 << 20)

    def one(j, carry):
        row, big_count, starts = carry
        big = jnp.where(order_ref[0, j] < BIGS, 1, 0)
        rank = jnp.where(big == 1, big_count, BIGS + j - big_count)
        starts = tuple(jnp.where(rank == k, row, start) for k, start in enumerate(starts))
        return row + SMALL_LEN + (BIG_LEN - SMALL_LEN) * big, big_count + big, starts

    _, _, starts = lax.fori_loop(
        0, BIGS + SMALLS, one, (jnp.int32(0), jnp.int32(0), (far,) * (BIGS + SMALLS + 2))
    )
    for k in range(BIGS):
        big_start[k] = starts[k]
    for k in range(SMALLS + 2):
        small_start[k] = starts[BIGS + k]


def window(start, size):
    first = jnp.minimum(start - lax.rem(start, jnp.int32(128)), ROWS_PAD - size)
    return pl.ds(pl.multiple_of(first, 128), size), start - first


def pieces_of(block, big_start, small_start, paired):
    if paired:
        return [
            (big_start[block], BIG_LEN, 0, BIG_WIN),
            (small_start[block], SMALL_LEN, BIG_LEN, SMALL_WIN),
        ]
    base = BIGS + 6 * (block - BIGS)
    return [(small_start[base + k], SMALL_LEN, SMALL_LEN * k, SMALL_WIN) for k in range(6)]


def chooser(offset, length, lane0, size, inward):
    shape = (size, LANES) if inward else (LANES, size)
    lane = iota(shape, 1 if inward else 0)
    column = iota(shape, 0 if inward else 1)
    hit = (column - lane == offset - lane0) & (lane >= lane0) & (lane < lane0 + length)
    return jnp.where(hit, 1.0, 0.0).astype(BF)


def crop_mask(paired):
    key = iota((KEYS, LANES), 0)
    query = iota((KEYS, LANES), 1)
    if paired:
        label_key = jnp.where(key < BIG_LEN, 0, jnp.where(key < BIG_LEN + SMALL_LEN, 1, 2))
        label_query = jnp.where(query < BIG_LEN, 0, jnp.where(query < BIG_LEN + SMALL_LEN, 1, 2))
    else:
        label_key = jnp.zeros_like(key)
        label_query = jnp.zeros_like(key)
        for k in range(1, 7):
            label_key = label_key + jnp.where(key >= SMALL_LEN * k, 1, 0)
            label_query = label_query + jnp.where(query >= SMALL_LEN * k, 1, 0)
    return jnp.where(label_key == label_query, 0.0, -1e30)


def pack_own(plan, q, r, qkv_ref, proj_ref, up_ref, down_ref, vector_refs):
    q[...] = jnp.zeros_like(q)
    r[...] = jnp.zeros_like(r)
    put(q, 0, plan.q_wide, 0, 0, qkv_ref[...])
    for k, ref in enumerate(vector_refs):
        put(q, 0, plan.q_wide, plan.qkv + k, 0, ref[...].reshape(1, ref.shape[0]))
    put(r, 0, 1, 0, 0, up_ref[...])
    put(r, plan.u_tiles, plan.d_wide, 0, 0, down_ref[...])
    put(r, plan.u_tiles, plan.d_wide, 0, 4 * plan.rows, proj_ref[...])


def unpack_q(plan, all_q, s):
    r, v, qkv, up = plan.rows, plan.vec, plan.qkv, plan.up
    s.vec_s[...] = jnp.zeros_like(s.vec_s)
    s.wup_n[WIDTH:, :] = jnp.zeros((EXT - WIDTH, FF), BF)
    for i in range(plan.n_dp):
        for j in range(plan.n_fs):
            get(all_q.at[i * plan.n_fs + j], 0, plan.q_wide, 0, 0, qkv, r, s.wqkv_t, i * qkv, j * r)
        one = all_q.at[i * plan.n_fs]
        get(one, 0, plan.q_wide, qkv, 0, VECTORS - 1, v, s.vec_s, 0, i * v)
        get(one, 0, plan.q_wide, qkv + VECTORS - 1, 0, 1, up, s.wup_n, WIDTH, i * up)
    columns = s.vec_s[...].T
    lane = iota((WIDTH, 16), 1)
    none = jnp.zeros((WIDTH, 16), BF)
    s.wqkv_t[:WIDTH, WIDTH:] = jnp.where(lane == 2, columns, none)
    s.wqkv_t[WIDTH : 2 * WIDTH, WIDTH:] = none
    s.wqkv_t[2 * WIDTH :, WIDTH:] = jnp.where(lane == 3, columns, none)
    s.wproj_t[:, WIDTH:] = jnp.where(lane == 4, columns, none)
    s.wdown_t[:, FF:] = jnp.where(lane == 7, columns, none)
    for n, k in enumerate((0, 1, 5, 6)):
        pick = jnp.where(iota((16, 128), 0) == k, 1.0, 0.0).astype(BF)
        s.gains[n] = tn(s.vec_s[...], pick)


def unpack_r(plan, all_r, s):
    r, v, up = plan.rows, plan.vec, plan.up
    for i in range(plan.n_dp):
        for j in range(plan.n_fs):
            one = all_r.at[i * plan.n_fs + j]
            get(one, 0, 1, 0, 0, r, up, s.wup_n, j * r, i * up)
            get(one, plan.u_tiles, plan.d_wide, 0, 0, v, 4 * r, s.wdown_t, i * v, j * 4 * r)
            get(one, plan.u_tiles, plan.d_wide, 0, 4 * r, v, r, s.wproj_t, i * v, j * r)


def pack_r(plan, part, s):
    r, v, up = plan.rows, plan.vec, plan.up
    for i in range(plan.n_dp):
        for j in range(plan.n_fs):
            one = part.at[i * plan.n_fs + j]
            put(one, 0, 1, 0, 0, s.dup_s[j * r : (j + 1) * r, i * up : (i + 1) * up].astype(BF))
            down = s.ddown_s[i * v : (i + 1) * v, j * 4 * r : (j + 1) * 4 * r].astype(BF)
            put(one, plan.u_tiles, plan.d_wide, 0, 0, down)
            proj = s.dproj_s[i * v : (i + 1) * v, j * r : (j + 1) * r].astype(BF)
            put(one, plan.u_tiles, plan.d_wide, 0, 4 * r, proj)


def pack_q(plan, part, s):
    r, v, qkv, up = plan.rows, plan.vec, plan.qkv, plan.up
    for i in range(plan.n_dp):
        vectors = s.dvec_s[:, i * v : (i + 1) * v].astype(BF)
        bias_up = s.dup_s[WIDTH : WIDTH + 1, i * up : (i + 1) * up].astype(BF)
        for j in range(plan.n_fs):
            one = part.at[i * plan.n_fs + j]
            put(one, 0, plan.q_wide, 0, 0, s.dqkv_s[i * qkv : (i + 1) * qkv, j * r : (j + 1) * r].astype(BF))
            put(one, 0, plan.q_wide, qkv, 0, vectors)
            put(one, 0, plan.q_wide, qkv + VECTORS - 1, 0, bias_up)


class Scratch:
    pass


def scratch_list(plan):
    vmem, smem = pltpu.VMEM, pltpu.SMEM
    tile = (16, 128)
    return dict(
        big_start=smem((BIGS,), jnp.int32),
        small_start=smem((SMALLS + 2,), jnp.int32),
        target_s=vmem((BLOCKS, 1, LANES), jnp.int32),
        wqkv_t=vmem((3 * WIDTH, EXT), BF),
        wproj_t=vmem((WIDTH, EXT), BF),
        wup_t=vmem((FF, EXT), BF),
        wdown_t=vmem((WIDTH, FF_EXT), BF),
        wqkv_n=vmem((WIDTH, 3 * WIDTH), BF),
        wproj_n=vmem((WIDTH, WIDTH), BF),
        wup_n=vmem((EXT, FF), BF),
        wdown_n=vmem((FF, WIDTH), BF),
        vec_s=vmem((16, WIDTH), BF),
        gains=vmem((4, WIDTH, 128), F32),
        mask_s=vmem((2, KEYS, LANES), F32),
        x_s=vmem((WIDTH, COLS), BF),
        c_s=vmem((WIDTH, COLS), BF),
        xhat_s=vmem((EXT, COLS), BF),
        qkv_s=vmem((3 * WIDTH, COLS), BF),
        prob_s=vmem((BLOCKS, HEADS, KEYS, LANES), BF),
        ctx_s=vmem((EXT, COLS), BF),
        h2_a=vmem((EXT, LANES), BF),
        h2_b=vmem((EXT, LANES), BF),
        act_a=vmem((FF_EXT, LANES), BF),
        act_b=vmem((FF_EXT, LANES), BF),
        du_a=vmem((FF, LANES), BF),
        du_b=vmem((FF, LANES), BF),
        mid_a=vmem((WIDTH, LANES), F32),
        mid_b=vmem((WIDTH, LANES), F32),
        da_s=vmem((WIDTH, COLS), BF),
        do_s=vmem((WIDTH, COLS), BF),
        da3_s=vmem((3 * WIDTH, COLS), BF),
        dqkv_s=vmem((3 * WIDTH, EXT), F32),
        dproj_s=vmem((WIDTH, EXT), F32),
        dup_s=vmem((EXT, FF), F32),
        ddown_s=vmem((WIDTH, FF_EXT), F32),
        dvec_s=vmem((8, WIDTH), F32),
        acc_s=vmem((2, WIDTH, LANES), F32),
        work_s=vmem((3, KEYS, LANES), F32),
        ds_s=vmem((3, KEYS, LANES), BF),
        out_sem=pltpu.SemaphoreType.DMA((2,)),
    )


def link_list(plan):
    vmem, dma = pltpu.VMEM, pltpu.SemaphoreType.DMA
    tile = (16, 128)
    hops = plan.slots - 1
    return dict(
        all_q=vmem((plan.slots, plan.q_tiles) + tile, BF),
        all_r=vmem((plan.slots, plan.r_tiles) + tile, BF),
        got_q=vmem((hops, plan.q_tiles) + tile, BF),
        got_r=vmem((hops, plan.r_tiles) + tile, BF),
        gq_send=dma((hops,)),
        gq_recv=dma((plan.slots,)),
        gr_send=dma((hops,)),
        gr_recv=dma((plan.slots,)),
        rq_send=dma((hops,)),
        rq_recv=dma((hops,)),
        rr_send=dma((hops,)),
        rr_recv=dma((hops,)),
    )


def pair_loop(first, even, odd, last, service=None):
    first()

    def one(i, _):
        if service is not None:
            service(i)
        even(2 * i)
        odd(2 * i + 1)
        return 0

    lax.fori_loop(0, (BLOCKS - 1) // 2, one, 0)
    last()


def at_step(i, actions):
    for step, action in actions.items():
        pl.when(i == step)(action)


def main_kernel(plan, solo, names, order_ref, tokens_ref, cotan_ref, qkv_ref, proj_ref, up_ref, down_ref, *refs):
    vector_refs, refs = refs[:VECTORS], refs[VECTORS:]
    s = Scratch()
    if solo:
        s.all_q, s.all_r = refs[:2]
        refs = refs[2:]
    out_ref, gtok_ref, sum_q, sum_r = refs[:4]
    for name, ref in zip(names, refs[4:]):
        setattr(s, name, ref)
    if solo:
        s.part_q, s.part_r = sum_q, sum_r
    else:
        s.part_q, s.part_r = s.all_q, s.all_r
        links = Links(plan)
        gq = Gather(links, s.all_q, s.gq_send, s.gq_recv)
        gr = Gather(links, s.all_r, s.gr_send, s.gr_recv)
        rq = Reduce(links, s.part_q, s.got_q, s.rq_send, s.rq_recv)
        rr = Reduce(links, s.part_r, s.got_r, s.rr_send, s.rr_recv)
        mine = links.slot(0, 0, 0, 0)
        pack_own(plan, s.all_q.at[mine], s.all_r.at[mine], qkv_ref, proj_ref, up_ref, down_ref, vector_refs)
        links.meet()
        gq.stage(0)

    s.da3_s[: 2 * WIDTH, ROWS_PAD - 128 : ROWS_PAD] = jnp.zeros((2 * WIDTH, 128), BF)
    s.da3_s[:WIDTH, :ROWS] = tokens_ref[...]
    s.da3_s[WIDTH : 2 * WIDTH, :ROWS] = cotan_ref[...]
    slot_starts(order_ref, s.big_start, s.small_start)
    lane = iota((1, LANES), 1)
    for b in range(BLOCKS):
        if b < BIGS:
            small = s.small_start[b] - BIG_LEN
            target = jnp.where(lane < BIG_LEN + SMALL_LEN, small + lane, -1)
            target = jnp.where(lane < BIG_LEN, s.big_start[b] + lane, target)
        else:
            target = jnp.full((1, LANES), -1, jnp.int32)
            for k in range(6):
                start = s.small_start[BIGS + 6 * (b - BIGS) + k] - SMALL_LEN * k
                target = jnp.where((lane >= SMALL_LEN * k) & (lane < SMALL_LEN * (k + 1)), start + lane, target)
        s.target_s[b] = target

    def load(b):
        if b < BIGS:
            low, high = SMALL_LEN * b, max(BIG_LEN * b + SMALL_LEN * SMALLS + BIG_LEN, SMALL_LEN * (b + 1) + BIG_LEN * BIGS)
        else:
            k = BIGS + 6 * (b - BIGS)
            low, high = SMALL_LEN * k, SMALL_LEN * min(k + 6, SMALLS) + BIG_LEN * BIGS
        low, high = low // 128 * 128, min(up_to(high, 128), ROWS_PAD)
        hit = iota((high - low, LANES), 0) + low == s.target_s[b]
        both = nn(s.da3_s[: 2 * WIDTH, low:high], jnp.where(hit, 1.0, 0.0).astype(BF))
        s.x_s[:, b * LANES : (b + 1) * LANES] = both[:WIDTH].astype(BF)
        s.c_s[:, b * LANES : (b + 1) * LANES] = both[WIDTH:].astype(BF)

    for b in range(0, 2):
        load(b)
    if not solo:
        gq.stage(1)
    for b in range(2, 4):
        load(b)
    if not solo:
        gq.stage(2)
    for b in range(4, 7):
        load(b)
    if not solo:
        gq.stage(3)
        gr.stage(0)
    for b in range(7, 11):
        load(b)
    if not solo:
        gr.stage(1)
        gq.stage(4)

    unpack_q(plan, s.all_q, s)
    s.mask_s[0] = crop_mask(True)
    s.mask_s[1] = crop_mask(False)
    ones = jnp.ones((16, COLS), BF)
    s.xhat_s[WIDTH:, :] = ones
    s.ctx_s[WIDTH:, :] = ones
    s.h1_a, s.h1_b, s.live_a, s.live_b = s.h2_a, s.h2_b, s.act_a, s.act_b
    for ref in (s.h2_a, s.h2_b):
        ref[WIDTH:, :] = ones[:, :LANES]
    for ref in (s.act_a, s.act_b):
        ref[FF:, :] = ones[:, :LANES]
    s.acc_s[...] = jnp.zeros_like(s.acc_s)
    s.dup_s[...] = jnp.zeros_like(s.dup_s)
    s.ddown_s[...] = jnp.zeros_like(s.ddown_s)
    scale = HEAD_DIM ** (-0.5)
    blank = jnp.zeros((HEAD_DIM, LANES), BF)

    def head_rows(part, h):
        return slice(part * WIDTH + HEAD_DIM * h, part * WIDTH + HEAD_DIM * (h + 1))

    def pair_rows(part, h):
        low = part * WIDTH + 2 * HEAD_DIM * (h // 2)
        return slice(low, low + 2 * HEAD_DIM)

    def beside(rows, h):
        return jnp.concatenate([rows, blank] if h % 2 == 0 else [blank, rows], axis=0)

    def project(b, live, h1):
        cols = block_cols(b)

        def norm():
            normal, _ = normal_parts(s.x_s[:, cols].astype(F32))
            s.xhat_s[:WIDTH, cols] = normal.astype(BF)
            h1[:WIDTH, :] = (normal * wide(s.gains[0]) + wide(s.gains[1])).astype(BF)

        def part(k):
            rows = slice(k * WIDTH, (k + 1) * WIDTH)
            mixed = nn(s.wqkv_t[rows, :], h1[...])
            mixed = ((mixed * scale) if k == 0 else mixed).astype(BF)
            live[rows, :] = mixed
            s.qkv_s[rows, cols] = mixed

        return [norm, lambda: part(0), lambda: part(1), lambda: part(2)]

    def attend(b, live, beside_it=()):
        cols = block_cols(b)
        kind = jnp.where(b < BIGS, 0, 1)
        beside_it = list(beside_it)

        def score(h):
            keys = live[pair_rows(1, h), :KEYS].T
            s.work_s[h % 3] = nn(keys, beside(live[head_rows(0, h), :], h))

        def spread_out(h):
            for tile in (slice(0, 128), slice(128, 256)):
                scores = s.work_s[h % 3, :, tile] + s.mask_s[kind, :, tile]
                top = jnp.max(scores, axis=0, keepdims=True)
                expo = jnp.exp(scores - top)
                total = jnp.sum(expo, axis=0, keepdims=True)
                s.prob_s[b, h, :, tile] = (expo * (1.0 / total)).astype(BF)

        def mix(h):
            s.ctx_s[head_rows(0, h), cols] = nn(live[head_rows(2, h), :KEYS], s.prob_s[b, h]).astype(BF)

        score(0)
        score(1)
        for h in range(HEADS):
            if beside_it:
                beside_it.pop(0)()
            if h + 2 < HEADS:
                score(h + 2)
            spread_out(h)
            if h > 1:
                mix(h - 2)
        mix(HEADS - 2)
        mix(HEADS - 1)

    def run(steps):
        for step in steps:
            step()

    pair_loop(
        lambda: run(project(0, s.live_a, s.h1_a)),
        lambda b: attend(b, s.live_a, project(b + 1, s.live_b, s.h1_b)),
        lambda b: attend(b, s.live_b, project(b + 1, s.live_a, s.h1_a)),
        lambda: attend(BLOCKS - 1, s.live_a),
        None if solo else lambda i: at_step(i, {1: lambda: gr.stage(2), 3: lambda: gr.stage(3)}),
    )

    if not solo:
        gr.stage(4)
    unpack_r(plan, s.all_r, s)
    s.wup_t[...] = s.wup_n[...].T
    s.wproj_n[...] = s.wproj_t[:, :WIDTH].T
    s.wdown_n[...] = s.wdown_t[:, :FF].T

    def widen(b, h2, act, du, mid_ref):
        cols = block_cols(b)

        def enter():
            mid = s.x_s[:, cols].astype(F32) + nn(s.wproj_t[...], s.ctx_s[:, cols])
            mid_ref[...] = mid
            normal, _ = normal_parts(mid)
            h2[:WIDTH, :] = (normal * wide(s.gains[2]) + wide(s.gains[3])).astype(BF)

        def hidden(f):
            part = slice(f, f + FF_STEP)
            value, slope = gelu_both(nn(s.wup_t[part, :], h2[...]))
            act[part, :] = value.astype(BF)
            du[part, :] = (nn(s.wdown_n[part, :], s.c_s[:, cols]) * slope).astype(BF)

        return [enter] + [partial(hidden, f) for f in range(0, FF, FF_STEP)]

    def narrow(b, h2, act, du, mid_ref):
        cols = block_cols(b)

        def leave():
            s.c_s[:, cols] = (mid_ref[...] + nn(s.wdown_t[...], act[...])).astype(BF)

        def weights_up():
            s.dup_s[...] += nt(h2[...], du[...])

        def weights_down():
            s.ddown_s[...] += nt(s.c_s[:, cols], act[...])

        def back():
            grad = nn(s.wup_n[:WIDTH, :], du[...])
            normal, inverse = normal_parts(mid_ref[...])
            s.acc_s[0] += grad * normal
            s.acc_s[1] += grad
            dy1 = s.c_s[:, cols].astype(F32) + norm_back(grad, normal, inverse, wide(s.gains[2]))
            da = dy1.astype(BF)
            s.da_s[:, cols] = da
            s.do_s[:, cols] = nn(s.wproj_n[...], da).astype(BF)

        return [back, weights_down, weights_up, leave]

    def weave(one, two):
        one, two = list(one), list(two)
        while one or two:
            if one:
                one.pop(0)()
            if two:
                two.pop(0)()

    set_a = (s.h2_a, s.act_a, s.du_a, s.mid_a)
    set_b = (s.h2_b, s.act_b, s.du_b, s.mid_b)
    pair_loop(
        lambda: run(widen(0, *set_a)),
        lambda b: weave(widen(b + 1, *set_b), narrow(b, *set_a)),
        lambda b: weave(widen(b + 1, *set_a), narrow(b, *set_b)),
        lambda: run(narrow(BLOCKS - 1, *set_a)),
    )
    write_out = pltpu.make_async_copy(s.c_s, out_ref, s.out_sem.at[0])
    write_out.start()
    s.dproj_s[...] = nt(s.da_s[...], s.ctx_s[...])
    if not solo:
        gr.close()
    pack_r(plan, s.part_r, s)
    if not solo:
        rr.start()

    def padded(rows):
        return jnp.concatenate([rows, jnp.zeros((HEAD_DIM, LANES - KEYS), F32)], axis=1).astype(BF)

    def backward(b):
        cols = block_cols(b)
        key_cols = pl.ds(pl.multiple_of(b * LANES, LANES), KEYS)

        def slope(h):
            values = s.qkv_s[pair_rows(2, h), key_cols].T
            s.work_s[h % 3] = nn(values, beside(s.do_s[head_rows(0, h), cols], h))

        def score_grad(h):
            for tile in (slice(0, 128), slice(128, 256)):
                prob = s.prob_s[b, h, :, tile].astype(F32)
                term = prob * s.work_s[h % 3, :, tile]
                weighted = jnp.sum(term, axis=0, keepdims=True)
                s.ds_s[h % 3, :, tile] = (term - prob * weighted).astype(BF)

        def back(h):
            ds = s.ds_s[h % 3]
            s.da3_s[head_rows(0, h), cols] = (nn(s.qkv_s[head_rows(1, h), key_cols], ds) * scale).astype(BF)
            s.da3_s[head_rows(1, h), cols] = padded(nt(s.qkv_s[head_rows(0, h), cols], ds))
            s.da3_s[head_rows(2, h), cols] = padded(nt(s.do_s[head_rows(0, h), cols], s.prob_s[b, h]))

        slope(0)
        slope(1)
        for h in range(HEADS):
            if h + 2 < HEADS:
                slope(h + 2)
            score_grad(h)
            if h > 1:
                back(h - 2)
        back(HEADS - 2)
        back(HEADS - 1)

    def backward_loop(b, _):
        if not solo:
            at_step(b, {3: lambda: rr.stage(0), 7: lambda: rr.stage(1)})
        backward(b)
        return 0

    lax.fori_loop(0, BLOCKS, backward_loop, 0)

    product = nt(s.da3_s[...], s.xhat_s[...])
    sums = product[:, WIDTH : WIDTH + 1]
    weights = s.wqkv_t[:, :WIDTH].astype(F32)
    gain, shift = s.vec_s[0:1, :].astype(F32), s.vec_s[1:2, :].astype(F32)
    s.dvec_s[0:1, :] = jnp.sum(weights * product[:, :WIDTH], axis=0, keepdims=True)
    s.dvec_s[1:2, :] = jnp.sum(weights * sums, axis=0, keepdims=True)
    s.dqkv_s[:, :WIDTH] = product[:, :WIDTH] * gain + sums * shift
    s.dqkv_s[:, WIDTH:] = product[:, WIDTH:]
    rows = s.dqkv_s[:, 256:].T
    s.dvec_s[2:3, :] = rows[WIDTH - 256 : WIDTH - 255, :WIDTH]
    s.dvec_s[3:4, :] = rows[WIDTH - 256 : WIDTH - 255, 2 * WIDTH :]
    s.dvec_s[4:5, :] = s.dproj_s[:, 256:].T[WIDTH - 256 : WIDTH - 255, :]
    for k in range(2):
        both = s.acc_s[k]
        s.dvec_s[5 + k : 6 + k, :] = jnp.sum((both[:, :128] + both[:, 128:]).T, axis=0, keepdims=True)
    s.dvec_s[7:8, :] = s.ddown_s[:, FF:].T[0:1, :]
    if not solo:
        gq.close()
    pack_q(plan, s.part_q, s)
    if not solo:
        rq.start()
        rr.stage(2)
    s.wqkv_n[...] = s.wqkv_t[:, :WIDTH].T

    def finish(b, _):
        if not solo:
            at_step(b, {2: lambda: rq.stage(0), 5: lambda: rq.stage(1), 8: lambda: rq.stage(2)})
        cols = block_cols(b)
        grad = nn(s.wqkv_n[...], s.da3_s[:, cols])
        normal, inverse = normal_parts(s.x_s[:, cols].astype(F32))
        gtok = s.da_s[:, cols].astype(F32) + norm_back(grad, normal, inverse, wide(s.gains[0]))
        s.x_s[:, cols] = gtok.astype(BF)
        return 0

    lax.fori_loop(0, BLOCKS, finish, 0)
    write_gtok = pltpu.make_async_copy(s.x_s, gtok_ref, s.out_sem.at[1])
    write_gtok.start()
    if not solo:
        sum_r[...] = rr.stage(3)
        sum_q[...] = rq.stage(3)
        rr.close()
        rq.close()
    write_out.wait()
    write_gtok.wait()


def main_call(plan, order, tokens, cotan, weights, vectors, packs=None):
    vmem = pl.BlockSpec(memory_space=pltpu.VMEM)
    solo = packs is not None
    scratch = scratch_list(plan)
    if not solo:
        scratch.update(link_list(plan))
    tile = (16, 128)
    if solo:
        sums = [jax.ShapeDtypeStruct((plan.slots, n) + tile, BF) for n in (plan.q_tiles, plan.r_tiles)]
        params = pltpu.CompilerParams(vmem_limit_bytes=VMEM_LIMIT)
    else:
        sums = [jax.ShapeDtypeStruct((n,) + tile, F32) for n in (plan.q_tiles, plan.r_tiles)]
        params = pltpu.CompilerParams(collective_id=0, has_side_effects=True, vmem_limit_bytes=VMEM_LIMIT)
    args = (tokens, cotan) + tuple(weights) + tuple(vectors) + tuple(packs or ())
    return pl.pallas_call(
        partial(main_kernel, plan, solo, tuple(scratch)),
        out_shape=(
            jax.ShapeDtypeStruct((WIDTH, COLS), BF),
            jax.ShapeDtypeStruct((WIDTH, COLS), BF),
            *sums,
        ),
        in_specs=[pl.BlockSpec(memory_space=pltpu.SMEM)] + [vmem] * len(args),
        out_specs=(pl.BlockSpec(memory_space=pl.ANY),) * 2 + (vmem,) * 2,
        scratch_shapes=list(scratch.values()),
        compiler_params=params,
        name="block_main",
    )(order, *args)


def place_kernel(plan, order_ref, out_c_ref, gtok_c_ref, sum_q, sum_r, *refs):
    out_ref, gtok_ref, dqkv_ref, dproj_ref, dup_ref, ddown_ref = refs[:6]
    vectors = refs[6:15]
    big_start, small_start, out_s, gtok_s = refs[15:]
    slot_starts(order_ref, big_start, small_start)
    out_s[...] = jnp.zeros_like(out_s)
    gtok_s[...] = jnp.zeros_like(gtok_s)

    def place(block, paired):
        cols = block_cols(block)
        rows = jnp.concatenate([out_c_ref[:, cols], gtok_c_ref[:, cols]], axis=0)
        for start, length, lane0, size in pieces_of(block, big_start, small_start, paired):
            columns, offset = window(start, size)
            moved = nn(rows, chooser(offset, length, lane0, size, False))
            out_s[:, columns] += moved[:WIDTH].astype(BF)
            gtok_s[:, columns] += moved[WIDTH:]

    def place_paired(b, _):
        place(b, True)
        return 0

    def place_small(b, _):
        place(b, False)
        return 0

    lax.fori_loop(0, BIGS, place_paired, 0)
    lax.fori_loop(BIGS, BLOCKS, place_small, 0)
    out_ref[...] = out_s[:, :ROWS]
    gtok_ref[...] = gtok_s[:, :ROWS]
    r, v = plan.rows, plan.vec
    get(sum_q, 0, plan.q_wide, 0, 0, plan.qkv, r, dqkv_ref, 0, 0)
    get(sum_r, 0, 1, 0, 0, r, plan.up, dup_ref, 0, 0)
    get(sum_r, plan.u_tiles, plan.d_wide, 0, 0, v, 4 * r, ddown_ref, 0, 0)
    get(sum_r, plan.u_tiles, plan.d_wide, 0, 4 * r, v, r, dproj_ref, 0, 0)
    for k in range(VECTORS):
        get(sum_q, 0, plan.q_wide, plan.qkv + k, 0, 1, vectors[k].shape[1], vectors[k], 0, 0)


def place_call(plan, order, out_c, gtok_c, sum_q, sum_r):
    vmem = pl.BlockSpec(memory_space=pltpu.VMEM)
    f32 = lambda *shape: jax.ShapeDtypeStruct(shape, F32)
    r, v = plan.rows, plan.vec
    return pl.pallas_call(
        partial(place_kernel, plan),
        out_shape=(
            jax.ShapeDtypeStruct((WIDTH, ROWS), BF),
            f32(WIDTH, ROWS),
            f32(plan.qkv, r),
            f32(v, r),
            f32(r, plan.up),
            f32(v, 4 * r),
        )
        + (f32(1, v),) * 8
        + (f32(1, plan.up),),
        in_specs=[pl.BlockSpec(memory_space=pltpu.SMEM)] + [vmem] * 4,
        out_specs=(vmem,) * 15,
        scratch_shapes=[
            pltpu.SMEM((BIGS,), jnp.int32),
            pltpu.SMEM((SMALLS + 2,), jnp.int32),
            pltpu.VMEM((WIDTH, ROWS_PAD), BF),
            pltpu.VMEM((WIDTH, ROWS_PAD), F32),
        ],
        compiler_params=pltpu.CompilerParams(vmem_limit_bytes=VMEM_LIMIT),
        name="block_place",
    )(order, out_c, gtok_c, sum_q, sum_r)


def local(plan, *args):
    (
        tokens,
        cotangent,
        crop_order,
        ln1_gain,
        ln1_bias,
        w_qkv,
        b_query,
        b_value,
        w_proj,
        b_proj,
        ln2_gain,
        ln2_bias,
        w_up,
        b_up,
        w_down,
        b_down,
    ) = args
    vectors = (ln1_gain, ln1_bias, b_query, b_value, b_proj, ln2_gain, ln2_bias, b_down, b_up)
    weights = (w_qkv.T, w_proj.T, w_up, w_down.T)
    out_c, gtok_c, sum_q, sum_r = main_call(plan, crop_order, tokens.T, cotangent.T, weights, vectors)
    out, gtok, dqkv, dproj, dup, ddown, *grads = place_call(plan, crop_order, out_c, gtok_c, sum_q, sum_r)
    g1, s1, bq, bv, bp, g2, s2, bd, bu = [one[0] for one in grads]
    return (out.T, gtok.T, g1, s1, dqkv.T, bq, bv, dproj.T, bp, g2, s2, dup, bu, ddown.T, bd)


def solution(mesh):
    plan = Plan(mesh.shape["dp"], mesh.shape["fsdp"])
    rows = P(("dp", "fsdp"), None)
    vec = P("dp")
    mat = P("fsdp", "dp")
    return jax.shard_map(
        partial(local, plan),
        mesh=mesh,
        in_specs=(rows, rows, rows, vec, vec, mat, vec, vec, mat, vec, vec, vec, mat, vec, mat, vec),
        out_specs=(rows, rows, vec, vec, mat, vec, vec, mat, vec, vec, vec, mat, vec, mat, vec),
        check_vma=False,
    )
```

```python
from functools import partial

import jax
import jax.numpy as jnp
from jax import lax
from jax.experimental import pallas as pl
from jax.experimental.pallas import tpu as pltpu
from jax.sharding import PartitionSpec as P

HEADS = 6
HEAD_DIM = 48
BIG_LEN = 197
SMALL_LEN = 37
BIGS = 8
SMALLS = 24
WIDTH = 288
EXT = 304
FF = 1152
FF_EXT = 1168
ROWS = 2464
ROWS_PAD = 2560
LANES = 256
BLOCKS = 11
COLS = BLOCKS * LANES
KEYS = 240
BIG_WIN = 384
SMALL_WIN = 256
FF_STEP = 192
VECTORS = 9
EPS = 1e-06
BF = jnp.bfloat16
F32 = jnp.float32
MESH = pl.DeviceIdType.MESH
VMEM_LIMIT = 64 * 1024 * 1024 - 65536


def nn(a, b):
    return jnp.dot(a, b, preferred_element_type=F32)


def nt(a, b):
    return lax.dot_general(a, b, (((1,), (1,)), ((), ())), preferred_element_type=F32)


def tn(a, b):
    return lax.dot_general(a, b, (((0,), (0,)), ((), ())), preferred_element_type=F32)


def iota(shape, dim):
    return lax.broadcasted_iota(jnp.int32, shape, dim)


def wide(col):
    return jnp.concatenate([col, col], axis=1)


def block_cols(b):
    return pl.ds(pl.multiple_of(b * LANES, LANES), LANES)


def up_to(size, unit):
    return -(-size // unit) * unit


class Plan:
    def __init__(self, n_dp, n_fs):
        self.n_dp, self.n_fs = n_dp, n_fs
        self.n_core = 2
        self.n_z = 4
        self.n_x = n_dp // (self.n_core * self.n_z)
        self.slots = n_dp * n_fs
        self.rows = WIDTH // n_fs
        self.qkv, self.vec, self.up = 3 * WIDTH // n_dp, WIDTH // n_dp, FF // n_dp
        self.q_rows = up_to(self.qkv + VECTORS, 16) // 16
        self.q_left = max(self.rows - 128, 0)
        self.q_beside = 128 // self.q_left if self.q_left else 1
        left = -(-(up_to(self.qkv, 16) // 16) // self.q_beside) if self.q_left else 0
        self.q_tiles = self.q_rows + left
        self.u_tiles = up_to(self.rows, 16) // 16
        self.d_wide = up_to(5 * self.rows, 128) // 128
        self.d_left = max(self.vec - 16, 0)
        self.d_under = 16 // self.d_left if self.d_left else 1
        left = -(-self.d_wide // self.d_under) if self.d_left else 0
        self.r_tiles = self.u_tiles + self.d_wide + left


    def q_cuts(self):
        for tile in range(-(-self.qkv // 16)):
            rows = min(16, self.qkv - 16 * tile)
            yield tile, 0, 0, rows, min(self.rows, 128), 16 * tile, 0
            if self.q_left:
                across, beside = divmod(tile, self.q_beside)
                yield self.q_rows + across, 0, beside * self.q_left, rows, self.q_left, 16 * tile, 128

    def vector_cuts(self, first, count, cols):
        done = 0
        while done < count:
            tile, row = divmod(self.qkv + first + done, 16)
            rows = min(16 - row, count - done)
            yield tile, row, 0, rows, cols, done, 0
            done += rows

    def u_cuts(self):
        for tile in range(self.u_tiles):
            yield tile, 0, 0, min(16, self.rows - 16 * tile), self.up, 16 * tile, 0

    def d_cuts(self, col, cols):
        done = 0
        while done < cols:
            across, lane = divmod(col + done, 128)
            width = min(128 - lane, cols - done)
            yield self.u_tiles + across, 0, lane, min(self.vec, 16), width, 0, done
            if self.d_left:
                tile, under = divmod(across, self.d_under)
                tile += self.u_tiles + self.d_wide
                yield tile, under * self.d_left, lane, self.d_left, width, 16, done
            done += width

    def down_cuts(self):
        return self.d_cuts(0, 4 * self.rows)

    def proj_cuts(self):
        return self.d_cuts(4 * self.rows, self.rows)

    def dp(self, z, x, core):
        return (z * self.n_x + x) * self.n_core + core

    def slot(self, z, x, core, fs):
        return self.dp(z, x, core) * self.n_fs + fs

    def here(self):
        dp, fs = lax.axis_index("dp"), lax.axis_index("fsdp")
        core = lax.rem(dp, self.n_core)
        rest = lax.div(dp, self.n_core)
        return lax.div(rest, self.n_x), lax.rem(rest, self.n_x), core, fs


def put(ref, cuts, value):
    for tile, row, lane, rows, cols, i, j in cuts:
        ref[tile, row : row + rows, lane : lane + cols] = value[i : i + rows, j : j + cols]


def get(ref, cuts, target, top, left):
    for tile, row, lane, rows, cols, i, j in cuts:
        target[top + i : top + i + rows, left + j : left + j + cols] = ref[
            tile, row : row + rows, lane : lane + cols
        ]


class Links:
    def __init__(self, plan):
        self.plan = plan
        self.z, self.x, self.core, self.fs = plan.here()
        self.zs = [lax.rem(self.z + d, plan.n_z) for d in range(plan.n_z)]
        self.xs = [lax.rem(self.x + d, plan.n_x) for d in range(plan.n_x)]
        self.fss = [lax.rem(self.fs + d, plan.n_fs) for d in range(plan.n_fs)]
        self.peer = lax.rem(self.core + 1, 2)
        self.to_core = (plan.dp(self.z, self.x, self.peer), self.fs)
        self.to_fs = [(plan.dp(self.z, self.x, self.core), fs) for fs in self.fss]
        self.to_x = [(plan.dp(self.z, x, self.core), self.fs) for x in self.xs]
        self.to_z = [(plan.dp(z, self.x, self.core), self.fs) for z in self.zs]

    def slot(self, dz, dx, dc, df):
        return self.plan.slot(self.zs[dz], self.xs[dx], (self.core, self.peer)[dc], self.fss[df])

    def meet(self):
        barrier = pltpu.get_barrier_semaphore()
        places = [self.to_core] + self.to_fs[1:] + self.to_x[1:] + self.to_z[1:]
        for place in places:
            pl.semaphore_signal(barrier, inc=1, device_id=place, device_id_type=MESH)
        pl.semaphore_wait(barrier, len(places))


def remote(src, dst, send_sem, recv_sem, place):
    return pltpu.make_async_remote_copy(
        src_ref=src, dst_ref=dst, send_sem=send_sem, recv_sem=recv_sem, device_id=place, device_id_type=MESH
    )


class Axes:
    def __init__(self, links, x_first):
        plan = links.plan
        x, f = (plan.n_x, links.to_x), (plan.n_fs, links.to_fs)
        (self.n1, self.to1), (self.n2, self.to2) = (x, f) if x_first else (f, x)
        self.slot = lambda dz, d1, d2, dc: links.slot(dz, *((d1, dc, d2) if x_first else (d2, dc, d1)))


class Gather:
    def __init__(self, links, whole, tiles, x_first, send_sem, recv_sem):
        self.whole, self.tiles, self.send_sem, self.recv_sem = whole, tiles, send_sem, recv_sem
        axes = Axes(links, x_first)
        nz = links.plan.n_z
        to_core = [links.to_core]
        to_2 = axes.to2[1:] + to_core
        to_12 = axes.to1[1:] + to_2
        all_z, all_1, all_2 = range(nz), range(axes.n1), range(axes.n2)
        stages = [
            [((0, 0, 0, 0), links.to_z[1:] + to_12)],
            [((dz, 0, 0, 0), to_12) for dz in all_z[1:]],
            [((dz, d1, 0, 0), to_2) for d1 in all_1[1:] for dz in all_z],
            [((dz, d1, d2, 0), to_core) for d2 in all_2[1:] for d1 in all_1 for dz in all_z],
            [((dz, d1, d2, 1), []) for d2 in all_2 for d1 in all_1 for dz in all_z],
        ]
        count = 0
        self.work = []
        for stage in stages:
            steps = []
            for steps_to, places in stage:
                steps.append((axes.slot(*steps_to), [(count + n, place) for n, place in enumerate(places)]))
                count += len(places)
            self.work.append(steps)
        self.any_place = links.to_core

    def copy(self, slot, index, place):
        one = self.whole.at[slot, self.tiles]
        return remote(one, one, self.send_sem.at[index], self.recv_sem.at[slot], place)

    def stage(self, number):
        for slot, sends in self.work[number]:
            if number:
                self.copy(slot, 0, self.any_place).wait_recv()
            for index, place in sends:
                self.copy(slot, index, place).start()

    def close(self):
        for steps in self.work:
            for slot, sends in steps:
                for index, place in sends:
                    self.copy(slot, index, place).wait_send()


class Reduce:
    def __init__(self, links, part, got, tiles, x_first, send_sem, recv_sem):
        self.part, self.got, self.tiles, self.send_sem, self.recv_sem = part, got, tiles, send_sem, recv_sem
        axes = Axes(links, x_first)
        nz, n1, n2 = links.plan.n_z, axes.n1, axes.n2
        last = lambda n: list(range(1, n)) + [0]
        order = [(d1, d2, dz) for d1 in last(n1) for d2 in last(n2) for dz in last(nz)]
        at_1 = n1 * n2 * nz
        at_2 = at_1 + (n1 - 1) * n2 * nz
        at_z = at_2 + (n2 - 1) * nz
        spot_c = lambda d1, d2, dz: (d1 * n2 + d2) * nz + dz
        spot_1 = lambda d1, d2, dz: at_1 + ((d1 - 1) * n2 + d2) * nz + dz
        spot_2 = lambda d2, dz: at_2 + (d2 - 1) * nz + dz
        spot_z = lambda dz: at_z + dz - 1
        self.first = [(axes.slot(dz, d1, d2, 1), spot_c(d1, d2, dz), links.to_core) for d1, d2, dz in order]
        self.stages = [[], [], [], []]
        for d1, d2, dz in order:
            slot = axes.slot(dz, d1, d2, 0)
            takes = [spot_c(d1, d2, dz)]
            if d1:
                self.stages[0].append((slot, takes, spot_1(n1 - d1, d2, dz), axes.to1[d1]))
                continue
            takes += [spot_1(d, d2, dz) for d in range(1, n1)]
            if d2:
                self.stages[1].append((slot, takes, spot_2(n2 - d2, dz), axes.to2[d2]))
                continue
            takes += [spot_2(d, dz) for d in range(1, n2)]
            if dz:
                self.stages[2].append((slot, takes, spot_z(nz - dz), links.to_z[dz]))
                continue
            takes += [spot_z(d) for d in range(1, nz)]
            self.stages[3].append((slot, takes, None, None))
        self.any_place = links.to_core

    def copy(self, slot, spot, place):
        return remote(
            self.part.at[slot, self.tiles],
            self.got.at[spot, self.tiles],
            self.send_sem.at[spot],
            self.recv_sem.at[spot],
            place,
        )

    def start(self):
        for slot, spot, place in self.first:
            self.copy(slot, spot, place).start()

    def stage(self, number):
        for slot, takes, spot, place in self.stages[number]:
            total = self.part[slot, self.tiles].astype(F32)
            for index in takes:
                self.copy(slot, index, self.any_place).wait_recv()
                total = total + self.got[index, self.tiles].astype(F32)
            if place is None:
                return total
            self.part[slot, self.tiles] = total.astype(BF)
            self.copy(slot, spot, place).start()

    def close(self):
        for slot, spot, place in self.first:
            self.copy(slot, spot, place).wait_send()
        for steps in self.stages[:3]:
            for slot, _, spot, place in steps:
                self.copy(slot, spot, place).wait_send()


def normal_parts(rows):
    mean = jnp.sum(rows, axis=0, keepdims=True) * (1.0 / WIDTH)
    centered = rows - mean
    variance = jnp.sum(centered * centered, axis=0, keepdims=True) * (1.0 / WIDTH)
    inverse = lax.rsqrt(variance + EPS)
    return centered * inverse, inverse


def norm_back(grad, normal, inverse, gain):
    scaled = grad * gain
    first = jnp.sum(scaled, axis=0, keepdims=True) * (1.0 / WIDTH)
    second = jnp.sum(scaled * normal, axis=0, keepdims=True) * (1.0 / WIDTH)
    return inverse * (scaled - first - normal * second)


def gelu_both(u):
    z = jnp.abs(u)
    d = 1.0 + z * (0.3275911 * 0.7071067811865476)
    t = pl.reciprocal(d, approx=True)
    t = t * (2.0 - d * t)
    e = jnp.exp(u * u * -0.5)
    poly = 0.5 * 1.061405429
    poly = poly * t + 0.5 * -1.453152027
    poly = poly * t + 0.5 * 1.421413741
    poly = poly * t + 0.5 * -0.284496736
    poly = poly * t + 0.5 * 0.254829592
    tail = poly * t * e
    phi = jnp.where(u >= 0.0, 1.0 - tail, tail)
    return u * phi, phi + u * e * 0.3989422804014327


def slot_starts(order_ref, big_start, small_start):
    far = jnp.int32(1 << 20)

    def one(j, carry):
        row, big_count, starts = carry
        big = jnp.where(order_ref[0, j] < BIGS, 1, 0)
        rank = jnp.where(big == 1, big_count, BIGS + j - big_count)
        starts = tuple(jnp.where(rank == k, row, start) for k, start in enumerate(starts))
        return row + SMALL_LEN + (BIG_LEN - SMALL_LEN) * big, big_count + big, starts

    _, _, starts = lax.fori_loop(
        0, BIGS + SMALLS, one, (jnp.int32(0), jnp.int32(0), (far,) * (BIGS + SMALLS + 2))
    )
    for k in range(BIGS):
        big_start[k] = starts[k]
    for k in range(SMALLS + 2):
        small_start[k] = starts[BIGS + k]


def window(start, size):
    first = jnp.minimum(start - lax.rem(start, jnp.int32(128)), ROWS_PAD - size)
    return pl.ds(pl.multiple_of(first, 128), size), start - first


def pieces_of(block, big_start, small_start, paired):
    if paired:
        return [
            (big_start[block], BIG_LEN, 0, BIG_WIN),
            (small_start[block], SMALL_LEN, BIG_LEN, SMALL_WIN),
        ]
    base = BIGS + 6 * (block - BIGS)
    return [(small_start[base + k], SMALL_LEN, SMALL_LEN * k, SMALL_WIN) for k in range(6)]


def chooser(offset, length, lane0, size, inward):
    shape = (size, LANES) if inward else (LANES, size)
    lane = iota(shape, 1 if inward else 0)
    column = iota(shape, 0 if inward else 1)
    hit = (column - lane == offset - lane0) & (lane >= lane0) & (lane < lane0 + length)
    return jnp.where(hit, 1.0, 0.0).astype(BF)


def crop_mask(paired):
    key = iota((KEYS, LANES), 0)
    query = iota((KEYS, LANES), 1)
    if paired:
        label_key = jnp.where(key < BIG_LEN, 0, jnp.where(key < BIG_LEN + SMALL_LEN, 1, 2))
        label_query = jnp.where(query < BIG_LEN, 0, jnp.where(query < BIG_LEN + SMALL_LEN, 1, 2))
    else:
        label_key = jnp.zeros_like(key)
        label_query = jnp.zeros_like(key)
        for k in range(1, 7):
            label_key = label_key + jnp.where(key >= SMALL_LEN * k, 1, 0)
            label_query = label_query + jnp.where(query >= SMALL_LEN * k, 1, 0)
    return jnp.where(label_key == label_query, 0.0, -1e30)


def pack_own(plan, q, r, qkv_ref, proj_ref, up_ref, down_ref, vector_refs):
    q[...] = jnp.zeros_like(q)
    r[...] = jnp.zeros_like(r)
    put(q, plan.q_cuts(), qkv_ref[...])
    for k, ref in enumerate(vector_refs):
        put(q, plan.vector_cuts(k, 1, ref.shape[0]), ref[...].reshape(1, ref.shape[0]))
    put(r, plan.u_cuts(), up_ref[...])
    put(r, plan.down_cuts(), down_ref[...])
    put(r, plan.proj_cuts(), proj_ref[...])


def unpack_q(plan, all_q, s):
    r, v, qkv, up = plan.rows, plan.vec, plan.qkv, plan.up
    s.vec_s[...] = jnp.zeros_like(s.vec_s)
    s.wup_n[WIDTH:, :] = jnp.zeros((EXT - WIDTH, FF), BF)
    for i in range(plan.n_dp):
        for j in range(plan.n_fs):
            get(all_q.at[i * plan.n_fs + j], plan.q_cuts(), s.wqkv_t, i * qkv, j * r)
        one = all_q.at[i * plan.n_fs]
        get(one, plan.vector_cuts(0, VECTORS - 1, v), s.vec_s, 0, i * v)
        get(one, plan.vector_cuts(VECTORS - 1, 1, up), s.wup_n, WIDTH, i * up)
    columns = s.vec_s[...].T
    lane = iota((WIDTH, 16), 1)
    none = jnp.zeros((WIDTH, 16), BF)
    s.wqkv_t[:WIDTH, WIDTH:] = jnp.where(lane == 2, columns, none)
    s.wqkv_t[WIDTH : 2 * WIDTH, WIDTH:] = none
    s.wqkv_t[2 * WIDTH :, WIDTH:] = jnp.where(lane == 3, columns, none)
    s.wproj_t[:, WIDTH:] = jnp.where(lane == 4, columns, none)
    s.wdown_t[:, FF:] = jnp.where(lane == 7, columns, none)
    for n, k in enumerate((0, 1, 5, 6)):
        pick = jnp.where(iota((16, 128), 0) == k, 1.0, 0.0).astype(BF)
        s.gains[n] = tn(s.vec_s[...], pick)


def unpack_r(plan, all_r, s):
    r, v, up = plan.rows, plan.vec, plan.up
    for i in range(plan.n_dp):
        for j in range(plan.n_fs):
            one = all_r.at[i * plan.n_fs + j]
            get(one, plan.u_cuts(), s.wup_n, j * r, i * up)
            get(one, plan.down_cuts(), s.wdown_t, i * v, j * 4 * r)
            get(one, plan.proj_cuts(), s.wproj_t, i * v, j * r)


def pack_r(plan, part, s):
    r, v, up = plan.rows, plan.vec, plan.up
    for i in range(plan.n_dp):
        for j in range(plan.n_fs):
            one = part.at[i * plan.n_fs + j]
            put(one, plan.u_cuts(), s.dup_s[j * r : (j + 1) * r, i * up : (i + 1) * up].astype(BF))
            down = s.ddown_s[i * v : (i + 1) * v, j * 4 * r : (j + 1) * 4 * r].astype(BF)
            put(one, plan.down_cuts(), down)
            put(one, plan.proj_cuts(), s.dproj_s[i * v : (i + 1) * v, j * r : (j + 1) * r].astype(BF))


def pack_q(plan, part, s):
    r, v, qkv, up = plan.rows, plan.vec, plan.qkv, plan.up
    for i in range(plan.n_dp):
        vectors = s.dvec_s[:, i * v : (i + 1) * v].astype(BF)
        bias_up = s.dup_s[WIDTH : WIDTH + 1, i * up : (i + 1) * up].astype(BF)
        for j in range(plan.n_fs):
            one = part.at[i * plan.n_fs + j]
            put(one, plan.q_cuts(), s.dqkv_s[i * qkv : (i + 1) * qkv, j * r : (j + 1) * r].astype(BF))
            put(one, plan.vector_cuts(0, VECTORS - 1, v), vectors)
            put(one, plan.vector_cuts(VECTORS - 1, 1, up), bias_up)


class Scratch:
    pass


def scratch_list(plan):
    vmem, smem = pltpu.VMEM, pltpu.SMEM
    tile = (16, 128)
    return dict(
        big_start=smem((BIGS,), jnp.int32),
        small_start=smem((SMALLS + 2,), jnp.int32),
        target_s=vmem((BLOCKS, 1, LANES), jnp.int32),
        wqkv_t=vmem((3 * WIDTH, EXT), BF),
        wproj_t=vmem((WIDTH, EXT), BF),
        wup_t=vmem((FF, EXT), BF),
        wdown_t=vmem((WIDTH, FF_EXT), BF),
        wqkv_n=vmem((WIDTH, 3 * WIDTH), BF),
        wproj_n=vmem((WIDTH, WIDTH), BF),
        wup_n=vmem((EXT, FF), BF),
        wdown_n=vmem((FF, WIDTH), BF),
        vec_s=vmem((16, WIDTH), BF),
        gains=vmem((4, WIDTH, 128), F32),
        mask_s=vmem((2, KEYS, LANES), F32),
        x_s=vmem((WIDTH, COLS), BF),
        c_s=vmem((WIDTH, COLS), BF),
        xhat_s=vmem((EXT, COLS), BF),
        qkv_s=vmem((3 * WIDTH, COLS), BF),
        prob_s=vmem((BLOCKS, HEADS, KEYS, LANES), BF),
        ctx_s=vmem((EXT, COLS), BF),
        h2_a=vmem((EXT, LANES), BF),
        h2_b=vmem((EXT, LANES), BF),
        act_a=vmem((FF_EXT, LANES), BF),
        act_b=vmem((FF_EXT, LANES), BF),
        du_a=vmem((FF, LANES), BF),
        du_b=vmem((FF, LANES), BF),
        mid_a=vmem((WIDTH, LANES), F32),
        mid_b=vmem((WIDTH, LANES), F32),
        da_s=vmem((WIDTH, COLS), BF),
        do_s=vmem((WIDTH, COLS), BF),
        da3_s=vmem((3 * WIDTH, COLS), BF),
        dqkv_s=vmem((3 * WIDTH, EXT), F32),
        dproj_s=vmem((WIDTH, EXT), F32),
        dup_s=vmem((EXT, FF), F32),
        ddown_s=vmem((WIDTH, FF_EXT), F32),
        dvec_s=vmem((8, WIDTH), F32),
        acc_s=vmem((2, WIDTH, LANES), F32),
        grad_s=vmem((WIDTH, LANES), F32),
        work_s=vmem((4, KEYS, LANES), F32),
        ds_s=vmem((3, KEYS, LANES), BF),
        out_sem=pltpu.SemaphoreType.DMA((ROWS_PAD // LANES,)),
    )


def link_list(plan):
    vmem, dma = pltpu.VMEM, pltpu.SemaphoreType.DMA
    tile = (16, 128)
    hops = plan.slots - 1
    return dict(
        all_q=vmem((plan.slots, plan.q_tiles) + tile, BF),
        all_r=vmem((plan.slots, plan.r_tiles) + tile, BF),
        got_q=vmem((hops, plan.q_tiles) + tile, BF),
        got_r=vmem((hops, plan.r_tiles) + tile, BF),
        gq_send=dma((hops,)),
        gq_recv=dma((plan.slots,)),
        gr_send=dma((hops,)),
        gr_recv=dma((plan.slots,)),
        gt_send=dma((hops,)),
        gt_recv=dma((plan.slots,)),
        rq_send=dma((hops,)),
        rq_recv=dma((hops,)),
        rr_send=dma((hops,)),
        rr_recv=dma((hops,)),
        rt_send=dma((hops,)),
        rt_recv=dma((hops,)),
    )


def pair_loop(first, even, odd, last, service=None):
    first()

    def one(i, _):
        if service is not None:
            service(i)
        even(2 * i)
        odd(2 * i + 1)
        return 0

    lax.fori_loop(0, (BLOCKS - 1) // 2, one, 0)
    last()


def row_range(b):
    if b < BIGS:
        big_high = BIG_LEN * (b + 1) + SMALL_LEN * SMALLS
        return SMALL_LEN * b, max(big_high, SMALL_LEN * (b + 1) + BIG_LEN * BIGS)
    k = BIGS + 6 * (b - BIGS)
    return SMALL_LEN * k, SMALL_LEN * min(k + 6, SMALLS) + BIG_LEN * BIGS


def block_runs(low, high):
    runs = []
    for b in range(BLOCKS):
        first, last = row_range(b)
        if first < high and last > low:
            if runs and runs[-1][1] == b:
                runs[-1][1] = b + 1
            else:
                runs.append([b, b + 1])
    return runs


def at_step(i, actions):
    for step, action in actions.items():
        pl.when(i == step)(action)


def main_kernel(plan, solo, names, order_ref, tokens_ref, cotan_ref, qkv_ref, proj_ref, up_ref, down_ref, *refs):
    vector_refs, refs = refs[:VECTORS], refs[VECTORS:]
    s = Scratch()
    if solo:
        s.all_q, s.all_r = refs[:2]
        refs = refs[2:]
    rows_ref, sum_q, sum_r = refs[:3]
    for name, ref in zip(names, refs[3:]):
        setattr(s, name, ref)
    if solo:
        s.part_q, s.part_r = sum_q, sum_r
    else:
        s.part_q, s.part_r = s.all_q, s.all_r
        links = Links(plan)
        whole, top = slice(0, plan.q_tiles), slice(0, plan.r_tiles // 2)
        rest = slice(plan.r_tiles // 2, plan.r_tiles)
        gq = Gather(links, s.all_q, whole, True, s.gq_send, s.gq_recv)
        gr = Gather(links, s.all_r, top, True, s.gr_send, s.gr_recv)
        gt = Gather(links, s.all_r, rest, False, s.gt_send, s.gt_recv)
        rq = Reduce(links, s.part_q, s.got_q, whole, False, s.rq_send, s.rq_recv)
        rr = Reduce(links, s.part_r, s.got_r, top, True, s.rr_send, s.rr_recv)
        rt = Reduce(links, s.part_r, s.got_r, rest, False, s.rt_send, s.rt_recv)

        def gather_r(number):
            gr.stage(number)
            gt.stage(number)

        def reduce_r(number):
            rr.stage(number)
            rt.stage(number)

        mine = links.slot(0, 0, 0, 0)
        pack_own(plan, s.all_q.at[mine], s.all_r.at[mine], qkv_ref, proj_ref, up_ref, down_ref, vector_refs)
        links.meet()
        gq.stage(0)
        gather_r(0)

    s.da3_s[: 2 * WIDTH, ROWS_PAD - 128 : ROWS_PAD] = jnp.zeros((2 * WIDTH, 128), BF)
    s.da3_s[:WIDTH, :ROWS] = tokens_ref[...]
    s.da3_s[WIDTH : 2 * WIDTH, :ROWS] = cotan_ref[...]
    slot_starts(order_ref, s.big_start, s.small_start)
    lane = iota((1, LANES), 1)
    for b in range(BLOCKS):
        if b < BIGS:
            small = s.small_start[b] - BIG_LEN
            target = jnp.where(lane < BIG_LEN + SMALL_LEN, small + lane, -1)
            target = jnp.where(lane < BIG_LEN, s.big_start[b] + lane, target)
        else:
            target = jnp.full((1, LANES), -1, jnp.int32)
            for k in range(6):
                start = s.small_start[BIGS + 6 * (b - BIGS) + k] - SMALL_LEN * k
                target = jnp.where((lane >= SMALL_LEN * k) & (lane < SMALL_LEN * (k + 1)), start + lane, target)
        s.target_s[b] = target

    def load(b):
        low, high = row_range(b)
        low, high = low // 128 * 128, min(up_to(high, 128), ROWS_PAD)
        hit = iota((high - low, LANES), 0) + low == s.target_s[b]
        both = nn(s.da3_s[: 2 * WIDTH, low:high], jnp.where(hit, 1.0, 0.0).astype(BF))
        s.x_s[:, b * LANES : (b + 1) * LANES] = both[:WIDTH].astype(BF)
        s.c_s[:, b * LANES : (b + 1) * LANES] = both[WIDTH:].astype(BF)

    for b in range(0, 2):
        load(b)
    if not solo:
        gq.stage(1)
    for b in range(2, 4):
        load(b)
    if not solo:
        gq.stage(2)
    for b in range(4, 7):
        load(b)
    if not solo:
        gq.stage(3)
        gather_r(1)
    for b in range(7, 11):
        load(b)
    if not solo:
        gq.stage(4)
        gather_r(2)

    unpack_q(plan, s.all_q, s)
    s.mask_s[0] = crop_mask(True)
    s.mask_s[1] = crop_mask(False)
    ones = jnp.ones((16, COLS), BF)
    s.xhat_s[WIDTH:, :] = ones
    s.ctx_s[WIDTH:, :] = ones
    s.h1_a, s.h1_b, s.live_a, s.live_b = s.h2_a, s.h2_b, s.act_a, s.act_b
    for ref in (s.h2_a, s.h2_b):
        ref[WIDTH:, :] = ones[:, :LANES]
    for ref in (s.act_a, s.act_b):
        ref[FF:, :] = ones[:, :LANES]
    s.acc_s[...] = jnp.zeros_like(s.acc_s)
    s.dup_s[...] = jnp.zeros_like(s.dup_s)
    s.ddown_s[...] = jnp.zeros_like(s.ddown_s)
    scale = HEAD_DIM ** (-0.5)
    blank = jnp.zeros((HEAD_DIM, LANES), BF)

    def head_rows(part, h):
        return slice(part * WIDTH + HEAD_DIM * h, part * WIDTH + HEAD_DIM * (h + 1))

    def pair_rows(part, h):
        low = part * WIDTH + 2 * HEAD_DIM * (h // 2)
        return slice(low, low + 2 * HEAD_DIM)

    def beside(rows, h):
        return jnp.concatenate([rows, blank] if h % 2 == 0 else [blank, rows], axis=0)

    def project(b, live, h1):
        cols = block_cols(b)

        def norm():
            normal, _ = normal_parts(s.x_s[:, cols].astype(F32))
            s.xhat_s[:WIDTH, cols] = normal.astype(BF)
            h1[:WIDTH, :] = (normal * wide(s.gains[0]) + wide(s.gains[1])).astype(BF)

        def part(k):
            rows = slice(k * WIDTH, (k + 1) * WIDTH)
            mixed = nn(s.wqkv_t[rows, :], h1[...])
            mixed = ((mixed * scale) if k == 0 else mixed).astype(BF)
            live[rows, :] = mixed
            s.qkv_s[rows, cols] = mixed

        return [norm, lambda: part(0), lambda: part(1), lambda: part(2)]

    def attend(b, live, beside_it=()):
        cols = block_cols(b)
        kind = jnp.where(b < BIGS, 0, 1)
        beside_it = list(beside_it)

        def score(h):
            keys = live[pair_rows(1, h), :KEYS].T
            s.work_s[h % 3] = nn(keys, beside(live[head_rows(0, h), :], h))

        def spread_out(h):
            for tile in (slice(0, 128), slice(128, 256)):
                scores = s.work_s[h % 3, :, tile] + s.mask_s[kind, :, tile]
                top = jnp.max(scores, axis=0, keepdims=True)
                expo = jnp.exp(scores - top)
                total = jnp.sum(expo, axis=0, keepdims=True)
                s.prob_s[b, h, :, tile] = (expo * (1.0 / total)).astype(BF)

        def mix(h):
            s.ctx_s[head_rows(0, h), cols] = nn(live[head_rows(2, h), :KEYS], s.prob_s[b, h]).astype(BF)

        score(0)
        score(1)
        for h in range(HEADS):
            if beside_it:
                beside_it.pop(0)()
            if h + 2 < HEADS:
                score(h + 2)
            spread_out(h)
            if h > 1:
                mix(h - 2)
        mix(HEADS - 2)
        mix(HEADS - 1)

    def run(steps):
        for step in steps:
            step()

    pair_loop(
        lambda: run(project(0, s.live_a, s.h1_a)),
        lambda b: attend(b, s.live_a, project(b + 1, s.live_b, s.h1_b)),
        lambda b: attend(b, s.live_b, project(b + 1, s.live_a, s.h1_a)),
        lambda: attend(BLOCKS - 1, s.live_a),
        None if solo else lambda i: at_step(i, {2: lambda: gather_r(3)}),
    )

    if not solo:
        gather_r(4)
    unpack_r(plan, s.all_r, s)
    s.wup_t[...] = s.wup_n[...].T
    s.wproj_n[...] = s.wproj_t[:, :WIDTH].T
    s.wdown_n[...] = s.wdown_t[:, :FF].T

    def widen(b, h2, act, du, mid_ref):
        cols = block_cols(b)

        def enter():
            mid = s.x_s[:, cols].astype(F32) + nn(s.wproj_t[...], s.ctx_s[:, cols])
            mid_ref[...] = mid
            normal, _ = normal_parts(mid)
            h2[:WIDTH, :] = (normal * wide(s.gains[2]) + wide(s.gains[3])).astype(BF)

        def products(n):
            part = slice(n * FF_STEP, (n + 1) * FF_STEP)
            s.work_s[n % 2, :FF_STEP] = nn(s.wup_t[part, :], h2[...])
            s.work_s[2 + n % 2, :FF_STEP] = nn(s.wdown_n[part, :], s.c_s[:, cols])

        def curve(n):
            part = slice(n * FF_STEP, (n + 1) * FF_STEP)
            value, slope = gelu_both(s.work_s[n % 2, :FF_STEP])
            act[part, :] = value.astype(BF)
            du[part, :] = (s.work_s[2 + n % 2, :FF_STEP] * slope).astype(BF)

        steps = [enter, partial(products, 0)]
        for n in range(FF // FF_STEP):
            if (n + 1) * FF_STEP < FF:
                steps.append(partial(products, n + 1))
            steps.append(partial(curve, n))
        return steps

    def narrow(b, h2, act, du, mid_ref):
        cols = block_cols(b)

        def hidden_back(f):
            part = slice(f, f + 96)
            s.grad_s[part, :] = nn(s.wup_n[part, :], du[...])

        def norm_two():
            grad = s.grad_s[...]
            normal, inverse = normal_parts(mid_ref[...])
            s.acc_s[0] += grad * normal
            s.acc_s[1] += grad
            dy1 = s.c_s[:, cols].astype(F32) + norm_back(grad, normal, inverse, wide(s.gains[2]))
            s.da_s[:, cols] = dy1.astype(BF)

        def context_back():
            s.do_s[:, cols] = nn(s.wproj_n[...], s.da_s[:, cols]).astype(BF)

        def weights_down(f):
            part = slice(f, min(f + 256, FF_EXT))
            s.ddown_s[:, part] += nt(s.c_s[:, cols], act[part, :])

        def weights_up(f):
            part = slice(f, min(f + 256, FF))
            s.dup_s[:, part] += nt(h2[...], du[part, :])

        def leave(f):
            part = slice(f, f + 96)
            s.c_s[part, cols] = (mid_ref[part, :] + nn(s.wdown_t[part, :], act[...])).astype(BF)

        steps = [partial(hidden_back, f) for f in range(0, WIDTH, 96)]
        steps += [partial(weights_down, f) for f in range(0, FF_EXT, 256)]
        steps[5:5] = [norm_two]
        steps += [context_back]
        steps += [partial(weights_up, f) for f in range(0, FF, 256)]
        steps += [partial(leave, f) for f in range(0, WIDTH, 96)]
        return steps

    def weave(one, two):
        steps = [((n + 0.5) / len(one), step) for n, step in enumerate(one)]
        steps += [((n + 0.5) / len(two), step) for n, step in enumerate(two)]
        run(step for _, step in sorted(steps, key=lambda pair: pair[0]))

    set_a = (s.h2_a, s.act_a, s.du_a, s.mid_a)
    set_b = (s.h2_b, s.act_b, s.du_b, s.mid_b)
    pair_loop(
        lambda: run(widen(0, *set_a)),
        lambda b: weave(widen(b + 1, *set_b), narrow(b, *set_a)),
        lambda b: weave(widen(b + 1, *set_a), narrow(b, *set_b)),
        lambda: run(narrow(BLOCKS - 1, *set_a)),
    )
    s.dproj_s[...] = nt(s.da_s[...], s.ctx_s[...])
    if not solo:
        gr.close()
        gt.close()
    pack_r(plan, s.part_r, s)
    if not solo:
        rr.start()
        rt.start()

    def padded(rows):
        return jnp.concatenate([rows, jnp.zeros((HEAD_DIM, LANES - KEYS), F32)], axis=1).astype(BF)

    def backward(b):
        cols = block_cols(b)
        key_cols = pl.ds(pl.multiple_of(b * LANES, LANES), KEYS)

        def slope(h):
            values = s.qkv_s[pair_rows(2, h), key_cols].T
            s.work_s[h % 3] = nn(values, beside(s.do_s[head_rows(0, h), cols], h))

        def score_grad(h):
            for tile in (slice(0, 128), slice(128, 256)):
                prob = s.prob_s[b, h, :, tile].astype(F32)
                term = prob * s.work_s[h % 3, :, tile]
                weighted = jnp.sum(term, axis=0, keepdims=True)
                s.ds_s[h % 3, :, tile] = (term - prob * weighted).astype(BF)

        def back(h):
            ds = s.ds_s[h % 3]
            s.da3_s[head_rows(0, h), cols] = (nn(s.qkv_s[head_rows(1, h), key_cols], ds) * scale).astype(BF)
            s.da3_s[head_rows(1, h), cols] = padded(nt(s.qkv_s[head_rows(0, h), cols], ds))
            s.da3_s[head_rows(2, h), cols] = padded(nt(s.do_s[head_rows(0, h), cols], s.prob_s[b, h]))

        slope(0)
        slope(1)
        for h in range(HEADS):
            if h + 2 < HEADS:
                slope(h + 2)
            score_grad(h)
            if h > 1:
                back(h - 2)
        back(HEADS - 2)
        back(HEADS - 1)

    def backward_loop(b, _):
        if not solo:
            at_step(b, {3: lambda: reduce_r(0), 7: lambda: reduce_r(1)})
        backward(b)
        return 0

    lax.fori_loop(0, BLOCKS, backward_loop, 0)

    product = nt(s.da3_s[...], s.xhat_s[...])
    sums = product[:, WIDTH : WIDTH + 1]
    weights = s.wqkv_t[:, :WIDTH].astype(F32)
    gain, shift = s.vec_s[0:1, :].astype(F32), s.vec_s[1:2, :].astype(F32)
    s.dvec_s[0:1, :] = jnp.sum(weights * product[:, :WIDTH], axis=0, keepdims=True)
    s.dvec_s[1:2, :] = jnp.sum(weights * sums, axis=0, keepdims=True)
    s.dqkv_s[:, :WIDTH] = product[:, :WIDTH] * gain + sums * shift
    s.dqkv_s[:, WIDTH:] = product[:, WIDTH:]
    rows = s.dqkv_s[:, 256:].T
    s.dvec_s[2:3, :] = rows[WIDTH - 256 : WIDTH - 255, :WIDTH]
    s.dvec_s[3:4, :] = rows[WIDTH - 256 : WIDTH - 255, 2 * WIDTH :]
    s.dvec_s[4:5, :] = s.dproj_s[:, 256:].T[WIDTH - 256 : WIDTH - 255, :]
    for k in range(2):
        both = s.acc_s[k]
        s.dvec_s[5 + k : 6 + k, :] = jnp.sum((both[:, :128] + both[:, 128:]).T, axis=0, keepdims=True)
    s.dvec_s[7:8, :] = s.ddown_s[:, FF:].T[0:1, :]
    if not solo:
        gq.close()
    pack_q(plan, s.part_q, s)
    if not solo:
        rq.start()
        reduce_r(2)
    s.wqkv_n[...] = s.wqkv_t[:, :WIDTH].T

    def finish(b, _):
        if not solo:
            at_step(b, {5: lambda: rq.stage(0)})
        cols = block_cols(b)
        grad = nn(s.wqkv_n[...], s.da3_s[:, cols])
        normal, inverse = normal_parts(s.x_s[:, cols].astype(F32))
        gtok = s.da_s[:, cols].astype(F32) + norm_back(grad, normal, inverse, wide(s.gains[0]))
        s.x_s[:, cols] = gtok.astype(BF)
        return 0

    lax.fori_loop(0, BLOCKS, finish, 0)

    def restore(t):
        first = t * LANES
        cols = slice(first, first + LANES)
        total = None
        for low, high in block_runs(first, min(first + LANES, ROWS)):
            target = jnp.concatenate([s.target_s[b] for b in range(low, high)], axis=1)
            hit = iota((LANES, (high - low) * LANES), 0) + first == target
            choice = jnp.where(hit, 1.0, 0.0).astype(BF)
            here = slice(low * LANES, high * LANES)
            both = jnp.concatenate([s.c_s[:, here], s.x_s[:, here]], axis=0)
            part = nt(both, choice)
            total = part if total is None else total + part
        s.da3_s[: 2 * WIDTH, cols] = total.astype(BF)
        write(t).start()

    def write(t):
        cols = slice(t * LANES, (t + 1) * LANES)
        return pltpu.make_async_copy(s.da3_s.at[: 2 * WIDTH, cols], rows_ref.at[:, cols], s.out_sem.at[t])

    tiles = ROWS_PAD // LANES
    for t in range(tiles):
        if not solo and t == 0:
            rq.stage(1)
        if not solo and t == 5:
            rq.stage(2)
            sum_r[top] = rr.stage(3)
            sum_r[rest] = rt.stage(3)
        restore(t)
    if not solo:
        sum_q[...] = rq.stage(3)
        rr.close()
        rt.close()
        rq.close()
    for t in range(tiles):
        write(t).wait()


def main_call(plan, order, tokens, cotan, weights, vectors, packs=None):
    vmem = pl.BlockSpec(memory_space=pltpu.VMEM)
    solo = packs is not None
    scratch = scratch_list(plan)
    if not solo:
        scratch.update(link_list(plan))
    tile = (16, 128)
    if solo:
        sums = [jax.ShapeDtypeStruct((plan.slots, n) + tile, BF) for n in (plan.q_tiles, plan.r_tiles)]
        params = pltpu.CompilerParams(vmem_limit_bytes=VMEM_LIMIT)
    else:
        sums = [jax.ShapeDtypeStruct((n,) + tile, F32) for n in (plan.q_tiles, plan.r_tiles)]
        params = pltpu.CompilerParams(collective_id=0, has_side_effects=True, vmem_limit_bytes=VMEM_LIMIT)
    args = (tokens, cotan) + tuple(weights) + tuple(vectors) + tuple(packs or ())
    return pl.pallas_call(
        partial(main_kernel, plan, solo, tuple(scratch)),
        out_shape=(
            jax.ShapeDtypeStruct((2 * WIDTH, ROWS_PAD), BF),
            *sums,
        ),
        in_specs=[pl.BlockSpec(memory_space=pltpu.SMEM)] + [vmem] * len(args),
        out_specs=(pl.BlockSpec(memory_space=pl.ANY),) + (vmem,) * 2,
        scratch_shapes=list(scratch.values()),
        compiler_params=params,
        name="block_main",
    )(order, *args)


def place_kernel(plan, rows_ref, sum_q, sum_r, *refs):
    out_ref, gtok_ref, dqkv_ref, dproj_ref, dup_ref, ddown_ref = refs[:6]
    vectors = refs[6:]
    out_ref[...] = rows_ref[:WIDTH, :]
    gtok_ref[...] = rows_ref[WIDTH:, :].astype(F32)

    @pl.when(pl.program_id(0) == 0)
    def _():
        get(sum_q, plan.q_cuts(), dqkv_ref, 0, 0)
        get(sum_r, plan.u_cuts(), dup_ref, 0, 0)
        get(sum_r, plan.down_cuts(), ddown_ref, 0, 0)
        get(sum_r, plan.proj_cuts(), dproj_ref, 0, 0)
        for k in range(VECTORS):
            get(sum_q, plan.vector_cuts(k, 1, vectors[k].shape[1]), vectors[k], 0, 0)


def place_call(plan, rows, sum_q, sum_r):
    r, v = plan.rows, plan.vec
    step = 512
    shapes = [(plan.qkv, r), (v, r), (r, plan.up), (v, 4 * r)] + [(1, v)] * 8 + [(1, plan.up)]
    moving = lambda height: pl.BlockSpec((height, step), lambda n: (0, n))
    still = lambda shape: pl.BlockSpec(shape, lambda n: (0,) * len(shape))
    return pl.pallas_call(
        partial(place_kernel, plan),
        grid=(ROWS_PAD // step,),
        out_shape=[jax.ShapeDtypeStruct((WIDTH, ROWS), BF), jax.ShapeDtypeStruct((WIDTH, ROWS), F32)]
        + [jax.ShapeDtypeStruct(shape, F32) for shape in shapes],
        in_specs=[moving(2 * WIDTH), still(sum_q.shape), still(sum_r.shape)],
        out_specs=[moving(WIDTH), moving(WIDTH)] + [still(shape) for shape in shapes],
        compiler_params=pltpu.CompilerParams(vmem_limit_bytes=VMEM_LIMIT),
        name="block_place",
    )(rows, sum_q, sum_r)


def local(plan, *args):
    (
        tokens,
        cotangent,
        crop_order,
        ln1_gain,
        ln1_bias,
        w_qkv,
        b_query,
        b_value,
        w_proj,
        b_proj,
        ln2_gain,
        ln2_bias,
        w_up,
        b_up,
        w_down,
        b_down,
    ) = args
    vectors = (ln1_gain, ln1_bias, b_query, b_value, b_proj, ln2_gain, ln2_bias, b_down, b_up)
    weights = (w_qkv.T, w_proj.T, w_up, w_down.T)
    rows, sum_q, sum_r = main_call(plan, crop_order, tokens.T, cotangent.T, weights, vectors)
    out, gtok, dqkv, dproj, dup, ddown, *grads = place_call(plan, rows, sum_q, sum_r)
    g1, s1, bq, bv, bp, g2, s2, bd, bu = [one[0] for one in grads]
    return (out.T, gtok.T, g1, s1, dqkv.T, bq, bv, dproj.T, bp, g2, s2, dup, bu, ddown.T, bd)


def solution(mesh):
    plan = Plan(mesh.shape["dp"], mesh.shape["fsdp"])
    rows = P(("dp", "fsdp"), None)
    vec = P("dp")
    mat = P("fsdp", "dp")
    return jax.shard_map(
        partial(local, plan),
        mesh=mesh,
        in_specs=(rows, rows, rows, vec, vec, mat, vec, vec, mat, vec, vec, vec, mat, vec, mat, vec),
        out_specs=(rows, rows, vec, vec, mat, vec, vec, mat, vec, vec, vec, mat, vec, mat, vec),
        check_vma=False,
    )
```

```python
from functools import partial

import jax
import jax.numpy as jnp
from jax import lax
from jax.experimental import pallas as pl
from jax.experimental.pallas import tpu as pltpu
from jax.sharding import PartitionSpec as P

HEADS = 6
HEAD_DIM = 48
BIG_LEN = 197
SMALL_LEN = 37
BIGS = 8
SMALLS = 24
WIDTH = 288
EXT = 304
FF = 1152
FF_EXT = 1168
ROWS = 2464
ROWS_PAD = 2560
LANES = 256
BLOCKS = 11
COLS = BLOCKS * LANES
KEYS = 240
TURNED = 2 * HEAD_DIM + 16
BIG_WIN = 384
SMALL_WIN = 256
FF_STEP = 192
VECTORS = 9
RANKS = 40
EPS = 1e-06
BF = jnp.bfloat16
F32 = jnp.float32
MESH = pl.DeviceIdType.MESH
VMEM_LIMIT = 64 * 1024 * 1024 - 65536


def nn(a, b):
    return jnp.dot(a, b, preferred_element_type=F32)


def nt(a, b):
    return lax.dot_general(a, b, (((1,), (1,)), ((), ())), preferred_element_type=F32)


def tn(a, b):
    return lax.dot_general(a, b, (((0,), (0,)), ((), ())), preferred_element_type=F32)


def iota(shape, dim):
    return lax.broadcasted_iota(jnp.int32, shape, dim)


def wide(col):
    return jnp.concatenate([col, col], axis=1)


def block_cols(b):
    return pl.ds(pl.multiple_of(b * LANES, LANES), LANES)


def up_to(size, unit):
    return -(-size // unit) * unit


class Plan:
    def __init__(self, n_dp, n_fs):
        self.n_dp, self.n_fs = n_dp, n_fs
        self.n_core = 2
        self.n_z = 4
        self.n_x = n_dp // (self.n_core * self.n_z)
        self.slots = n_dp * n_fs
        self.groups = self.slots // self.n_z
        self.rows = WIDTH // n_fs
        self.qkv, self.vec, self.up = 3 * WIDTH // n_dp, WIDTH // n_dp, FF // n_dp
        self.q_rows = up_to(self.qkv + VECTORS, 16) // 16
        self.q_left = max(self.rows - 128, 0)
        self.q_beside = 128 // self.q_left if self.q_left else 1
        left = -(-(up_to(self.qkv, 16) // 16) // self.q_beside) if self.q_left else 0
        self.q_tiles = self.q_rows + left
        self.u_tiles = up_to(self.rows, 16) // 16
        self.d_free = 128 - self.up
        self.d_beside = self.u_tiles * self.d_free
        self.d_wide = up_to(max(5 * self.rows - self.d_beside, 0), 128) // 128
        self.d_left = max(self.vec - 16, 0)
        self.d_under = 16 // self.d_left if self.d_left else 1
        left = -(-(up_to(5 * self.rows, 128) // 128) // self.d_under) if self.d_left else 0
        self.r_tiles = self.u_tiles + self.d_wide + left


    def q_cuts(self):
        for tile in range(-(-self.qkv // 16)):
            rows = min(16, self.qkv - 16 * tile)
            yield tile, 0, 0, rows, min(self.rows, 128), 16 * tile, 0
            if self.q_left:
                across, beside = divmod(tile, self.q_beside)
                yield self.q_rows + across, 0, beside * self.q_left, rows, self.q_left, 16 * tile, 128

    def vector_cuts(self, first, count, cols):
        done = 0
        while done < count:
            tile, row = divmod(self.qkv + first + done, 16)
            rows = min(16 - row, count - done)
            yield tile, row, 0, rows, cols, done, 0
            done += rows

    def u_cuts(self):
        for tile in range(self.u_tiles):
            yield tile, 0, 0, min(16, self.rows - 16 * tile), self.up, 16 * tile, 0

    def d_cuts(self, col, cols):
        done = 0
        while done < cols:
            at = col + done
            if at < self.d_beside:
                tile, lane = divmod(at, self.d_free)
                width = min(self.d_free - lane, cols - done)
                lane += self.up
            else:
                tile, lane = divmod(at - self.d_beside, 128)
                width = min(128 - lane, cols - done)
                tile += self.u_tiles
            yield tile, 0, lane, min(self.vec, 16), width, 0, done
            done += width
        done = 0
        while self.d_left and done < cols:
            across, lane = divmod(col + done, 128)
            width = min(128 - lane, cols - done)
            tile, under = divmod(across, self.d_under)
            yield self.u_tiles + self.d_wide + tile, under * self.d_left, lane, self.d_left, width, 16, done
            done += width

    def down_cuts(self):
        return self.d_cuts(0, 4 * self.rows)

    def proj_cuts(self):
        return self.d_cuts(4 * self.rows, self.rows)

    def dp(self, z, x, core):
        return (z * self.n_x + x) * self.n_core + core

    def slot(self, z, x, core, fs):
        return self.dp(z, x, core) * self.n_fs + fs

    def here(self):
        dp, fs = lax.axis_index("dp"), lax.axis_index("fsdp")
        core = lax.rem(dp, self.n_core)
        rest = lax.div(dp, self.n_core)
        return lax.div(rest, self.n_x), lax.rem(rest, self.n_x), core, fs


def put(ref, cuts, value):
    for tile, row, lane, rows, cols, i, j in cuts:
        ref[tile, row : row + rows, lane : lane + cols] = value[i : i + rows, j : j + cols]


def get(ref, cuts, target, top, left):
    for tile, row, lane, rows, cols, i, j in cuts:
        target[top + i : top + i + rows, left + j : left + j + cols] = ref[
            tile, row : row + rows, lane : lane + cols
        ]


class Links:
    def __init__(self, plan):
        self.plan = plan
        self.z, self.x, self.core, self.fs = plan.here()
        self.zs = [lax.rem(self.z + d, plan.n_z) for d in range(plan.n_z)]
        self.xs = [lax.rem(self.x + d, plan.n_x) for d in range(plan.n_x)]
        self.fss = [lax.rem(self.fs + d, plan.n_fs) for d in range(plan.n_fs)]
        self.peer = lax.rem(self.core + 1, 2)
        self.to_core = (plan.dp(self.z, self.x, self.peer), self.fs)
        self.to_fs = [(plan.dp(self.z, self.x, self.core), fs) for fs in self.fss]
        self.to_x = [(plan.dp(self.z, x, self.core), self.fs) for x in self.xs]
        self.to_z = [(plan.dp(z, self.x, self.core), self.fs) for z in self.zs]

    def hail(self):
        places = [self.to_core] + self.to_fs[1:] + self.to_x[1:] + self.to_z[1:]
        for place in places:
            pl.semaphore_signal(pltpu.get_barrier_semaphore(), inc=1, device_id=place, device_id_type=MESH)
        return len(places)


def remote(src, dst, send_sem, recv_sem, place):
    return pltpu.make_async_remote_copy(
        src_ref=src, dst_ref=dst, send_sem=send_sem, recv_sem=recv_sem, device_id=place, device_id_type=MESH
    )


class Axes:
    def __init__(self, links, x_first):
        plan = links.plan
        x, f = (links.xs, links.to_x), (links.fss, links.to_fs)
        (self.at1, self.to1), (self.at2, self.to2) = (x, f) if x_first else (f, x)
        self.n1, self.n2 = len(self.at1), len(self.at2)
        cores = (links.core, links.peer)

        def group(d1, d2, dc):
            x, f = (self.at1[d1], self.at2[d2]) if x_first else (self.at2[d2], self.at1[d1])
            return (x * plan.n_core + cores[dc]) * plan.n_fs + f

        self.group = group


class Gather:
    def __init__(self, links, whole, tiles, x_first, send_sem, recv_sem):
        self.whole, self.tiles, self.send_sem, self.recv_sem = whole, tiles, send_sem, recv_sem
        self.links = links
        axes = Axes(links, x_first)
        nz, n1, n2 = links.plan.n_z, axes.n1, axes.n2
        to_core = [links.to_core]
        at_1 = nz
        at_2 = at_1 + n1
        at_c = at_2 + n1 * n2
        own = axes.group(0, 0, 0)
        both = lambda d1, d2: axes.at1[d1] * n2 + axes.at2[d2]
        first = (links.z, own, links.z)
        along_1, along_2 = (None, own, at_1 + axes.at1[0]), (None, own, at_2 + both(0, 0))
        stages = [[([], [(first, links.to_z[1:])])]]
        arrivals = [(links.zs[dz], own, links.zs[dz]) for dz in range(1, nz)]
        sends = [(along_1, axes.to1[1:]), (along_2, axes.to2[1:]), ((None, own, at_c + both(0, 0)), to_core)]
        stages.append([(arrivals, sends)])
        stage = []
        for d1 in range(1, n1):
            group = axes.group(d1, 0, 0)
            sends = [
                ((None, group, at_2 + both(d1, 0)), axes.to2[1:]),
                ((None, group, at_c + both(d1, 0)), to_core),
            ]
            stage.append(([(None, group, at_1 + axes.at1[d1])], sends))
        stages.append(stage)
        stage = []
        for d2 in range(1, n2):
            for d1 in range(n1):
                group = axes.group(d1, d2, 0)
                sends = [((None, group, at_c + both(d1, d2)), to_core)]
                stage.append(([(None, group, at_2 + both(d1, d2))], sends))
        stages.append(stage)
        stages.append(
            [([(None, axes.group(d1, d2, 1), at_c + both(d1, d2))], []) for d2 in range(n2) for d1 in range(n1)]
        )
        count = 0
        self.work = []
        for stage in stages:
            steps = []
            for waits, sends in stage:
                copies = []
                for what, places in sends:
                    for place in places:
                        copies.append((what, count, place))
                        count += 1
                steps.append((waits, copies))
            self.work.append(steps)

    def copy(self, what, index, place):
        z, group, sem = what
        one = self.whole.at[slice(None) if z is None else z, group, self.tiles]
        return remote(one, one, self.send_sem.at[index], self.recv_sem.at[sem], place)

    def stage(self, number):
        for waits, copies in self.work[number]:
            for what in waits:
                self.copy(what, 0, self.links.to_core).wait_recv()
            for what, index, place in copies:
                self.copy(what, index, place).start()

    def close(self):
        for steps in self.work:
            for _, copies in steps:
                for what, index, place in copies:
                    self.copy(what, index, place).wait_send()


class Reduce:
    def __init__(self, links, part, got, got_z, tiles, x_first, send_sem, recv_sem):
        self.part, self.got, self.got_z, self.tiles = part, got, got_z, tiles
        self.send_sem, self.recv_sem, self.links = send_sem, recv_sem, links
        axes = Axes(links, x_first)
        self.nz, n1, n2 = links.plan.n_z, axes.n1, axes.n2
        last = lambda n: list(range(1, n)) + [0]
        order = [(d1, d2) for d1 in last(n1) for d2 in last(n2)]
        at_1 = n1 * n2
        at_2 = at_1 + (n1 - 1) * n2
        self.at_z = at_2 + n2 - 1
        spot_c = lambda d1, d2: d1 * n2 + d2
        spot_1 = lambda d1, d2: at_1 + (d1 - 1) * n2 + d2
        spot_2 = lambda d2: at_2 + d2 - 1
        self.first = [(axes.group(d1, d2, 1), spot_c(d1, d2), links.to_core) for d1, d2 in order]
        self.stages = [[], []]
        for d1, d2 in order:
            group = axes.group(d1, d2, 0)
            takes = [spot_c(d1, d2)]
            if d1:
                self.stages[0].append((group, takes, spot_1(n1 - d1, d2), axes.to1[d1]))
                continue
            takes += [spot_1(d, d2) for d in range(1, n1)]
            if d2:
                self.stages[1].append((group, takes, spot_2(n2 - d2), axes.to2[d2]))
                continue
            self.own = (group, takes + [spot_2(d) for d in range(1, n2)])

    def copy(self, group, spot, place):
        return remote(
            self.part.at[:, group, self.tiles],
            self.got.at[spot, :, self.tiles],
            self.send_sem.at[spot],
            self.recv_sem.at[spot],
            place,
        )

    def along_z(self, dz):
        spot = self.at_z + self.nz - dz - 1
        return remote(
            self.part.at[self.links.zs[dz], self.own[0], self.tiles],
            self.got_z.at[self.nz - dz - 1, self.tiles],
            self.send_sem.at[spot],
            self.recv_sem.at[spot],
            self.links.to_z[dz],
        )

    def start(self):
        for group, spot, place in self.first:
            self.copy(group, spot, place).start()

    def total(self, group, takes):
        total = self.part[:, group, self.tiles].astype(F32)
        for index in takes:
            self.copy(group, index, self.links.to_core).wait_recv()
            total = total + self.got[index, :, self.tiles].astype(F32)
        self.part[:, group, self.tiles] = total.astype(BF)

    def stage(self, number):
        if number < 2:
            for group, takes, spot, place in self.stages[number]:
                self.total(group, takes)
                self.copy(group, spot, place).start()
        elif number == 2:
            self.total(*self.own)
            for dz in range(1, self.nz):
                self.along_z(dz).start()
        else:
            total = self.part[self.links.z, self.own[0], self.tiles].astype(F32)
            for dz in range(1, self.nz):
                self.along_z(dz).wait_recv()
                total = total + self.got_z[self.nz - dz - 1, self.tiles].astype(F32)
            return total

    def close(self):
        for group, spot, place in self.first:
            self.copy(group, spot, place).wait_send()
        for steps in self.stages:
            for group, _, spot, place in steps:
                self.copy(group, spot, place).wait_send()
        for dz in range(1, self.nz):
            self.along_z(dz).wait_send()


def normal_parts(rows):
    mean = jnp.sum(rows, axis=0, keepdims=True) * (1.0 / WIDTH)
    centered = rows - mean
    variance = jnp.sum(centered * centered, axis=0, keepdims=True) * (1.0 / WIDTH)
    inverse = lax.rsqrt(variance + EPS)
    return centered * inverse, inverse


def norm_back(grad, normal, inverse, gain):
    scaled = grad * gain
    first = jnp.sum(scaled, axis=0, keepdims=True) * (1.0 / WIDTH)
    second = jnp.sum(scaled * normal, axis=0, keepdims=True) * (1.0 / WIDTH)
    return inverse * (scaled - first - normal * second)


def gelu_both(u):
    t = pl.reciprocal(1.0 + jnp.abs(u) * (0.3275911 * 0.7071067811865476), approx=True)
    e = jnp.exp2(u * u * (-0.5 * 1.4426950408889634))
    poly = 0.5 * 1.061405429
    poly = poly * t + 0.5 * -1.453152027
    poly = poly * t + 0.5 * 1.421413741
    poly = poly * t + 0.5 * -0.284496736
    poly = poly * t + 0.5 * 0.254829592
    tail = poly * t * e
    phi = jnp.where(u >= 0.0, 1.0 - tail, tail)
    return u * phi, phi + u * e * 0.3989422804014327


def crop_starts(order):
    slots = BIGS + SMALLS
    big = jnp.where(order < BIGS, 1.0, 0.0)
    size = SMALL_LEN + (BIG_LEN - SMALL_LEN) * big
    before = jnp.where(iota((slots, slots), 0) < iota((slots, slots), 1), 1.0, 0.0).astype(BF)
    rows = jnp.where(iota((16, slots), 0) == 0, size, big).astype(BF)
    sums = nn(rows, before)
    start, big_rank = sums[0:1], sums[1:2]
    small_rank = BIGS + iota((1, slots), 1).astype(F32) - big_rank
    rank = jnp.where(order < BIGS, big_rank, small_rank)
    hit = jnp.where(iota((RANKS, slots), 0).astype(F32) == rank, 1.0, 0.0)
    found = jnp.sum(hit, axis=1, keepdims=True)
    column = jnp.sum(hit * start, axis=1, keepdims=True)
    return jnp.where(found > 0.5, column, 1e6)


def crop_marks(paired):
    lane = iota((16, LANES), 1)
    crop = iota((16, LANES), 0)
    starts = [0, BIG_LEN, BIG_LEN + SMALL_LEN] if paired else [SMALL_LEN * k for k in range(7)]
    label = jnp.full((16, LANES), -1, jnp.int32)
    for start in starts:
        label = label + jnp.where(lane >= start, 1, 0)
    real = crop < len(starts) - 1
    query = jnp.where(real & (label == crop), 1.0, 0.0)
    key = jnp.where(real & (label != crop), -1e30, 0.0)
    return query.astype(BF), key.astype(BF)


def pack_own(plan, q, r, qkv_ref, proj_ref, up_ref, down_ref, vector_refs):
    q[...] = jnp.zeros_like(q)
    r[...] = jnp.zeros_like(r)
    put(q, plan.q_cuts(), qkv_ref[...])
    for k, ref in enumerate(vector_refs):
        put(q, plan.vector_cuts(k, 1, ref.shape[0]), ref[...].reshape(1, ref.shape[0]))
    put(r, plan.u_cuts(), up_ref[...])
    put(r, plan.down_cuts(), down_ref[...])
    put(r, plan.proj_cuts(), proj_ref[...])


def unpack_q(plan, all_q, s):
    r, v, qkv, up = plan.rows, plan.vec, plan.qkv, plan.up
    s.vec_s[...] = jnp.zeros_like(s.vec_s)
    s.wup_n[WIDTH:, :] = jnp.zeros((EXT - WIDTH, FF), BF)
    for i in range(plan.n_dp):
        for j in range(plan.n_fs):
            get(all_q.at[divmod(i * plan.n_fs + j, plan.groups)], plan.q_cuts(), s.wqkv_t, i * qkv, j * r)
        one = all_q.at[divmod(i * plan.n_fs, plan.groups)]
        get(one, plan.vector_cuts(0, VECTORS - 1, v), s.vec_s, 0, i * v)
        get(one, plan.vector_cuts(VECTORS - 1, 1, up), s.wup_n, WIDTH, i * up)
    columns = s.vec_s[...].T
    lane = iota((WIDTH, 16), 1)
    none = jnp.zeros((WIDTH, 16), BF)
    s.wqkv_t[:WIDTH, WIDTH:] = jnp.where(lane == 2, columns, none)
    s.wqkv_t[WIDTH : 2 * WIDTH, WIDTH:] = none
    s.wqkv_t[2 * WIDTH :, WIDTH:] = jnp.where(lane == 3, columns, none)
    s.wproj_t[:, WIDTH:] = jnp.where(lane == 4, columns, none)
    s.wdown_t[:, FF:] = jnp.where(lane == 7, columns, none)
    for n, k in enumerate((0, 1, 5, 6)):
        pick = jnp.where(iota((16, 128), 0) == k, 1.0, 0.0).astype(BF)
        s.gains[n] = tn(s.vec_s[...], pick)


def unpack_r(plan, all_r, s):
    r, v, up = plan.rows, plan.vec, plan.up
    for i in range(plan.n_dp):
        for j in range(plan.n_fs):
            one = all_r.at[divmod(i * plan.n_fs + j, plan.groups)]
            get(one, plan.u_cuts(), s.wup_n, j * r, i * up)
            get(one, plan.down_cuts(), s.wdown_t, i * v, j * 4 * r)
            get(one, plan.proj_cuts(), s.wproj_t, i * v, j * r)


def pack_r(plan, part, s):
    r, v, up = plan.rows, plan.vec, plan.up
    for i in range(plan.n_dp):
        for j in range(plan.n_fs):
            one = part.at[divmod(i * plan.n_fs + j, plan.groups)]
            put(one, plan.u_cuts(), s.dup_s[j * r : (j + 1) * r, i * up : (i + 1) * up].astype(BF))
            down = s.ddown_s[i * v : (i + 1) * v, j * 4 * r : (j + 1) * 4 * r].astype(BF)
            put(one, plan.down_cuts(), down)
            put(one, plan.proj_cuts(), s.dproj_s[i * v : (i + 1) * v, j * r : (j + 1) * r].astype(BF))


def pack_q(plan, part, s):
    r, v, qkv, up = plan.rows, plan.vec, plan.qkv, plan.up
    for i in range(plan.n_dp):
        vectors = s.dvec_s[:, i * v : (i + 1) * v].astype(BF)
        bias_up = s.dup_s[WIDTH : WIDTH + 1, i * up : (i + 1) * up].astype(BF)
        for j in range(plan.n_fs):
            one = part.at[divmod(i * plan.n_fs + j, plan.groups)]
            put(one, plan.q_cuts(), s.dqkv_s[i * qkv : (i + 1) * qkv, j * r : (j + 1) * r].astype(BF))
            put(one, plan.vector_cuts(0, VECTORS - 1, v), vectors)
            put(one, plan.vector_cuts(VECTORS - 1, 1, up), bias_up)


class Scratch:
    pass


def scratch_list(plan):
    vmem = pltpu.VMEM
    return dict(
        target_s=vmem((BLOCKS, 1, LANES), jnp.int32),
        wqkv_t=vmem((3 * WIDTH, EXT), BF),
        wproj_t=vmem((WIDTH, EXT), BF),
        wup_t=vmem((FF, EXT), BF),
        wdown_t=vmem((WIDTH, FF_EXT), BF),
        wqkv_n=vmem((WIDTH, 3 * WIDTH), BF),
        wproj_n=vmem((WIDTH, WIDTH), BF),
        wup_n=vmem((EXT, FF), BF),
        wdown_n=vmem((FF, WIDTH), BF),
        vec_s=vmem((16, WIDTH), BF),
        gains=vmem((4, WIDTH, 128), F32),
        marks_s=vmem((2, 2, 16, LANES), BF),
        turned_s=vmem((HEADS // 2, KEYS, 128), BF),
        x_s=vmem((WIDTH, COLS), BF),
        c_s=vmem((WIDTH, COLS), BF),
        xhat_s=vmem((EXT, COLS), BF),
        qkv_s=vmem((3 * WIDTH, COLS), BF),
        prob_s=vmem((BLOCKS, HEADS, KEYS, LANES), BF),
        ctx_s=vmem((EXT, COLS), BF),
        h2_a=vmem((EXT, LANES), BF),
        h2_b=vmem((EXT, LANES), BF),
        act_a=vmem((FF_EXT, LANES), BF),
        act_b=vmem((FF_EXT, LANES), BF),
        du_a=vmem((FF, LANES), BF),
        du_b=vmem((FF, LANES), BF),
        mid_a=vmem((WIDTH, LANES), F32),
        mid_b=vmem((WIDTH, LANES), F32),
        da_s=vmem((WIDTH, COLS), BF),
        do_s=vmem((WIDTH, COLS), BF),
        da3_s=vmem((3 * WIDTH, COLS), BF),
        dqkv_s=vmem((3 * WIDTH, EXT), F32),
        dproj_s=vmem((WIDTH, EXT), F32),
        dup_s=vmem((EXT, FF), F32),
        ddown_s=vmem((WIDTH, FF_EXT), F32),
        dvec_s=vmem((8, WIDTH), F32),
        acc_s=vmem((2, WIDTH, LANES), F32),
        grad_s=vmem((WIDTH, LANES), F32),
        work_s=vmem((4, KEYS, LANES), F32),
        ds_s=vmem((3, KEYS, LANES), BF),
        out_sem=pltpu.SemaphoreType.DMA((ROWS_PAD // LANES,)),
    )


def link_list(plan):
    vmem, dma = pltpu.VMEM, pltpu.SemaphoreType.DMA
    tile = (16, 128)
    n_z, groups = plan.n_z, plan.groups
    crossed = plan.n_x * plan.n_fs
    taken = crossed + crossed - 1
    scratch = dict(
        all_q=vmem((n_z, groups, plan.q_tiles) + tile, BF),
        all_r=vmem((n_z, groups, plan.r_tiles) + tile, BF),
        got_q=vmem((taken, n_z, plan.q_tiles) + tile, BF),
        got_r=vmem((taken, n_z, plan.r_tiles) + tile, BF),
        last_q=vmem((n_z - 1, plan.q_tiles) + tile, BF),
        last_r=vmem((n_z - 1, plan.r_tiles) + tile, BF),
    )
    sends = n_z - 1 + crossed - 1 + crossed
    for name in ("gq", "gp", "gr", "gt"):
        scratch[name + "_send"] = dma((sends,))
        scratch[name + "_recv"] = dma((n_z + max(plan.n_x, plan.n_fs) + 2 * crossed,))
    for name in ("rq", "rp", "rr", "rt"):
        scratch[name + "_send"] = dma((taken + n_z - 1,))
        scratch[name + "_recv"] = dma((taken + n_z - 1,))
    return scratch


def pair_loop(first, even, odd, last, service=None):
    first()

    def one(i, _):
        if service is not None:
            service(i)
        even(2 * i)
        odd(2 * i + 1)
        return 0

    lax.fori_loop(0, (BLOCKS - 1) // 2, one, 0)
    last()


def row_range(b):
    if b < BIGS:
        big_high = BIG_LEN * (b + 1) + SMALL_LEN * SMALLS
        return SMALL_LEN * b, max(big_high, SMALL_LEN * (b + 1) + BIG_LEN * BIGS)
    k = BIGS + 6 * (b - BIGS)
    return SMALL_LEN * k, SMALL_LEN * min(k + 6, SMALLS) + BIG_LEN * BIGS


def block_runs(low, high):
    runs = []
    for b in range(BLOCKS):
        first, last = row_range(b)
        if first < high and last > low:
            if runs and runs[-1][1] == b:
                runs[-1][1] = b + 1
            else:
                runs.append([b, b + 1])
    return runs


def at_step(i, actions):
    for step, action in actions.items():
        pl.when(i == step)(action)


def main_kernel(plan, solo, names, order_ref, tokens_ref, cotan_ref, qkv_ref, proj_ref, up_ref, down_ref, *refs):
    vector_refs, refs = refs[:VECTORS], refs[VECTORS:]
    s = Scratch()
    if solo:
        s.all_q, s.all_r = refs[:2]
        refs = refs[2:]
    rows_ref, sum_q, sum_r = refs[:3]
    for name, ref in zip(names, refs[3:]):
        setattr(s, name, ref)
    if solo:
        s.part_q, s.part_r = sum_q, sum_r
    else:
        s.part_q, s.part_r = s.all_q, s.all_r
        links = Links(plan)
        hailed = links.hail()
        q_top, q_rest = slice(0, plan.q_tiles // 2), slice(plan.q_tiles // 2, plan.q_tiles)
        top = slice(0, plan.r_tiles // 2)
        rest = slice(plan.r_tiles // 2, plan.r_tiles)
        gq = Gather(links, s.all_q, q_top, True, s.gq_send, s.gq_recv)
        gp = Gather(links, s.all_q, q_rest, False, s.gp_send, s.gp_recv)
        gr = Gather(links, s.all_r, top, True, s.gr_send, s.gr_recv)
        gt = Gather(links, s.all_r, rest, False, s.gt_send, s.gt_recv)
        rq = Reduce(links, s.part_q, s.got_q, s.last_q, q_top, True, s.rq_send, s.rq_recv)
        rp = Reduce(links, s.part_q, s.got_q, s.last_q, q_rest, False, s.rp_send, s.rp_recv)
        rr = Reduce(links, s.part_r, s.got_r, s.last_r, top, True, s.rr_send, s.rr_recv)
        rt = Reduce(links, s.part_r, s.got_r, s.last_r, rest, False, s.rt_send, s.rt_recv)

        def gather_q(number):
            gq.stage(number)
            gp.stage(number)

        def reduce_q(number):
            rq.stage(number)
            rp.stage(number)

        def gather_r(number):
            gr.stage(number)
            gt.stage(number)

        def reduce_r(number):
            rr.stage(number)
            rt.stage(number)

        mine = (links.z, (links.x * plan.n_core + links.core) * plan.n_fs + links.fs)
        pack_own(plan, s.all_q.at[mine], s.all_r.at[mine], qkv_ref, proj_ref, up_ref, down_ref, vector_refs)
        pl.semaphore_wait(pltpu.get_barrier_semaphore(), hailed)
        gather_q(0)
        gather_r(0)

    s.da3_s[: 2 * WIDTH, ROWS_PAD - 128 : ROWS_PAD] = jnp.zeros((2 * WIDTH, 128), BF)
    s.da3_s[:WIDTH, :ROWS] = tokens_ref[...]
    s.da3_s[WIDTH : 2 * WIDTH, :ROWS] = cotan_ref[...]
    starts = crop_starts(order_ref[...])
    lane = iota((1, LANES), 1)
    place = lane.astype(F32)
    for b in range(BLOCKS):
        if b < BIGS:
            small = starts[BIGS + b : BIGS + b + 1, :] - BIG_LEN
            target = jnp.where(lane < BIG_LEN + SMALL_LEN, small + place, -1.0)
            target = jnp.where(lane < BIG_LEN, starts[b : b + 1, :] + place, target)
        else:
            target = jnp.full((1, LANES), -1.0, F32)
            for k in range(6):
                n = 2 * BIGS + 6 * (b - BIGS) + k
                here = (lane >= SMALL_LEN * k) & (lane < SMALL_LEN * (k + 1))
                target = jnp.where(here, starts[n : n + 1, :] - SMALL_LEN * k + place, target)
        s.target_s[b] = target.astype(jnp.int32)

    def load(b):
        low, high = row_range(b)
        low, high = low // 128 * 128, min(up_to(high, 128), ROWS_PAD)
        hit = iota((high - low, LANES), 0) + low == s.target_s[b]
        both = nn(s.da3_s[: 2 * WIDTH, low:high], jnp.where(hit, 1.0, 0.0).astype(BF))
        s.x_s[:, b * LANES : (b + 1) * LANES] = both[:WIDTH].astype(BF)
        s.c_s[:, b * LANES : (b + 1) * LANES] = both[WIDTH:].astype(BF)

    for b in range(0, 2):
        load(b)
    if not solo:
        gather_q(1)
    for b in range(2, 4):
        load(b)
    if not solo:
        gather_q(2)
    for b in range(4, 7):
        load(b)
    if not solo:
        gather_q(3)
    for b in range(7, 11):
        load(b)
    if not solo:
        gather_q(4)
        gather_r(1)

    unpack_q(plan, s.all_q, s)
    for kind, paired in enumerate((True, False)):
        s.marks_s[kind, 0], s.marks_s[kind, 1] = crop_marks(paired)
    ones = jnp.ones((16, COLS), BF)
    s.xhat_s[WIDTH:, :] = ones
    s.ctx_s[WIDTH:, :] = ones
    s.h1_a, s.h1_b, s.live_a, s.live_b = s.h2_a, s.h2_b, s.act_a, s.act_b
    for ref in (s.h2_a, s.h2_b):
        ref[WIDTH:, :] = ones[:, :LANES]
    for ref in (s.act_a, s.act_b):
        ref[FF:, :] = ones[:, :LANES]
    s.acc_s[...] = jnp.zeros_like(s.acc_s)
    s.dup_s[...] = jnp.zeros_like(s.dup_s)
    s.ddown_s[...] = jnp.zeros_like(s.ddown_s)
    scale = HEAD_DIM ** (-0.5)
    blank = jnp.zeros((HEAD_DIM, LANES), BF)

    def head_rows(part, h):
        return slice(part * WIDTH + HEAD_DIM * h, part * WIDTH + HEAD_DIM * (h + 1))

    def pair_rows(part, h):
        low = part * WIDTH + 2 * HEAD_DIM * (h // 2)
        return slice(low, low + 2 * HEAD_DIM)

    def beside(rows, h):
        return jnp.concatenate([rows, blank] if h % 2 == 0 else [blank, rows], axis=0)

    def project(b, live, h1):
        cols = block_cols(b)

        def norm():
            normal, _ = normal_parts(s.x_s[:, cols].astype(F32))
            s.xhat_s[:WIDTH, cols] = normal.astype(BF)
            h1[:WIDTH, :] = (normal * wide(s.gains[0]) + wide(s.gains[1])).astype(BF)

        def part(k):
            rows = slice(k * WIDTH, (k + 1) * WIDTH)
            mixed = nn(s.wqkv_t[rows, :], h1[...])
            mixed = ((mixed * scale) if k == 0 else mixed).astype(BF)
            live[rows, :] = mixed
            s.qkv_s[rows, cols] = mixed

        return [norm, lambda: part(0), lambda: part(1), lambda: part(2)]

    def attend(b, live, beside_it=()):
        cols = block_cols(b)
        kind = jnp.where(b < BIGS, 0, 1)
        beside_it = list(beside_it)

        def score(h):
            if h % 2 == 0:
                keys = jnp.concatenate([live[pair_rows(1, h), :KEYS], s.marks_s[kind, 1, :, :KEYS]], axis=0)
                s.turned_s[h // 2, :, :TURNED] = keys.T
            query = jnp.concatenate([beside(live[head_rows(0, h), :], h), s.marks_s[kind, 0]], axis=0)
            s.work_s[h % 3] = nn(s.turned_s[h // 2, :, :TURNED], query)

        def spread_out(h):
            for tile in (slice(0, 128), slice(128, 256)):
                scores = s.work_s[h % 3, :, tile]
                top = jnp.max(scores, axis=0, keepdims=True)
                expo = jnp.exp(scores - top)
                total = jnp.sum(expo, axis=0, keepdims=True)
                s.prob_s[b, h, :, tile] = (expo * (1.0 / total)).astype(BF)

        def mix(h):
            s.ctx_s[head_rows(0, h), cols] = nn(live[head_rows(2, h), :KEYS], s.prob_s[b, h]).astype(BF)

        score(0)
        score(1)
        for h in range(HEADS):
            if beside_it:
                beside_it.pop(0)()
            if h + 2 < HEADS:
                score(h + 2)
            spread_out(h)
            if h > 1:
                mix(h - 2)
        mix(HEADS - 2)
        mix(HEADS - 1)

    def run(steps):
        for step in steps:
            step()

    pair_loop(
        lambda: run(project(0, s.live_a, s.h1_a)),
        lambda b: attend(b, s.live_a, project(b + 1, s.live_b, s.h1_b)),
        lambda b: attend(b, s.live_b, project(b + 1, s.live_a, s.h1_a)),
        lambda: attend(BLOCKS - 1, s.live_a),
        None if solo else lambda i: at_step(i, {1: lambda: gather_r(2), 3: lambda: gather_r(3)}),
    )

    if not solo:
        gather_r(4)
    unpack_r(plan, s.all_r, s)
    s.wup_t[...] = s.wup_n[...].T
    s.wproj_n[...] = s.wproj_t[:, :WIDTH].T
    s.wdown_n[...] = s.wdown_t[:, :FF].T

    def widen(b, h2, act, du, mid_ref):
        cols = block_cols(b)

        def enter():
            mid = s.x_s[:, cols].astype(F32) + nn(s.wproj_t[...], s.ctx_s[:, cols])
            mid_ref[...] = mid
            normal, _ = normal_parts(mid)
            h2[:WIDTH, :] = (normal * wide(s.gains[2]) + wide(s.gains[3])).astype(BF)

        def products(n):
            part = slice(n * FF_STEP, (n + 1) * FF_STEP)
            s.work_s[n % 2, :FF_STEP] = nn(s.wup_t[part, :], h2[...])
            s.work_s[2 + n % 2, :FF_STEP] = nn(s.wdown_n[part, :], s.c_s[:, cols])

        def curve(n):
            part = slice(n * FF_STEP, (n + 1) * FF_STEP)
            value, slope = gelu_both(s.work_s[n % 2, :FF_STEP])
            act[part, :] = value.astype(BF)
            du[part, :] = (s.work_s[2 + n % 2, :FF_STEP] * slope).astype(BF)

        steps = [enter, partial(products, 0), partial(products, 1)]
        for n in range(FF // FF_STEP):
            steps.append(partial(curve, n))
            if (n + 2) * FF_STEP < FF:
                steps.append(partial(products, n + 2))
        return steps

    def narrow(b, h2, act, du, mid_ref):
        cols = block_cols(b)

        def hidden_back(f):
            part = slice(f, f + 96)
            s.grad_s[part, :] = nn(s.wup_n[part, :], du[...])

        def norm_two():
            grad = s.grad_s[...]
            normal, inverse = normal_parts(mid_ref[...])
            s.acc_s[0] += grad * normal
            s.acc_s[1] += grad
            dy1 = s.c_s[:, cols].astype(F32) + norm_back(grad, normal, inverse, wide(s.gains[2]))
            s.da_s[:, cols] = dy1.astype(BF)

        def context_back():
            s.do_s[:, cols] = nn(s.wproj_n[...], s.da_s[:, cols]).astype(BF)

        def weights_down(f):
            part = slice(f, min(f + 256, FF_EXT))
            s.ddown_s[:, part] += nt(s.c_s[:, cols], act[part, :])

        def weights_up(f):
            part = slice(f, min(f + 256, FF))
            s.dup_s[:, part] += nt(h2[...], du[part, :])

        def leave(f):
            part = slice(f, f + 96)
            s.c_s[part, cols] = (mid_ref[part, :] + nn(s.wdown_t[part, :], act[...])).astype(BF)

        steps = [partial(hidden_back, f) for f in range(0, WIDTH, 96)]
        steps += [partial(weights_down, f) for f in range(0, FF_EXT, 256)]
        steps[5:5] = [norm_two]
        steps += [context_back]
        steps += [partial(weights_up, f) for f in range(0, FF, 256)]
        steps += [partial(leave, f) for f in range(0, WIDTH, 96)]
        return steps

    def weave(one, two):
        steps = [((n + 0.5) / len(one), step) for n, step in enumerate(one)]
        steps += [((n + 0.5) / len(two), step) for n, step in enumerate(two)]
        run(step for _, step in sorted(steps, key=lambda pair: pair[0]))

    set_a = (s.h2_a, s.act_a, s.du_a, s.mid_a)
    set_b = (s.h2_b, s.act_b, s.du_b, s.mid_b)
    pair_loop(
        lambda: run(widen(0, *set_a)),
        lambda b: weave(widen(b + 1, *set_b), narrow(b, *set_a)),
        lambda b: weave(widen(b + 1, *set_a), narrow(b, *set_b)),
        lambda: run(narrow(BLOCKS - 1, *set_a)),
    )
    s.dproj_s[...] = nt(s.da_s[...], s.ctx_s[...])
    if not solo:
        gr.close()
        gt.close()
    pack_r(plan, s.part_r, s)
    if not solo:
        rr.start()
        rt.start()

    def padded(rows):
        return jnp.concatenate([rows, jnp.zeros((HEAD_DIM, LANES - KEYS), F32)], axis=1).astype(BF)

    def backward(b):
        cols = block_cols(b)
        key_cols = pl.ds(pl.multiple_of(b * LANES, LANES), KEYS)

        def slope(h):
            if h % 2 == 0:
                s.turned_s[h // 2, :, : 2 * HEAD_DIM] = s.qkv_s[pair_rows(2, h), key_cols].T
            values = s.turned_s[h // 2, :, : 2 * HEAD_DIM]
            s.work_s[h % 3] = nn(values, beside(s.do_s[head_rows(0, h), cols], h))

        def score_grad(h):
            for tile in (slice(0, 128), slice(128, 256)):
                prob = s.prob_s[b, h, :, tile].astype(F32)
                term = prob * s.work_s[h % 3, :, tile]
                weighted = jnp.sum(term, axis=0, keepdims=True)
                s.ds_s[h % 3, :, tile] = (term - prob * weighted).astype(BF)

        def back(h):
            ds = s.ds_s[h % 3]
            s.da3_s[head_rows(0, h), cols] = (nn(s.qkv_s[head_rows(1, h), key_cols], ds) * scale).astype(BF)
            s.da3_s[head_rows(1, h), cols] = padded(nt(s.qkv_s[head_rows(0, h), cols], ds))
            s.da3_s[head_rows(2, h), cols] = padded(nt(s.do_s[head_rows(0, h), cols], s.prob_s[b, h]))

        slope(0)
        slope(1)
        for h in range(HEADS):
            if h + 2 < HEADS:
                slope(h + 2)
            score_grad(h)
            if h > 1:
                back(h - 2)
        back(HEADS - 2)
        back(HEADS - 1)

    def backward_loop(b, _):
        if not solo:
            at_step(b, {3: lambda: reduce_r(0), 7: lambda: reduce_r(1)})
        backward(b)
        return 0

    lax.fori_loop(0, BLOCKS, backward_loop, 0)

    product = nt(s.da3_s[...], s.xhat_s[...])
    sums = product[:, WIDTH : WIDTH + 1]
    weights = s.wqkv_t[:, :WIDTH].astype(F32)
    gain, shift = s.vec_s[0:1, :].astype(F32), s.vec_s[1:2, :].astype(F32)
    s.dvec_s[0:1, :] = jnp.sum(weights * product[:, :WIDTH], axis=0, keepdims=True)
    s.dvec_s[1:2, :] = jnp.sum(weights * sums, axis=0, keepdims=True)
    s.dqkv_s[:, :WIDTH] = product[:, :WIDTH] * gain + sums * shift
    s.dqkv_s[:, WIDTH:] = product[:, WIDTH:]
    rows = s.dqkv_s[:, 256:].T
    s.dvec_s[2:3, :] = rows[WIDTH - 256 : WIDTH - 255, :WIDTH]
    s.dvec_s[3:4, :] = rows[WIDTH - 256 : WIDTH - 255, 2 * WIDTH :]
    s.dvec_s[4:5, :] = s.dproj_s[:, 256:].T[WIDTH - 256 : WIDTH - 255, :]
    for k in range(2):
        both = s.acc_s[k]
        s.dvec_s[5 + k : 6 + k, :] = jnp.sum((both[:, :128] + both[:, 128:]).T, axis=0, keepdims=True)
    s.dvec_s[7:8, :] = s.ddown_s[:, FF:].T[0:1, :]
    if not solo:
        gq.close()
        gp.close()
    pack_q(plan, s.part_q, s)
    if not solo:
        rq.start()
        rp.start()
        reduce_r(2)
    s.wqkv_n[...] = s.wqkv_t[:, :WIDTH].T

    def finish(b, _):
        if not solo:
            at_step(b, {5: lambda: reduce_q(0)})
        cols = block_cols(b)
        grad = nn(s.wqkv_n[...], s.da3_s[:, cols])
        normal, inverse = normal_parts(s.x_s[:, cols].astype(F32))
        gtok = s.da_s[:, cols].astype(F32) + norm_back(grad, normal, inverse, wide(s.gains[0]))
        s.x_s[:, cols] = gtok.astype(BF)
        return 0

    lax.fori_loop(0, BLOCKS, finish, 0)

    def restore(t):
        first = t * LANES
        cols = slice(first, first + LANES)
        total = None
        for low, high in block_runs(first, min(first + LANES, ROWS)):
            target = jnp.concatenate([s.target_s[b] for b in range(low, high)], axis=1)
            hit = iota((LANES, (high - low) * LANES), 0) + first == target
            choice = jnp.where(hit, 1.0, 0.0).astype(BF)
            here = slice(low * LANES, high * LANES)
            both = jnp.concatenate([s.c_s[:, here], s.x_s[:, here]], axis=0)
            part = nt(both, choice)
            total = part if total is None else total + part
        s.da3_s[: 2 * WIDTH, cols] = total.astype(BF)
        write(t).start()

    def write(t):
        cols = slice(t * LANES, (t + 1) * LANES)
        return pltpu.make_async_copy(s.da3_s.at[: 2 * WIDTH, cols], rows_ref.at[:, cols], s.out_sem.at[t])

    tiles = ROWS_PAD // LANES
    for t in range(tiles):
        if not solo and t == 0:
            reduce_q(1)
        if not solo and t == 5:
            reduce_q(2)
            sum_r[top] = rr.stage(3)
            sum_r[rest] = rt.stage(3)
        restore(t)
    if not solo:
        sum_q[q_top] = rq.stage(3)
        sum_q[q_rest] = rp.stage(3)
        rr.close()
        rt.close()
        rq.close()
        rp.close()
    for t in range(tiles):
        write(t).wait()


def main_call(plan, order, tokens, cotan, weights, vectors, packs=None):
    vmem = pl.BlockSpec(memory_space=pltpu.VMEM)
    solo = packs is not None
    scratch = scratch_list(plan)
    if not solo:
        scratch.update(link_list(plan))
    tile = (16, 128)
    if solo:
        shape = (plan.n_z, plan.groups)
        sums = [jax.ShapeDtypeStruct(shape + (n,) + tile, BF) for n in (plan.q_tiles, plan.r_tiles)]
        params = pltpu.CompilerParams(vmem_limit_bytes=VMEM_LIMIT)
    else:
        sums = [jax.ShapeDtypeStruct((n,) + tile, F32) for n in (plan.q_tiles, plan.r_tiles)]
        params = pltpu.CompilerParams(collective_id=0, has_side_effects=True, vmem_limit_bytes=VMEM_LIMIT)
    args = (tokens, cotan) + tuple(weights) + tuple(vectors) + tuple(packs or ())
    return pl.pallas_call(
        partial(main_kernel, plan, solo, tuple(scratch)),
        out_shape=(
            jax.ShapeDtypeStruct((2 * WIDTH, ROWS_PAD), BF),
            *sums,
        ),
        in_specs=[vmem] * (1 + len(args)),
        out_specs=(pl.BlockSpec(memory_space=pl.ANY),) + (vmem,) * 2,
        scratch_shapes=list(scratch.values()),
        compiler_params=params,
        name="block_main",
    )(order, *args)


def place_kernel(plan, rows_ref, sum_q, sum_r, *refs):
    out_ref, gtok_ref, dqkv_ref, dproj_ref, dup_ref, ddown_ref = refs[:6]
    vectors = refs[6:]
    out_ref[...] = rows_ref[:WIDTH, :]
    gtok_ref[...] = rows_ref[WIDTH:, :].astype(F32)

    @pl.when(pl.program_id(0) == 0)
    def _():
        get(sum_q, plan.q_cuts(), dqkv_ref, 0, 0)
        get(sum_r, plan.u_cuts(), dup_ref, 0, 0)
        get(sum_r, plan.down_cuts(), ddown_ref, 0, 0)
        get(sum_r, plan.proj_cuts(), dproj_ref, 0, 0)
        for k in range(VECTORS):
            get(sum_q, plan.vector_cuts(k, 1, vectors[k].shape[1]), vectors[k], 0, 0)


def place_call(plan, rows, sum_q, sum_r):
    r, v = plan.rows, plan.vec
    step = 512
    shapes = [(plan.qkv, r), (v, r), (r, plan.up), (v, 4 * r)] + [(1, v)] * 8 + [(1, plan.up)]
    moving = lambda height: pl.BlockSpec((height, step), lambda n: (0, n))
    still = lambda shape: pl.BlockSpec(shape, lambda n: (0,) * len(shape))
    return pl.pallas_call(
        partial(place_kernel, plan),
        grid=(ROWS_PAD // step,),
        out_shape=[jax.ShapeDtypeStruct((WIDTH, ROWS), BF), jax.ShapeDtypeStruct((WIDTH, ROWS), F32)]
        + [jax.ShapeDtypeStruct(shape, F32) for shape in shapes],
        in_specs=[moving(2 * WIDTH), still(sum_q.shape), still(sum_r.shape)],
        out_specs=[moving(WIDTH), moving(WIDTH)] + [still(shape) for shape in shapes],
        compiler_params=pltpu.CompilerParams(vmem_limit_bytes=VMEM_LIMIT),
        name="block_place",
    )(rows, sum_q, sum_r)


def local(plan, *args):
    (
        tokens,
        cotangent,
        crop_order,
        ln1_gain,
        ln1_bias,
        w_qkv,
        b_query,
        b_value,
        w_proj,
        b_proj,
        ln2_gain,
        ln2_bias,
        w_up,
        b_up,
        w_down,
        b_down,
    ) = args
    vectors = (ln1_gain, ln1_bias, b_query, b_value, b_proj, ln2_gain, ln2_bias, b_down, b_up)
    weights = (w_qkv.T, w_proj.T, w_up, w_down.T)
    rows, sum_q, sum_r = main_call(plan, crop_order, tokens.T, cotangent.T, weights, vectors)
    out, gtok, dqkv, dproj, dup, ddown, *grads = place_call(plan, rows, sum_q, sum_r)
    g1, s1, bq, bv, bp, g2, s2, bd, bu = [one[0] for one in grads]
    return (out.T, gtok.T, g1, s1, dqkv.T, bq, bv, dproj.T, bp, g2, s2, dup, bu, ddown.T, bd)


def solution(mesh):
    plan = Plan(mesh.shape["dp"], mesh.shape["fsdp"])
    rows = P(("dp", "fsdp"), None)
    vec = P("dp")
    mat = P("fsdp", "dp")
    return jax.shard_map(
        partial(local, plan),
        mesh=mesh,
        in_specs=(rows, rows, rows, vec, vec, mat, vec, vec, mat, vec, vec, vec, mat, vec, mat, vec),
        out_specs=(rows, rows, vec, vec, mat, vec, vec, mat, vec, vec, vec, mat, vec, mat, vec),
        check_vma=False,
    )
```
